256 devices in a mesh: gx: 8 (over x, core), gy: 4 (over z_hi), gz: 8 (over z_lo, y).
Axes of the slice: x: 4, y: 4, z: 8 (z_hi: 4, z_lo: 2; z = z_hi * 2 + z_lo), core: 2. Of those that a mesh axis runs over, the one named last changes fastest.
Arguments:
- features: bfloat16 [16, 8, 16, 2, 49, 128], P('gx', 'gy', 'gz'), may hold values from -6 to 6
- cotangent: bfloat16 [16, 8, 16, 2, 49, 128], P('gx', 'gy', 'gz'), may hold values from -1.5 to 1.5
- counts: int32 [16, 8, 16], P('gx', 'gy', 'gz'), may hold values from 1 to 2, as said below
- sources: int32 [16, 8, 16, 2, 12], P('gx', 'gy', 'gz'), may hold values from 0 to 53, as said below
- wigner: bfloat16 [235, 16, 8, 16, 2, 12], P(None, 'gx', 'gy', 'gz'), may hold values from -2.5 to 2.5
- distance: float32 [16, 8, 16, 2, 12], P('gx', 'gy', 'gz'), may hold values from 1 to 5.5
- direction: float32 [3, 16, 8, 16, 2, 12], P(None, 'gx', 'gy', 'gz'), may hold values from -3 to 3
- weight_zero: bfloat16 [896, 896], replicated, may hold values from -0.1875 to 0.1875
- weight_one: bfloat16 [2, 768, 768], replicated, may hold values from -0.15625 to 0.15625
- weight_two: bfloat16 [2, 640, 640], replicated, may hold values from -0.15625 to 0.15625
- radial_in: float32 [256, 128], replicated, may hold values from -1 to 1
- radial_out: float32 [128, 896], replicated, may hold values from -0.5 to 0.5
Outputs:
- updated: bfloat16 [16, 8, 16, 2, 49, 128], P('gx', 'gy', 'gz')
- grad_features: float32 [16, 8, 16, 2, 49, 128], P('gx', 'gy', 'gz')
- forces: float32 [3, 16, 8, 16, 2], P(None, 'gx', 'gy', 'gz')
The draws below stay inside these ranges and needn't reach their ends.
Inputs may be any that keep to these rules, and one draw needn't show every extreme that they name: Each cell's atoms fill its first counts slots; some cell holds exactly 2 atoms in every draw. sources = o * 2 + s names slot s, below that cell's count, of the cell displaced by (o // 9 - 1, (o // 3) % 3 - 1, o % 3 - 1) with periodic wrap; the 12 displacements of one slot are distinct; where the displacement is (0, 0, 0), s is another slot of the target's own cell.
All inputs are finite; a program needn't handle non-finite values.
Results may differ from the reference program's by a relative error of at most 0.0075.
Values may be sent and summed in bfloat16 or wider, within the bound.
No kernel may reach another device: no remote copies, remote signals or barrier semaphores. Data moves between devices by JAX's collectives and lax.ppermute only.
A program may use at most 128 MiB of HBM per device.

```python
import math
import jax
import jax.numpy as jnp
from jax import lax

C = 128
LMAX = 6
MMAX = 2
HID = 128
NB = 256
NBR = 12
CAP = 2
L2 = 49
WIG = 235
NCX = 16
NCY = 8
NCZ = 16
N_GX = 8
N_GY = 4
N_GZ = 8


def cell_counts(key):
    num_cells = NCX * NCY * NCZ
    drawn = jax.random.randint(jax.random.fold_in(key, 7), (num_cells,), 1, CAP + 1)
    chosen = jax.random.randint(jax.random.fold_in(key, 8), (), 0, num_cells)
    drawn = jnp.where(jnp.arange(num_cells) == chosen, CAP, drawn)
    return drawn.reshape(NCX, NCY, NCZ).astype(jnp.int32)


def draw_counts(key, part):
    return cell_counts(key)


def draw_sources(key, part):
    counts = cell_counts(key)
    base_scores = jax.random.randint(jax.random.fold_in(key, 9), (NCX, NCY, NCZ, CAP, 27), 0, 1 << 20) * 32 + jnp.arange(27, dtype=jnp.int32)
    lonely = (counts < 2)[:, :, :, None, None]
    blocked = jnp.logical_and(lonely, (jnp.arange(27, dtype=jnp.int32) == 13)[None, None, None, None, :])
    scores = jnp.where(blocked, base_scores + (1 << 26), base_scores)
    offsets = jnp.argsort(scores, axis=-1)[..., :NBR].astype(jnp.int32)
    step_x = offsets // 9 - 1
    step_y = offsets // 3 % 3 - 1
    step_z = offsets % 3 - 1
    cell_x = jnp.arange(NCX, dtype=jnp.int32).reshape(NCX, 1, 1, 1, 1)
    cell_y = jnp.arange(NCY, dtype=jnp.int32).reshape(1, NCY, 1, 1, 1)
    cell_z = jnp.arange(NCZ, dtype=jnp.int32).reshape(1, 1, NCZ, 1, 1)
    nearby = counts[(cell_x + step_x) % NCX, (cell_y + step_y) % NCY, (cell_z + step_z) % NCZ]
    general_ids = jax.random.randint(jax.random.fold_in(key, 10), offsets.shape, 0, nearby)
    own_slot = jnp.arange(CAP, dtype=jnp.int32).reshape(1, 1, 1, CAP, 1)
    other_step = jax.random.randint(jax.random.fold_in(key, 11), offsets.shape, 0, jnp.maximum(nearby - 1, 1))
    same_ids = (own_slot + 1 + other_step) % nearby
    slot_ids = jnp.where(offsets == 13, same_ids, general_ids)
    return (offsets * CAP + slot_ids).astype(jnp.int32)


def shard_levels(stream_key, dims, cuts, low, top_value):
    def one(axis_at, shards_of):
        heights = jax.random.uniform(jax.random.fold_in(jax.random.fold_in(stream_key, 6), axis_at), (shards_of,), jnp.float32, low / len(cuts), top_value / len(cuts))
        return jnp.repeat(jnp.exp(heights), dims[axis_at] // shards_of).reshape((-1,) + (1,) * (len(dims) - axis_at - 1))

    gain = one(*cuts[0])
    for cut in cuts[1:]:
        gain = gain * one(*cut)
    return gain


def gaussian(stream_key, dims, width, reach, split=(), held_as=jnp.bfloat16):
    values = jax.random.normal(stream_key, dims, jnp.float32) * width
    if len(split) > 0:
        values = shard_levels(stream_key, dims, split, -0.22, 0.18) * values
    return jnp.clip(values, min=-reach, max=reach).astype(held_as)


def setup_inputs(seed: int = 0) -> dict:
    seeds = jax.random.split(jax.random.key(seed), 13)
    return {
        "features": gaussian(seeds[0], (NCX, NCY, NCZ, CAP, L2, C), 1.0, 6.0, ((0, 8), (1, 4), (2, 8))),
        "cotangent": gaussian(seeds[1], (NCX, NCY, NCZ, CAP, L2, C), 0.1, 1.5, ((0, 8), (1, 4), (2, 8))),
        "counts": draw_counts(jax.random.fold_in(seeds[12], 71), 0),
        "sources": draw_sources(jax.random.fold_in(seeds[12], 71), 0),
        "wigner": gaussian(seeds[4], (WIG, NCX, NCY, NCZ, CAP, NBR), 0.35, 2.5, ((1, 8), (2, 4), (3, 8))),
        "distance": jnp.clip(1.0 + 4.5 * jax.random.uniform(seeds[5], (NCX, NCY, NCZ, CAP, NBR), jnp.float32) ** shard_levels(seeds[5], (NCX, NCY, NCZ, CAP, NBR), ((0, 8), (1, 4), (2, 8)), -0.2, 0.2), 1.0, 5.5),
        "direction": gaussian(seeds[6], (3, NCX, NCY, NCZ, CAP, NBR), 0.577, 3.0, ((1, 8), (2, 4), (3, 8)), jnp.float32),
        "weight_zero": gaussian(seeds[7], ((LMAX + 1) * C, (LMAX + 1) * C), ((LMAX + 1) * C) ** -0.5, 0.1875),
        "weight_one": gaussian(seeds[8], (2, LMAX * C, LMAX * C), (2 * LMAX * C) ** -0.5, 0.15625),
        "weight_two": gaussian(seeds[9], (2, (LMAX - 1) * C, (LMAX - 1) * C), (2 * (LMAX - 1) * C) ** -0.5, 0.15625),
        "radial_in": gaussian(seeds[10], (NB, HID), (NB // 8) ** -0.5, 1.0, (), jnp.float32),
        "radial_out": gaussian(seeds[11], (HID, (LMAX + 1) * C), HID ** -0.5, 0.5, (), jnp.float32),
    }


cutoff = 6.0
sigma_width = 0.5
highest = lax.Precision.HIGHEST

def block_rows(degree):
    return min(2 * degree + 1, 2 * MMAX + 1)

def rotate_forward(values, wigner):
    pieces = []
    offset = 0
    for degree in range(LMAX + 1):
        height = block_rows(degree)
        breadth = 2 * degree + 1
        wig_block = wigner[offset:offset + height * breadth].reshape(height, breadth, -1).astype(jnp.float32)
        offset += height * breadth
        section = values[:, degree * degree:degree * degree + breadth].astype(jnp.float32)
        pieces.append(jnp.einsum('rje,ejc->erc', wig_block, section, precision=highest))
    return pieces

def rotate_back(pieces, wigner):
    result = []
    offset = 0
    for degree in range(LMAX + 1):
        height = block_rows(degree)
        breadth = 2 * degree + 1
        wig_block = wigner[offset:offset + height * breadth].reshape(height, breadth, -1).astype(jnp.float32)
        offset += height * breadth
        result.append(jnp.einsum('rje,erc->ejc', wig_block, pieces[degree].astype(jnp.float32), precision=highest))
    return jnp.concatenate(result, axis=1)

def split_orders(pieces):
    groups = [jnp.stack([pieces[degree][:, min(degree, MMAX)] for degree in range(LMAX + 1)], axis=1)]
    for m_order in range(1, MMAX + 1):
        plus_rows = jnp.stack([pieces[degree][:, min(degree, MMAX) + m_order] for degree in range(m_order, LMAX + 1)], axis=1)
        minus_rows = jnp.stack([pieces[degree][:, min(degree, MMAX) - m_order] for degree in range(m_order, LMAX + 1)], axis=1)
        groups.append((plus_rows, minus_rows))
    return groups

def join_orders(groups):
    pieces = []
    for degree in range(LMAX + 1):
        top_order = min(degree, MMAX)
        row_list = []
        for m_order in range(-top_order, top_order + 1):
            if m_order == 0:
                row_list.append(groups[0][:, degree])
            elif m_order > 0:
                row_list.append(groups[m_order][0][:, degree - m_order])
            else:
                row_list.append(groups[-m_order][1][:, degree + m_order])
        pieces.append(jnp.stack(row_list, axis=1))
    return pieces

def times_transposed(left, weight):
    return lax.dot_general(left, weight, (((1,), (1,)), ((), ())), preferred_element_type=jnp.float32)

def mix_forward(groups, weight_zero, weight_one, weight_two):
    num_edges = groups[0].shape[0]
    channels = groups[0].shape[2]
    result = [jnp.dot(groups[0].reshape(num_edges, -1), weight_zero, preferred_element_type=jnp.float32).reshape(num_edges, LMAX + 1, channels)]
    for m_order, weight in ((1, weight_one), (2, weight_two)):
        plus_rows = groups[m_order][0].reshape(num_edges, -1)
        minus_rows = groups[m_order][1].reshape(num_edges, -1)
        first_out = jnp.dot(plus_rows, weight[0], preferred_element_type=jnp.float32) - jnp.dot(minus_rows, weight[1], preferred_element_type=jnp.float32)
        second_out = jnp.dot(plus_rows, weight[1], preferred_element_type=jnp.float32) + jnp.dot(minus_rows, weight[0], preferred_element_type=jnp.float32)
        shape_out = (num_edges, LMAX + 1 - m_order, channels)
        result.append((first_out.reshape(shape_out), second_out.reshape(shape_out)))
    return result

def mix_backward(groups, weight_zero, weight_one, weight_two):
    num_edges = groups[0].shape[0]
    channels = groups[0].shape[2]
    result = [times_transposed(groups[0].reshape(num_edges, -1), weight_zero).reshape(num_edges, LMAX + 1, channels)]
    for m_order, weight in ((1, weight_one), (2, weight_two)):
        plus_rows = groups[m_order][0].reshape(num_edges, -1)
        minus_rows = groups[m_order][1].reshape(num_edges, -1)
        grad_plus = times_transposed(plus_rows, weight[0]) + times_transposed(minus_rows, weight[1])
        grad_minus = times_transposed(minus_rows, weight[0]) - times_transposed(plus_rows, weight[1])
        shape_out = (num_edges, LMAX + 1 - m_order, channels)
        result.append((grad_plus.reshape(shape_out), grad_minus.reshape(shape_out)))
    return result

def local_pass(source_rows, own_rows, own_cot, occupied, wigner, distance, weight_zero, weight_one, weight_two, radial_in, radial_out):
    num_edges = distance.shape[0]
    num_slots = own_rows.shape[0]
    per_atom = num_edges // num_slots
    coeffs = own_rows.shape[1]
    channels = own_rows.shape[2]
    occupied_edge = jnp.repeat(occupied, per_atom)
    centers = jnp.arange(NB, dtype=jnp.float32) * (cutoff / (NB - 1))
    offset = distance[:, None] - centers[None, :]
    basis_vals = jnp.exp(-0.5 * (offset / sigma_width) ** 2)
    inner_sum = jnp.dot(basis_vals, radial_in, precision=highest)
    activated = jax.nn.silu(inner_sum)
    radial = jnp.dot(activated, radial_out, precision=highest).reshape(num_edges, LMAX + 1, channels)
    groups = split_orders(rotate_forward(source_rows, wigner))
    order_zero = groups[0]
    inputs = [(order_zero * radial).astype(jnp.bfloat16)] + [(pair[0].astype(jnp.bfloat16), pair[1].astype(jnp.bfloat16)) for pair in groups[1:]]
    mixed_out = mix_forward(inputs, weight_zero, weight_one, weight_two)
    hidden = [mixed_out[0].astype(jnp.bfloat16)] + [(pair[0].astype(jnp.bfloat16), pair[1].astype(jnp.bfloat16)) for pair in mixed_out[1:]]
    back_rot = rotate_back(join_orders(hidden), wigner)
    envelope = 0.5 * (jnp.cos(math.pi * distance / cutoff) + 1.0) * occupied_edge
    scale_fac = 1.0 / math.sqrt(per_atom)
    summed = lax.optimization_barrier(jnp.sum((back_rot * envelope[:, None, None]).reshape(num_slots, per_atom, coeffs, channels), axis=1))
    updated = ((own_rows.astype(jnp.float32) + scale_fac * summed) * occupied[:, None, None]).astype(jnp.bfloat16)
    cot_edges = jnp.broadcast_to(own_cot.astype(jnp.float32)[:, None], (num_slots, per_atom, coeffs, channels)).reshape(num_edges, coeffs, channels)
    grad_back = cot_edges * (envelope * scale_fac)[:, None, None]
    grad_env = lax.optimization_barrier(jnp.sum(cot_edges * back_rot, axis=(1, 2))) * scale_fac * occupied_edge
    grad_rot = split_orders(rotate_forward(grad_back, wigner))
    grad_mixed = [grad_rot[0].astype(jnp.bfloat16)] + [(pair[0].astype(jnp.bfloat16), pair[1].astype(jnp.bfloat16)) for pair in grad_rot[1:]]
    grad_input = mix_backward(grad_mixed, weight_zero, weight_one, weight_two)
    grad_radial = (grad_input[0] * order_zero).reshape(num_edges, -1)
    grad_rotated = [(grad_input[0] * radial).astype(jnp.bfloat16)] + [(pair[0].astype(jnp.bfloat16), pair[1].astype(jnp.bfloat16)) for pair in grad_input[1:]]
    grad_source = rotate_back(join_orders(grad_rotated), wigner)
    grad_act = lax.dot_general(grad_radial, radial_out, (((1,), (1,)), ((), ())), precision=highest)
    sigmoid_z = jax.nn.sigmoid(inner_sum)
    grad_inner = grad_act * sigmoid_z * (1.0 + inner_sum * (1.0 - sigmoid_z))
    grad_basis = lax.dot_general(grad_inner, radial_in, (((1,), (1,)), ((), ())), precision=highest)
    env_slope = -0.5 * (math.pi / cutoff) * jnp.sin(math.pi * distance / cutoff)
    grad_dist = grad_env * env_slope + lax.optimization_barrier(jnp.sum(grad_basis * basis_vals * (-offset / (sigma_width * sigma_width)), axis=1))
    return (updated, grad_source, grad_dist)

def padded_index(sources):
    cap_slots = sources.shape[3]
    cell_offset = sources // cap_slots
    slot_ids = sources % cap_slots
    pad_x = lax.broadcasted_iota(jnp.int32, sources.shape, 0) + cell_offset // 9
    pad_y = lax.broadcasted_iota(jnp.int32, sources.shape, 1) + cell_offset // 3 % 3
    pad_z = lax.broadcasted_iota(jnp.int32, sources.shape, 2) + cell_offset % 3
    return (((pad_x * 4 + pad_y) * 4 + pad_z) * cap_slots + slot_ids).reshape(-1).astype(jnp.int32)

def reference(features, cotangent, counts, sources, wigner, distance, direction, weight_zero, weight_one, weight_two, radial_in, radial_out):
    slot_range = jnp.arange(CAP, dtype=jnp.int32)
    occupied_all = (slot_range[None, None, None, :] < counts[..., None]).astype(jnp.float32)
    num_devices = N_GX * N_GY * N_GZ

    def device_step(state_pair, device):
        grad_all, force_all = state_pair
        dev_x = device // (N_GY * N_GZ)
        dev_y = device // N_GZ % N_GY
        dev_z = device % N_GZ
        four = jnp.arange(4, dtype=jnp.int32)
        two = jnp.arange(2, dtype=jnp.int32)
        cells_x = (2 * dev_x - 1 + four) % NCX
        cells_y = (2 * dev_y - 1 + four) % NCY
        cells_z = (2 * dev_z - 1 + four) % NCZ
        own_x = 2 * dev_x + two
        own_y = 2 * dev_y + two
        own_z = 2 * dev_z + two

        def own_take(array, first):
            taken = jnp.take(array, own_x, axis=first)
            taken = jnp.take(taken, own_y, axis=first + 1)
            return jnp.take(taken, own_z, axis=first + 2)
        padded = jnp.take(jnp.take(jnp.take(features, cells_x, axis=0), cells_y, axis=1), cells_z, axis=2)
        own_rows = padded[1:3, 1:3, 1:3].reshape(8 * CAP, L2, -1)
        own_cot = own_take(cotangent, 0).reshape(8 * CAP, L2, -1)
        own_occupied = own_take(occupied_all, 0).reshape(-1)
        own_sources = own_take(sources, 0)
        source_index = padded_index(own_sources)
        source_rows = padded.reshape(64 * CAP, L2, -1)[source_index]
        own_wigner = own_take(wigner, 1).reshape(WIG, -1)
        own_distance = own_take(distance, 0).reshape(-1)
        own_direction = own_take(direction, 1).reshape(3, -1)
        updated, grad_source, grad_dist = local_pass(source_rows, own_rows, own_cot, own_occupied, own_wigner, own_distance, weight_zero, weight_one, weight_two, radial_in, radial_out)
        edge_force = grad_dist[:, None] * own_direction.T
        grad_padded = jax.ops.segment_sum(grad_source, source_index, num_segments=64 * CAP).reshape(4, 4, 4, CAP, L2, -1)
        force_padded = jax.ops.segment_sum(edge_force, source_index, num_segments=64 * CAP).reshape(4, 4, 4, CAP, 3)
        target_force = -lax.optimization_barrier(jnp.sum(edge_force.reshape(2, 2, 2, CAP, NBR, 3), axis=4))
        grad_all = grad_all.at[cells_x[:, None, None], cells_y[None, :, None], cells_z[None, None, :]].add(grad_padded)
        force_all = force_all.at[cells_x[:, None, None], cells_y[None, :, None], cells_z[None, None, :]].add(force_padded)
        force_all = force_all.at[own_x[:, None, None], own_y[None, :, None], own_z[None, None, :]].add(target_force)
        return ((grad_all, force_all), updated.reshape(2, 2, 2, CAP, L2, -1))
    start = (jnp.zeros(features.shape, jnp.float32), jnp.zeros((NCX, NCY, NCZ, CAP, 3), jnp.float32))
    (grad_all, force_all), updates = lax.scan(device_step, start, jnp.arange(num_devices, dtype=jnp.int32))
    channels = features.shape[5]
    updates = updates.reshape(N_GX, N_GY, N_GZ, 2, 2, 2, CAP, L2, channels)
    updates = jnp.transpose(updates, (0, 3, 1, 4, 2, 5, 6, 7, 8)).reshape(NCX, NCY, NCZ, CAP, L2, channels)
    grad_features = grad_all + cotangent.astype(jnp.float32) * occupied_all[..., None, None]
    forces = jnp.moveaxis(force_all, 4, 0)
    return (updates, grad_features, forces)
```

```python
import math

import jax
import jax.numpy as jnp
import numpy as np
from jax import lax
from jax.experimental import pallas as pl
from jax.experimental.pallas import tpu as pltpu
from jax.sharding import PartitionSpec as P

LMAX = 6
NB = 256
E = 192
G = 24
CR = 104
cutoff = 6.0
sigma_width = 0.5
bf16 = jnp.bfloat16
f32 = jnp.float32
SCALE = 1.0 / math.sqrt(12.0)

PAIRS = (
    [((0, 2 * q), (0, 2 * q + 1)) for q in range(4)]
    + [((1, l), (-1, l)) for l in range(1, 7)]
    + [((2, l), (-2, l)) for l in range(2, 7)]
)


def rotation_table():
    starts = []
    total = 0
    for degree in range(LMAX + 1):
        starts.append(total)
        total += min(2 * degree + 1, 5) * (2 * degree + 1)
    table = np.zeros((256, 30 * 128), np.float32)
    for q, pair in enumerate(PAIRS):
        for half, (m, degree) in enumerate(pair):
            if degree > LMAX:
                continue
            breadth = 2 * degree + 1
            row = m + min(degree, 2)
            for col in range(breadth):
                for copy in range(2):
                    at = (2 * q + half) * 128 + copy * 64 + degree * degree + col
                    table[starts[degree] + row * breadth + col, at] = 1.0
    return table


def base_table():
    out = np.zeros((64,), np.int32)
    for px in range(4):
        for py in range(4):
            for pz in range(4):
                if px in (0, 3):
                    at = 784 + 392 * 2 + 784 * 2 + (px == 3) * 1568 + (py * 4 + pz) * 98
                elif pz in (0, 3):
                    at = 784 + 392 * 2 + (pz == 3) * 784 + ((px - 1) * 4 + py) * 98
                elif py in (0, 3):
                    at = 784 + (py == 3) * 392 + ((px - 1) * 2 + pz - 1) * 98
                else:
                    at = (((px - 1) * 2 + py - 1) * 2 + pz - 1) * 98
                out[(px * 4 + py) * 4 + pz] = at
    return out


def iota(shape, dim):
    return lax.broadcasted_iota(jnp.int32, shape, dim)


def dot(a, b):
    return lax.dot_general(a, b, (((1,), (0,)), ((), ())), preferred_element_type=f32)


def dot_nt(a, b):
    return lax.dot_general(a, b, (((1,), (1,)), ((), ())), preferred_element_type=f32)


def split2(a):
    hi = a.astype(bf16)
    return hi, (a - hi.astype(f32)).astype(bf16)


def dot3(a, b, op=dot):
    ah, al = split2(a)
    bh, bl = split2(b)
    return op(ah, bh) + (op(ah, bl) + op(al, bh))


def edge_ids():
    e = iota((E, 128), 0)
    cell = (e * 2731) >> 16
    rest = e - 24 * cell
    return cell, rest & 1, rest >> 1


def column(block):
    e = iota((E, 16), 0)
    cell = (e * 2731) >> 16
    rest = e - 24 * cell
    pick = (iota((E, 16), 1) == 2 * cell + (rest & 1)).astype(f32)
    rows = lax.dot_general(
        pick, block, (((1,), (0,)), ((), ())), precision=lax.Precision.HIGHEST, preferred_element_type=f32
    )
    e = iota((E, 12), 0)
    rest = e - 24 * ((e * 2731) >> 16)
    return jnp.sum(jnp.where(iota((E, 12), 1) == (rest >> 1), rows, 0.0), axis=1, keepdims=True)


def occupied_edges(counts_ref):
    cell, slot, _ = edge_ids()
    out = jnp.zeros((E, 128), f32)
    for c in range(8):
        out = jnp.where((cell == c) & (slot < counts_ref[c]), 1.0, out)
    return out


def basis_of(dist):
    centers = iota((E, NB), 1).astype(f32) * (cutoff / (NB - 1))
    offset = dist - centers
    return jnp.exp(-0.5 * (offset / sigma_width) ** 2), offset


def row_masks():
    r = iota((16, 128), 0) & 7
    h = iota((16, 128), 1) >> 6
    return [jnp.where(r == 2 * t + h, 1.0, 0.0).astype(bf16) for t in range(4)]


def lane_masks():
    lane = iota((16, 256), 1) & 7
    return [jnp.where(lane == e, 1.0, 0.0).astype(bf16) for e in range(8)]


def masked(block, mask):
    n, w = block.shape
    return (block.reshape(n // 16, 16, w) * mask[None]).reshape(n, w)


def padded_cell(q, cell):
    o = q >> 1
    dx = (o * 57) >> 9
    r = o - 9 * dx
    dy = (r * 11) >> 5
    dz = r - 3 * dy
    px = (cell >> 2) + dx
    py = ((cell >> 1) & 1) + dy
    pz = (cell & 1) + dz
    return (px * 4 + py) * 4 + pz


def pair_block(a, b):
    return jnp.concatenate([a.reshape(G, 8, 128), b.reshape(G, 8, 128)], axis=1).astype(bf16)


def z_place(m, degree):
    if m == 0:
        return 0, 0, degree * 128
    return abs(m), (0 if m > 0 else E), (degree - abs(m)) * 128


def kernel_a(
    wt_ref, tab_ref, cot_ref, dist_ref, counts_ref, src_ref, rin_ref, rout_ref, w0_ref, w1_ref, w2_ref,
    u_ref, v_ref, z0_ref, z1_ref, z2_ref, gi0_ref, rad_ref, inner_ref, xlo_ref, xhi_ref, mid_ref,
    w0v, w1v, w2v, gr_ref, acc_ref, cs_ref, env_ref, sems,
):
    copies = [
        pltpu.make_async_copy(src, dst, sems.at[i])
        for i, (src, dst) in enumerate(((w0_ref, w0v), (w1_ref, w1v), (w2_ref, w2v)))
    ]
    for c in copies:
        c.start()
    zs = (z0_ref, z1_ref, z2_ref)
    dist = column(dist_ref[...])
    basis, _ = basis_of(dist)
    inner = dot3(basis, rin_ref[...])
    inner_ref[...] = inner
    rad_ref[...] = dot3(inner * jax.nn.sigmoid(inner), rout_ref[...])
    env = 0.5 * (jnp.cos(jnp.broadcast_to(dist, (E, 128)) * (math.pi / cutoff)) + 1.0)
    env_ref[...] = env * (occupied_edges(counts_ref) * SCALE)
    wt = wt_ref[...]
    for q in range(15):
        res = dot(wt, tab_ref[:, 256 * q : 256 * q + 256])
        u_ref[:, 16 * q : 16 * q + 16, :] = pair_block(res[:, :128], res[:, 128:])
    u_ref[:, 240:256, :] = jnp.zeros((G, 16, 128), bf16)

    def turn(g, carry):
        v_ref[g] = u_ref[g].T[:64]
        return carry

    lax.fori_loop(0, G, turn, 0)
    cs_ref[0:784, :] = cot_ref[...].astype(f32)
    cs_ref[784:800, :] = jnp.zeros((16, 128), f32)
    m_rot = jnp.where((iota((16, 128), 0) & 1) == (iota((16, 128), 1) >> 6), 1.0, 0.0).astype(bf16)
    zero8 = jnp.zeros((8, 128), f32)

    def rotate(cp, carry):
        parts = []
        for half in range(2):
            cell = 2 * cp + half
            rhs = jnp.concatenate(
                [
                    cs_ref[pl.ds(98 * cell, 56, 2), :],
                    zero8,
                    cs_ref[pl.ds(98 * cell + 1, 56, 2), :],
                    zero8,
                ],
                axis=0,
            ).astype(bf16)
            for i in range(3):
                g = 3 * cell + i
                res = dot(masked(u_ref[g, 0:240, :], m_rot), rhs)
                scale = env_ref[pl.ds(pl.multiple_of(8 * g, 8), 8), :]
                parts.append(res.reshape(30, 8, 128) * scale[None])
        for j in range(3):
            both = jnp.concatenate([parts[2 * j], parts[2 * j + 1]], axis=1).astype(bf16)
            row = pl.multiple_of(48 * cp + 16 * j, 16)
            for q, pair in enumerate(PAIRS):
                for h, (m, degree) in enumerate(pair):
                    if degree <= LMAX:
                        z, up, col = z_place(m, degree)
                        zs[z][pl.ds(row + up, 16), col : col + 128] = both[2 * q + h]
        return carry

    lax.fori_loop(0, 4, rotate, 0)
    for c in copies:
        c.wait()
    gr_ref[:, 240:256, :] = jnp.zeros((G, 16, 128), bf16)
    z0 = z0_ref[...]
    for q in range(4):
        width = 256 if q < 3 else 128
        at = 256 * q
        gi = dot_nt(z0, w0v[at : at + width, :])
        gi0_ref[:, at : at + width] = gi
        gr = gi * rad_ref[:, at : at + width]
        second = gr[:, 128:] if q < 3 else jnp.zeros((E, 128), f32)
        gr_ref[:, 16 * q : 16 * q + 16, :] = pair_block(gr[:, :128], second)
    for m, wv, first in ((1, w1v, 4), (2, w2v, 10)):
        z = zs[m][...]
        count = 7 - m
        for l0 in range(0, count, 2):
            n = min(2, count - l0)
            a = dot_nt(z, wv[0, 128 * l0 : 128 * (l0 + n), :])
            b = dot_nt(z, wv[1, 128 * l0 : 128 * (l0 + n), :])
            gp = a[:E] + b[E:]
            gn = a[E:] - b[:E]
            for i in range(n):
                q = first + l0 + i
                gr_ref[:, 16 * q : 16 * q + 16, :] = pair_block(
                    gp[:, 128 * i : 128 * i + 128], gn[:, 128 * i : 128 * i + 128]
                )
    acc_ref[...] = jnp.zeros(acc_ref.shape, f32)
    row_ok = iota((56, 128), 0) < 49
    for cell in range(8):
        p = (((cell >> 2) + 1) * 4 + ((cell >> 1) & 1) + 1) * 4 + (cell & 1) + 1
        for s in range(2):
            occ = jnp.where(s < counts_ref[cell], 1.0, 0.0).astype(f32)
            acc_ref[pl.ds(p * CR + s, 56, 2), :] = jnp.where(
                row_ok, cs_ref[pl.ds(98 * cell + s, 56, 2), :] * occ, 0.0
            )
    masks = lane_masks()

    def back(cell, carry):
        for i in range(3):
            g = 3 * cell + i
            v = v_ref[g]
            lhs = jnp.concatenate([masked(v, m) for m in masks], axis=0)
            res = dot(lhs, gr_ref[g])
            for e in range(8):
                q = src_ref[2 * cell + (e & 1), 4 * i + (e >> 1)]
                row = padded_cell(q, cell) * CR + (q & 1)
                acc_ref[pl.ds(row, 56, 2), :] += res[64 * e : 64 * e + 56]
        return carry

    lax.fori_loop(0, 8, back, 0)
    xlo_ref[...] = acc_ref[0 : 16 * CR, :].astype(bf16)
    xhi_ref[...] = acc_ref[48 * CR : 64 * CR, :].astype(bf16)
    mid_ref[...] = acc_ref[16 * CR : 48 * CR, :]


def kernel_b(
    own_ref, ylo_ref, yhi_ref, zlo_ref, zhi_ref, xlo_ref, xhi_ref,
    base_ref, src_ref, counts_ref, srcv_ref, dist_ref, dir_ref,
    u_ref, v_ref, g0_ref, g1_ref, g2_ref, gi0_ref, rad_ref, inner_ref, rin_ref, rout_ref, w0_ref, w1_ref, w2_ref,
    upd_ref, force_ref,
    w0v, w1v, w2v, fs_ref, x0_ref, x1_ref, x2_ref, p0_ref, h_ref, env_ref, us_ref, sems,
):
    copies = [
        pltpu.make_async_copy(src, dst, sems.at[i])
        for i, (src, dst) in enumerate(((w0_ref, w0v), (w1_ref, w1v), (w2_ref, w2v)))
    ]
    for c in copies:
        c.start()
    at = 0
    for piece in (own_ref, ylo_ref, yhi_ref, zlo_ref, zhi_ref, xlo_ref, xhi_ref):
        n = piece.shape[0]
        fs_ref[at : at + n, :] = piece[...].astype(f32)
        at += n
    fs_ref[at : at + 16, :] = jnp.zeros((16, 128), f32)
    xs = (x0_ref, x1_ref, x2_ref)
    gs = (g0_ref, g1_ref, g2_ref)
    masks_r = row_masks()
    zero8 = jnp.zeros((8, 128), f32)

    def rotate(cp, carry):
        parts = []
        for half in range(2):
            cell = 2 * cp + half
            for i in range(3):
                g = 3 * cell + i
                rows = []
                for e in range(8):
                    q = src_ref[2 * cell + (e & 1), 4 * i + (e >> 1)]
                    base = base_ref[padded_cell(q, cell)] + (q & 1)
                    rows += [fs_ref[pl.ds(base, 56, 2), :], zero8]
                rhs = jnp.concatenate(rows, axis=0).astype(bf16)
                u = u_ref[g, 0:240, :]
                lhs = jnp.concatenate([masked(u, m) for m in masks_r], axis=1)
                parts.append(dot(lhs, rhs).reshape(30, 8, 128))
        for j in range(3):
            both = jnp.concatenate([parts[2 * j], parts[2 * j + 1]], axis=1)
            row = pl.multiple_of(48 * cp + 16 * j, 16)
            for q, pair in enumerate(PAIRS):
                for h, (m, degree) in enumerate(pair):
                    if degree > LMAX:
                        continue
                    z, up, col = z_place(m, degree)
                    value = both[2 * q + h]
                    if m == 0:
                        p0_ref[pl.ds(row, 16), col : col + 128] = value
                        value = value * rad_ref[pl.ds(row, 16), col : col + 128]
                    xs[z][pl.ds(row + up, 16), col : col + 128] = value.astype(bf16)
        return carry

    lax.fori_loop(0, 4, rotate, 0)
    for c in copies:
        c.wait()
    h_ref[:, 240:256, :] = jnp.zeros((G, 16, 128), bf16)
    along = jnp.zeros((E, 128), f32)

    def rounded(x):
        return x.astype(bf16).astype(f32)

    x0 = x0_ref[...]
    for q in range(4):
        width = 256 if q < 3 else 128
        at = 256 * q
        hid = rounded(dot(x0, w0v[:, at : at + width]))
        prod = hid * g0_ref[:, at : at + width].astype(f32)
        along = along + prod[:, :128]
        if q < 3:
            along = along + prod[:, 128:]
        second = hid[:, 128:] if q < 3 else jnp.zeros((E, 128), f32)
        h_ref[:, 16 * q : 16 * q + 16, :] = pair_block(hid[:, :128], second)
    for m, wv, first in ((1, w1v, 4), (2, w2v, 10)):
        x = xs[m][...]
        count = 7 - m
        for l0 in range(0, count, 2):
            n = min(2, count - l0)
            a = dot(x, wv[0, :, 128 * l0 : 128 * (l0 + n)])
            b = dot(x, wv[1, :, 128 * l0 : 128 * (l0 + n)])
            hp = rounded(a[:E] - b[E:])
            hn = rounded(b[:E] + a[E:])
            gp = gs[m][0:E, 128 * l0 : 128 * (l0 + n)].astype(f32)
            gn = gs[m][E : 2 * E, 128 * l0 : 128 * (l0 + n)].astype(f32)
            prod = hp * gp + hn * gn
            for i in range(n):
                cut = slice(128 * i, 128 * i + 128)
                along = along + prod[:, cut]
                q = first + l0 + i
                h_ref[:, 16 * q : 16 * q + 16, :] = pair_block(hp[:, cut], hn[:, cut])
    dist = column(dist_ref[...])
    angle = jnp.broadcast_to(dist, (E, 128)) * (math.pi / cutoff)
    env = 0.5 * (jnp.cos(angle) + 1.0)
    env_ref[...] = env
    slope = (-0.5 * math.pi / cutoff) * jnp.sin(angle)
    grad_env = jnp.sum(along, axis=1, keepdims=True) / env
    inner = inner_ref[...]
    grad_act = dot3(gi0_ref[...] * p0_ref[...], rout_ref[...], dot_nt)
    sig = jax.nn.sigmoid(inner)
    grad_inner = grad_act * sig * (1.0 + inner * (1.0 - sig))
    grad_basis = dot3(grad_inner, rin_ref[...], dot_nt)
    basis, offset = basis_of(dist)
    radial_part = jnp.sum(
        grad_basis * basis * (-offset / (sigma_width * sigma_width)), axis=1, keepdims=True
    )
    grad_dist = grad_env * slope + radial_part
    cell, slot, _ = edge_ids()
    q = jnp.broadcast_to(column(srcv_ref[...].astype(f32)), (E, 128)).astype(jnp.int32)
    lane = iota((E, 128), 1)
    from_slot = 2 * padded_cell(q, cell) + (q & 1)
    to_slot = 2 * padded_cell(jnp.full((E, 128), 26, jnp.int32), cell) + slot
    side = jnp.where(lane == from_slot, grad_dist, 0.0) - jnp.where(lane == to_slot, grad_dist, 0.0)
    force_ref[...] = jnp.zeros((8, 128), f32)
    for d in range(3):
        along_d = column(dir_ref[16 * d : 16 * d + 16, :])
        force_ref[d : d + 1, :] = jnp.sum(side * along_d, axis=0, keepdims=True)
    masks = lane_masks()

    def back(cell, carry):
        sums = [jnp.zeros((56, 128), f32), jnp.zeros((56, 128), f32)]
        for i in range(3):
            g = 3 * cell + i
            v = v_ref[g]
            lhs = jnp.concatenate([masked(v, m) for m in masks], axis=0)
            res = dot(lhs, h_ref[g])
            for e in range(8):
                scale = env_ref[pl.ds(8 * g + e, 1), :]
                sums[e & 1] = sums[e & 1] + res[64 * e : 64 * e + 56] * scale
        for s in range(2):
            occ = jnp.where(s < counts_ref[cell], 1.0, 0.0).astype(f32)
            own = fs_ref[pl.ds(98 * cell + s, 56, 2), :]
            us_ref[pl.ds(98 * cell + s, 56, 2), :] = (own + sums[s] * SCALE) * occ
        return carry

    lax.fori_loop(0, 8, back, 0)
    upd_ref[...] = us_ref[0:784, :].astype(bf16)


def fold_x(mid_ref, lo_ref, hi_ref, zlo_ref, zhi_ref, out_ref):
    for px in range(2):
        arrived = lo_ref if px == 0 else hi_ref
        for py in range(0, 4, 2):
            ends = {0: [], 3: []}
            for pj in range(2):
                for pz in range(4):
                    at = ((py + pj) * 4 + pz) * CR
                    both = mid_ref[px * 16 * CR + at : px * 16 * CR + at + CR, :]
                    if pz % 2 == 0:
                        pair = arrived[at : at + 2 * CR, :].astype(f32)
                    both = both + pair[(pz % 2) * CR : (pz % 2) * CR + CR]
                    if pz in ends:
                        ends[pz].append(both)
                    else:
                        to = ((px * 4 + py + pj) * 2 + pz - 1) * CR
                        out_ref[to : to + CR, :] = both
            to = (px * 4 + py) * CR
            zlo_ref[to : to + 2 * CR, :] = jnp.concatenate(ends[0], axis=0).astype(bf16)
            zhi_ref[to : to + 2 * CR, :] = jnp.concatenate(ends[3], axis=0).astype(bf16)


def fold_z(mid_ref, lo_ref, hi_ref, ylo_ref, yhi_ref, out_ref):
    for px in range(2):
        arrived = [[], []]
        for z, ref in enumerate((lo_ref, hi_ref)):
            for py in range(0, 4, 2):
                at = (px * 4 + py) * CR
                pair = ref[at : at + 2 * CR, :].astype(f32)
                arrived[z] += [pair[:CR], pair[CR:]]
        for py in range(4):
            done = []
            for z in range(2):
                at = ((px * 4 + py) * 2 + z) * CR
                done.append(mid_ref[at : at + CR, :] + arrived[z][py])
            if py in (0, 3):
                to = px * 2 * CR
                ref = ylo_ref if py == 0 else yhi_ref
                ref[to : to + 2 * CR, :] = jnp.concatenate(done, axis=0).astype(bf16)
            else:
                to = (px * 2 + py - 1) * 2 * CR
                out_ref[to : to + 2 * CR, :] = jnp.concatenate(done, axis=0)


def fold_y(mid_ref, lo_ref, hi_ref, out_ref):
    for px in range(2):
        for py, ref in enumerate((lo_ref, hi_ref)):
            pair = ref[px * 2 * CR : (px + 1) * 2 * CR, :].astype(f32)
            at = (px * 2 + py) * 2 * CR
            value = mid_ref[at : at + 2 * CR, :] + pair
            for z in range(2):
                to = ((px * 2 + py) * 2 + z) * 98
                out_ref[to : to + 98, :] = value[z * CR : z * CR + 98]


def fold_force(shift, bit, last):
    def kernel(mine_ref, lo_ref, hi_ref, out_ref):
        lane = iota((8, 128), 1)
        at = (lane >> bit) & 3
        lo = pltpu.roll(lo_ref[...], 128 - shift, 1)
        hi = pltpu.roll(hi_ref[...], shift, 1)
        total = mine_ref[...] + jnp.where(at == 1, lo, 0.0) + jnp.where(at == 2, hi, 0.0)
        if last:
            r = iota((128, 16), 0)
            o = iota((128, 16), 1)
            from_lane = ((o >> 3) + 1) * 32 + (((o >> 2) & 1) + 1) * 8 + (((o >> 1) & 1) + 1) * 2 + (o & 1)
            pick = (r == from_lane).astype(f32)
            out_ref[...] = lax.dot_general(
                total, pick, (((1,), (0,)), ((), ())), precision=lax.Precision.HIGHEST, preferred_element_type=f32
            )
        else:
            out_ref[...] = total

    return kernel


VM = pl.BlockSpec(memory_space=pltpu.VMEM)
SM = pl.BlockSpec(memory_space=pltpu.SMEM)
AN = pl.BlockSpec(memory_space=pl.ANY)


def shape(dims, dtype):
    return jax.ShapeDtypeStruct(dims, dtype)


def weights_scratch():
    return [pltpu.VMEM((896, 896), bf16), pltpu.VMEM((2, 768, 768), bf16), pltpu.VMEM((2, 640, 640), bf16)]


def call(kernel, out, specs, scratch, limit, name, cost=None):
    return pl.pallas_call(
        kernel,
        out_shape=out,
        in_specs=specs,
        out_specs=jax.tree.map(lambda _: VM, out),
        scratch_shapes=scratch,
        compiler_params=pltpu.CompilerParams(vmem_limit_bytes=limit),
        name=name,
        cost_estimate=cost,
    )


def run_a(wt, cot, dist, counts, src, rin, rout, w0, w1, w2):
    tab = jnp.asarray(rotation_table(), dtype=bf16)
    out = [
        shape((G, 256, 128), bf16), shape((G, 64, 256), bf16),
        shape((E, 896), bf16), shape((2 * E, 768), bf16), shape((2 * E, 640), bf16),
        shape((E, 896), f32), shape((E, 896), f32), shape((E, 128), f32),
        shape((16 * CR, 128), bf16), shape((16 * CR, 128), bf16), shape((32 * CR, 128), f32),
    ]
    scratch = weights_scratch() + [
        pltpu.VMEM((G, 256, 128), bf16), pltpu.VMEM((64 * CR + 16, 128), f32), pltpu.VMEM((800, 128), f32),
        pltpu.VMEM((E, 128), f32), pltpu.SemaphoreType.DMA((3,)),
    ]
    specs = [VM, VM, VM, VM, SM, SM, VM, VM, AN, AN, AN]
    return call(kernel_a, out, specs, scratch, 48 << 20, "backward_part",
                pl.CostEstimate(flops=2 * 10**10, bytes_accessed=20 << 20, transcendentals=10**5))(
        wt, tab, cot, dist, counts, src, rin, rout, w0, w1, w2
    )


def run_b(pieces, src, counts, dist, direction, saved, rin, rout, w0, w1, w2):
    out = [shape((784, 128), bf16), shape((8, 128), f32)]
    scratch = weights_scratch() + [
        pltpu.VMEM((6272 + 16, 128), f32),
        pltpu.VMEM((E, 896), bf16), pltpu.VMEM((2 * E, 768), bf16), pltpu.VMEM((2 * E, 640), bf16),
        pltpu.VMEM((E, 896), f32), pltpu.VMEM((G, 256, 128), bf16), pltpu.VMEM((E, 128), f32),
        pltpu.VMEM((800, 128), f32), pltpu.SemaphoreType.DMA((3,)),
    ]
    specs = [VM] * 7 + [SM, SM, SM] + [VM] * 13 + [AN] * 3
    return call(kernel_b, out, specs, scratch, 48 << 20, "forward_part",
                pl.CostEstimate(flops=2 * 10**10, bytes_accessed=20 << 20, transcendentals=10**5))(
        *pieces, jnp.asarray(base_table()), src, counts, src, dist, direction, *saved, rin, rout, w0, w1, w2
    )


def shifts(axis):
    n = lax.axis_size(axis)
    up = [(i, (i + 1) % n) for i in range(n)]
    return up, [(t, s) for s, t in up]


def exchange(to_up, to_down, axis):
    up, down = shifts(axis)
    return lax.ppermute(to_up, axis, up), lax.ppermute(to_down, axis, down)


def local(features, cotangent, counts, sources, wigner, distance, direction, w0, w1, w2, rin, rout):
    feats = jnp.transpose(features, (0, 1, 2, 4, 3, 5))
    ylo, yhi = exchange(feats[:, 1:2], feats[:, 0:1], "gy")
    tall = jnp.concatenate([ylo, feats, yhi], axis=1)
    zlo, zhi = exchange(tall[:, :, 1:2], tall[:, :, 0:1], "gz")
    top = jnp.concatenate([zlo[1:2], tall[1:2], zhi[1:2]], axis=2)
    low = jnp.concatenate([zlo[0:1], tall[0:1], zhi[0:1]], axis=2)
    xlo, xhi = exchange(top, low, "gx")
    rows = [p.reshape(-1, 128) for p in (feats, ylo, yhi, zlo, zhi, xlo, xhi)]

    cot = jnp.transpose(cotangent, (0, 1, 2, 4, 3, 5)).reshape(784, 128)
    wt = jnp.transpose(wigner, (1, 2, 3, 5, 4, 0)).reshape(E, -1)
    wt = jnp.pad(wt, ((0, 0), (0, 256 - wt.shape[1])))
    src = sources.reshape(16, 12)
    cnt = counts.reshape(8)
    dist = distance.reshape(16, 12)
    dirs = direction.reshape(48, 12)
    *saved, gxlo, gxhi, mid = run_a(wt, cot, dist, cnt, src, rin, rout, w0, w1, w2)
    updated, force = run_b(rows, src, cnt, dist, dirs, saved, rin, rout, w0, w1, w2)

    lo, hi = exchange(gxhi, gxlo, "gx")
    gzlo, gzhi, mid = call(
        fold_x,
        [shape((8 * CR, 128), bf16), shape((8 * CR, 128), bf16), shape((16 * CR, 128), f32)],
        [VM] * 3, [], 24 << 20, "fold_x",
    )(mid, lo, hi)
    lo, hi = exchange(gzhi, gzlo, "gz")
    gylo, gyhi, mid = call(
        fold_z,
        [shape((4 * CR, 128), bf16), shape((4 * CR, 128), bf16), shape((8 * CR, 128), f32)],
        [VM] * 3, [], 24 << 20, "fold_z",
    )(mid, lo, hi)
    lo, hi = exchange(gyhi, gylo, "gy")
    grads = call(fold_y, shape((784, 128), f32), [VM] * 3, [], 24 << 20, "fold_y")(mid, lo, hi)

    for axis, shift, bit in (("gx", 64, 5), ("gz", 4, 1), ("gy", 16, 3)):
        last = axis == "gy"
        lo, hi = exchange(force, force, axis)
        force = call(
            fold_force(shift, bit, last), shape((8, 16) if last else (8, 128), f32), [VM] * 3, [], 8 << 20,
            "fold_force_" + axis,
        )(force, lo, hi)
    forces = force[:3].reshape(3, 2, 2, 2, 2)

    def back(x):
        return jnp.transpose(x.reshape(2, 2, 2, 49, 2, 128), (0, 1, 2, 4, 3, 5))

    return back(updated), back(grads), forces


def solution(mesh):
    cells = P("gx", "gy", "gz")
    behind = P(None, "gx", "gy", "gz")
    in_specs = (cells, cells, cells, cells, behind, cells, behind, P(), P(), P(), P(), P())
    return jax.shard_map(local, mesh=mesh, in_specs=in_specs, out_specs=(cells, cells, behind), check_vma=False)
```

```python
import math

import jax
import jax.numpy as jnp
import numpy as np
from jax import lax
from jax.experimental import pallas as pl
from jax.experimental.pallas import tpu as pltpu
from jax.sharding import PartitionSpec as P

LMAX = 6
NB = 256
E = 192
G = 24
CR = 104
cutoff = 6.0
sigma_width = 0.5
bf16 = jnp.bfloat16
f32 = jnp.float32
SCALE = 1.0 / math.sqrt(12.0)

PAIRS = (
    [((0, 2 * q), (0, 2 * q + 1)) for q in range(4)]
    + [((1, l), (-1, l)) for l in range(1, 7)]
    + [((2, l), (-2, l)) for l in range(2, 7)]
)


def rotation_table():
    starts = []
    total = 0
    for degree in range(LMAX + 1):
        starts.append(total)
        total += min(2 * degree + 1, 5) * (2 * degree + 1)
    table = np.zeros((256, 30 * 128), np.float32)
    for q, pair in enumerate(PAIRS):
        for half, (m, degree) in enumerate(pair):
            if degree > LMAX:
                continue
            breadth = 2 * degree + 1
            row = m + min(degree, 2)
            for col in range(breadth):
                for copy in range(2):
                    at = (2 * q + half) * 128 + copy * 64 + degree * degree + col
                    table[starts[degree] + row * breadth + col, at] = 1.0
    return table


def base_table():
    out = np.zeros((64,), np.int32)
    for px in range(4):
        for py in range(4):
            for pz in range(4):
                if px in (0, 3):
                    at = 784 + 392 * 2 + 784 * 2 + (px == 3) * 1568 + (py * 4 + pz) * 98
                elif pz in (0, 3):
                    at = 784 + 392 * 2 + (pz == 3) * 784 + ((px - 1) * 4 + py) * 98
                elif py in (0, 3):
                    at = 784 + (py == 3) * 392 + ((px - 1) * 2 + pz - 1) * 98
                else:
                    at = (((px - 1) * 2 + py - 1) * 2 + pz - 1) * 98
                out[(px * 4 + py) * 4 + pz] = at
    return out


def iota(shape, dim):
    return lax.broadcasted_iota(jnp.int32, shape, dim)


def dot(a, b):
    return lax.dot_general(a, b, (((1,), (0,)), ((), ())), preferred_element_type=f32)


def dot_nt(a, b):
    return lax.dot_general(a, b, (((1,), (1,)), ((), ())), preferred_element_type=f32)


def split2(a):
    hi = a.astype(bf16)
    return hi, (a - hi.astype(f32)).astype(bf16)


def dot3(a, b, op=dot):
    ah, al = split2(a)
    bh, bl = split2(b)
    return op(ah, bh) + (op(ah, bl) + op(al, bh))


def edge_ids():
    e = iota((E, 128), 0)
    cell = (e * 2731) >> 16
    rest = e - 24 * cell
    return cell, rest & 1, rest >> 1


def column(block):
    e = iota((E, 16), 0)
    cell = (e * 2731) >> 16
    rest = e - 24 * cell
    pick = (iota((E, 16), 1) == 2 * cell + (rest & 1)).astype(f32)
    rows = lax.dot_general(
        pick, block, (((1,), (0,)), ((), ())), precision=lax.Precision.HIGHEST, preferred_element_type=f32
    )
    e = iota((E, 12), 0)
    rest = e - 24 * ((e * 2731) >> 16)
    return jnp.sum(jnp.where(iota((E, 12), 1) == (rest >> 1), rows, 0.0), axis=1, keepdims=True)


def occupied_edges(counts_ref):
    cell, slot, _ = edge_ids()
    out = jnp.zeros((E, 128), f32)
    for c in range(8):
        out = jnp.where((cell == c) & (slot < counts_ref[c >> 2, (c >> 1) & 1, c & 1]), 1.0, out)
    return out


def basis_of(dist):
    centers = iota((E, NB), 1).astype(f32) * (cutoff / (NB - 1))
    offset = dist - centers
    return jnp.exp(-0.5 * (offset / sigma_width) ** 2), offset


def row_masks():
    r = iota((16, 128), 0) & 7
    h = iota((16, 128), 1) >> 6
    return [jnp.where(r == 2 * t + h, 1.0, 0.0).astype(bf16) for t in range(4)]


def lane_masks():
    lane = iota((16, 256), 1) & 7
    return [jnp.where(lane == e, 1.0, 0.0).astype(bf16) for e in range(8)]


def masked(block, mask):
    n, w = block.shape
    return (block.reshape(n // 16, 16, w) * mask[None]).reshape(n, w)


def padded_cell(q, cell):
    o = q >> 1
    dx = (o * 57) >> 9
    r = o - 9 * dx
    dy = (r * 11) >> 5
    dz = r - 3 * dy
    px = (cell >> 2) + dx
    py = ((cell >> 1) & 1) + dy
    pz = (cell & 1) + dz
    return (px * 4 + py) * 4 + pz


def pair_block(a, b):
    return jnp.concatenate([a.reshape(G, 8, 128), b.reshape(G, 8, 128)], axis=1).astype(bf16)


def z_place(m, degree):
    if m == 0:
        return 0, 0, degree * 128
    return abs(m), (0 if m > 0 else E), (degree - abs(m)) * 128


def start_copies(pairs, sems):
    copies = [pltpu.make_async_copy(src, dst, sems.at[i]) for i, (src, dst) in enumerate(pairs)]
    for c in copies:
        c.start()
    return copies


def kernel_a1(
    wt_ref, tab_ref, cot_ref, dist_ref, counts_ref, srcv_ref, dir_ref, rin_ref, rout_ref,
    u_ref, v_ref, z0_ref, z1_ref, z2_ref, rad_ref, dsilu_ref, wb_ref, ratio_ref, envo_ref, side_ref, cs_ref,
    env_ref,
):
    zs = (z0_ref, z1_ref, z2_ref)
    dist = column(dist_ref[...])
    basis, offset = basis_of(dist)
    wb_ref[...] = basis * (-offset / (sigma_width * sigma_width))
    inner = dot3(basis, rin_ref[...])
    sig = jax.nn.sigmoid(inner)
    dsilu_ref[...] = sig * (1.0 + inner * (1.0 - sig))
    rad_ref[...] = dot3(inner * sig, rout_ref[...])
    angle = jnp.broadcast_to(dist, (E, 128)) * (math.pi / cutoff)
    env = 0.5 * (jnp.cos(angle) + 1.0)
    envo_ref[...] = env
    ratio_ref[...] = (-0.5 * math.pi / cutoff) * jnp.sin(angle) / env
    env_ref[...] = env * (occupied_edges(counts_ref) * SCALE)
    cell, slot, _ = edge_ids()
    q = jnp.broadcast_to(column(srcv_ref[...].astype(f32)), (E, 128)).astype(jnp.int32)
    lane = iota((E, 128), 1)
    from_slot = 2 * padded_cell(q, cell) + (q & 1)
    to_slot = 2 * padded_cell(jnp.full((E, 128), 26, jnp.int32), cell) + slot
    sign = jnp.where(lane == from_slot, 1.0, 0.0) - jnp.where(lane == to_slot, 1.0, 0.0)
    for d in range(3):
        side_ref[d] = sign * column(dir_ref[16 * d : 16 * d + 16, :])
    wt = wt_ref[...]
    for q in range(15):
        res = dot(wt, tab_ref[:, 256 * q : 256 * q + 256])
        u_ref[:, 16 * q : 16 * q + 16, :] = pair_block(res[:, :128], res[:, 128:])
    u_ref[:, 240:256, :] = jnp.zeros((G, 16, 128), bf16)

    def turn(g, carry):
        v_ref[g] = u_ref[g].T[:64]
        return carry

    lax.fori_loop(0, G, turn, 0)
    cs_ref[0:784, :] = cot_ref[...].astype(f32)
    cs_ref[784:800, :] = jnp.zeros((16, 128), f32)
    m_rot = jnp.where((iota((16, 128), 0) & 1) == (iota((16, 128), 1) >> 6), 1.0, 0.0).astype(bf16)
    zero8 = jnp.zeros((8, 128), f32)

    def rotate(cp, carry):
        parts = []
        for half in range(2):
            cell = 2 * cp + half
            rhs = jnp.concatenate(
                [
                    cs_ref[pl.ds(98 * cell, 56, 2), :],
                    zero8,
                    cs_ref[pl.ds(98 * cell + 1, 56, 2), :],
                    zero8,
                ],
                axis=0,
            ).astype(bf16)
            for i in range(3):
                g = 3 * cell + i
                res = dot(masked(u_ref[g, 0:240, :], m_rot), rhs)
                scale = env_ref[pl.ds(pl.multiple_of(8 * g, 8), 8), :]
                parts.append(res.reshape(30, 8, 128) * scale[None])
        for j in range(3):
            both = jnp.concatenate([parts[2 * j], parts[2 * j + 1]], axis=1).astype(bf16)
            row = pl.multiple_of(48 * cp + 16 * j, 16)
            for q, pair in enumerate(PAIRS):
                for h, (m, degree) in enumerate(pair):
                    if degree <= LMAX:
                        z, up, col = z_place(m, degree)
                        zs[z][pl.ds(row + up, 16), col : col + 128] = both[2 * q + h]
        return carry

    lax.fori_loop(0, 4, rotate, 0)


def kernel_a2(z0_ref, z1_ref, z2_ref, rad_ref, w0_ref, w1_ref, w2_ref, gi0_ref, gr_ref, w0v, w1v, w2v, sems):
    copies = start_copies(((w0_ref, w0v), (w1_ref, w1v), (w2_ref, w2v)), sems)
    zs = (z0_ref, z1_ref, z2_ref)
    gr_ref[:, 240:256, :] = jnp.zeros((G, 16, 128), bf16)
    z0 = z0_ref[...]
    copies[0].wait()
    for q in range(4):
        width = 256 if q < 3 else 128
        at = 256 * q
        gi = dot_nt(z0, w0v[at : at + width, :])
        gi0_ref[:, at : at + width] = gi
        gr = gi * rad_ref[:, at : at + width]
        second = gr[:, 128:] if q < 3 else jnp.zeros((E, 128), f32)
        gr_ref[:, 16 * q : 16 * q + 16, :] = pair_block(gr[:, :128], second)
    for m, wv, first in ((1, w1v, 4), (2, w2v, 10)):
        copies[m].wait()
        z = zs[m][...]
        count = 7 - m
        for l0 in range(0, count, 2):
            n = min(2, count - l0)
            a = dot_nt(z, wv[0, 128 * l0 : 128 * (l0 + n), :])
            b = dot_nt(z, wv[1, 128 * l0 : 128 * (l0 + n), :])
            gp = a[:E] + b[E:]
            gn = a[E:] - b[:E]
            for i in range(n):
                q = first + l0 + i
                gr_ref[:, 16 * q : 16 * q + 16, :] = pair_block(
                    gp[:, 128 * i : 128 * i + 128], gn[:, 128 * i : 128 * i + 128]
                )


def kernel_a3(v_ref, gr_ref, cs_ref, counts_ref, src_ref, xlo_ref, xhi_ref, mid_ref, acc_ref):
    acc_ref[...] = jnp.zeros(acc_ref.shape, f32)
    row_ok = iota((56, 128), 0) < 49
    for cell in range(8):
        p = (((cell >> 2) + 1) * 4 + ((cell >> 1) & 1) + 1) * 4 + (cell & 1) + 1
        for s in range(2):
            occ = jnp.where(s < counts_ref[cell >> 2, (cell >> 1) & 1, cell & 1], 1.0, 0.0).astype(f32)
            acc_ref[pl.ds(p * CR + s, 56, 2), :] = jnp.where(
                row_ok, cs_ref[pl.ds(98 * cell + s, 56, 2), :] * occ, 0.0
            )
    masks = lane_masks()

    def back(cell, carry):
        for i in range(3):
            g = 3 * cell + i
            v = v_ref[g]
            lhs = jnp.concatenate([masked(v, m) for m in masks], axis=0)
            res = dot(lhs, gr_ref[g])
            for e in range(8):
                q = src_ref[2 * cell + (e & 1), 4 * i + (e >> 1)]
                row = padded_cell(q, cell) * CR + (q & 1)
                acc_ref[pl.ds(row, 56, 2), :] += res[64 * e : 64 * e + 56]
        return carry

    lax.fori_loop(0, 8, back, 0)
    xlo_ref[...] = acc_ref[0 : 16 * CR, :].astype(bf16)
    xhi_ref[...] = acc_ref[48 * CR : 64 * CR, :].astype(bf16)
    mid_ref[...] = acc_ref[16 * CR : 48 * CR, :]


def kernel_b1(
    own_ref, ylo_ref, yhi_ref, zlo_ref, zhi_ref, xlo_ref, xhi_ref, base_ref, src_ref,
    u_ref, g0_ref, g1_ref, g2_ref, gi0_ref, rad_ref, dsilu_ref, wb_ref, ratio_ref, side_ref, rin_ref, rout_ref,
    w0_ref, w1_ref, w2_ref,
    h_ref, force_ref,
    w0v, w1v, w2v, fs_ref, x0_ref, x1_ref, x2_ref, p0_ref, sems,
):
    copies = start_copies(((w0_ref, w0v), (w1_ref, w1v), (w2_ref, w2v)), sems)
    at = 0
    for piece in (own_ref, ylo_ref, yhi_ref, zlo_ref, zhi_ref, xlo_ref, xhi_ref):
        n = piece.shape[0]
        fs_ref[at : at + n, :] = piece[...].astype(f32)
        at += n
    fs_ref[at : at + 16, :] = jnp.zeros((16, 128), f32)
    xs = (x0_ref, x1_ref, x2_ref)
    gs = (g0_ref, g1_ref, g2_ref)
    masks_r = row_masks()
    zero8 = jnp.zeros((8, 128), f32)

    def rotate(cp, carry):
        parts = []
        for half in range(2):
            cell = 2 * cp + half
            for i in range(3):
                g = 3 * cell + i
                rows = []
                for e in range(8):
                    q = src_ref[2 * cell + (e & 1), 4 * i + (e >> 1)]
                    base = base_ref[padded_cell(q, cell)] + (q & 1)
                    rows += [fs_ref[pl.ds(base, 56, 2), :], zero8]
                rhs = jnp.concatenate(rows, axis=0).astype(bf16)
                u = u_ref[g, 0:240, :]
                lhs = jnp.concatenate([masked(u, m) for m in masks_r], axis=1)
                parts.append(dot(lhs, rhs).reshape(30, 8, 128))
        for j in range(3):
            both = jnp.concatenate([parts[2 * j], parts[2 * j + 1]], axis=1)
            row = pl.multiple_of(48 * cp + 16 * j, 16)
            for q, pair in enumerate(PAIRS):
                for h, (m, degree) in enumerate(pair):
                    if degree > LMAX:
                        continue
                    z, up, col = z_place(m, degree)
                    value = both[2 * q + h]
                    if m == 0:
                        p0_ref[pl.ds(row, 16), col : col + 128] = value
                        value = value * rad_ref[pl.ds(row, 16), col : col + 128]
                    xs[z][pl.ds(row + up, 16), col : col + 128] = value.astype(bf16)
        return carry

    lax.fori_loop(0, 4, rotate, 0)
    h_ref[:, 240:256, :] = jnp.zeros((G, 16, 128), bf16)
    along = jnp.zeros((E, 128), f32)

    def rounded(x):
        return x.astype(bf16).astype(f32)

    copies[0].wait()
    x0 = x0_ref[...]
    for q in range(4):
        width = 256 if q < 3 else 128
        at = 256 * q
        hid = rounded(dot(x0, w0v[:, at : at + width]))
        prod = hid * g0_ref[:, at : at + width].astype(f32)
        along = along + prod[:, :128]
        if q < 3:
            along = along + prod[:, 128:]
        second = hid[:, 128:] if q < 3 else jnp.zeros((E, 128), f32)
        h_ref[:, 16 * q : 16 * q + 16, :] = pair_block(hid[:, :128], second)
    for m, wv, first in ((1, w1v, 4), (2, w2v, 10)):
        copies[m].wait()
        x = xs[m][...]
        count = 7 - m
        for l0 in range(0, count, 2):
            n = min(2, count - l0)
            a = dot(x, wv[0, :, 128 * l0 : 128 * (l0 + n)])
            b = dot(x, wv[1, :, 128 * l0 : 128 * (l0 + n)])
            hp = rounded(a[:E] - b[E:])
            hn = rounded(b[:E] + a[E:])
            gp = gs[m][0:E, 128 * l0 : 128 * (l0 + n)].astype(f32)
            gn = gs[m][E : 2 * E, 128 * l0 : 128 * (l0 + n)].astype(f32)
            prod = hp * gp + hn * gn
            for i in range(n):
                cut = slice(128 * i, 128 * i + 128)
                along = along + prod[:, cut]
                q = first + l0 + i
                h_ref[:, 16 * q : 16 * q + 16, :] = pair_block(hp[:, cut], hn[:, cut])
    grad_act = dot3(gi0_ref[...] * p0_ref[...], rout_ref[...], dot_nt)
    grad_basis = dot3(grad_act * dsilu_ref[...], rin_ref[...], dot_nt)
    parts = grad_basis * wb_ref[...]
    total = along * ratio_ref[...] + parts[:, :128] + parts[:, 128:]
    grad_dist = jnp.sum(total, axis=1, keepdims=True)
    force_ref[...] = jnp.zeros((8, 128), f32)
    for d in range(3):
        force_ref[d : d + 1, :] = jnp.sum(side_ref[d] * grad_dist, axis=0, keepdims=True)


def kernel_b2(own_ref, v_ref, h_ref, envo_ref, counts_ref, upd_ref, fs_ref, us_ref):
    fs_ref[0:784, :] = own_ref[...].astype(f32)
    fs_ref[784:800, :] = jnp.zeros((16, 128), f32)
    masks = lane_masks()

    def back(cell, carry):
        sums = [jnp.zeros((56, 128), f32), jnp.zeros((56, 128), f32)]
        for i in range(3):
            g = 3 * cell + i
            v = v_ref[g]
            lhs = jnp.concatenate([masked(v, m) for m in masks], axis=0)
            res = dot(lhs, h_ref[g])
            for e in range(8):
                scale = envo_ref[pl.ds(8 * g + e, 1), :]
                sums[e & 1] = sums[e & 1] + res[64 * e : 64 * e + 56] * scale
        for s in range(2):
            occ = jnp.where(s < counts_ref[cell >> 2, (cell >> 1) & 1, cell & 1], 1.0, 0.0).astype(f32)
            own = fs_ref[pl.ds(98 * cell + s, 56, 2), :]
            us_ref[pl.ds(98 * cell + s, 56, 2), :] = (own + sums[s] * SCALE) * occ
        return carry

    lax.fori_loop(0, 8, back, 0)
    upd_ref[...] = us_ref[0:784, :].astype(bf16)


def fold_x(mid_ref, lo_ref, hi_ref, zlo_ref, zhi_ref, out_ref):
    for px in range(2):
        arrived = lo_ref if px == 0 else hi_ref
        for py in range(0, 4, 2):
            ends = {0: [], 3: []}
            for pj in range(2):
                for pz in range(4):
                    at = ((py + pj) * 4 + pz) * CR
                    both = mid_ref[px * 16 * CR + at : px * 16 * CR + at + CR, :]
                    if pz % 2 == 0:
                        pair = arrived[at : at + 2 * CR, :].astype(f32)
                    both = both + pair[(pz % 2) * CR : (pz % 2) * CR + CR]
                    if pz in ends:
                        ends[pz].append(both)
                    else:
                        to = ((px * 4 + py + pj) * 2 + pz - 1) * CR
                        out_ref[to : to + CR, :] = both
            to = (px * 4 + py) * CR
            zlo_ref[to : to + 2 * CR, :] = jnp.concatenate(ends[0], axis=0).astype(bf16)
            zhi_ref[to : to + 2 * CR, :] = jnp.concatenate(ends[3], axis=0).astype(bf16)


def fold_z(mid_ref, lo_ref, hi_ref, ylo_ref, yhi_ref, out_ref):
    for px in range(2):
        arrived = [[], []]
        for z, ref in enumerate((lo_ref, hi_ref)):
            for py in range(0, 4, 2):
                at = (px * 4 + py) * CR
                pair = ref[at : at + 2 * CR, :].astype(f32)
                arrived[z] += [pair[:CR], pair[CR:]]
        for py in range(4):
            done = []
            for z in range(2):
                at = ((px * 4 + py) * 2 + z) * CR
                done.append(mid_ref[at : at + CR, :] + arrived[z][py])
            if py in (0, 3):
                to = px * 2 * CR
                ref = ylo_ref if py == 0 else yhi_ref
                ref[to : to + 2 * CR, :] = jnp.concatenate(done, axis=0).astype(bf16)
            else:
                to = (px * 2 + py - 1) * 2 * CR
                out_ref[to : to + 2 * CR, :] = jnp.concatenate(done, axis=0)


def fold_y(mid_ref, lo_ref, hi_ref, out_ref):
    for px in range(2):
        for py, ref in enumerate((lo_ref, hi_ref)):
            pair = ref[px * 2 * CR : (px + 1) * 2 * CR, :].astype(f32)
            at = (px * 2 + py) * 2 * CR
            value = mid_ref[at : at + 2 * CR, :] + pair
            for z in range(2):
                to = ((px * 2 + py) * 2 + z) * 98
                out_ref[to : to + 98, :] = value[z * CR : z * CR + 98]


def fold_force(shift, bit, last):
    def kernel(mine_ref, lo_ref, hi_ref, out_ref):
        lane = iota((8, 128), 1)
        at = (lane >> bit) & 3
        lo = pltpu.roll(lo_ref[...], 128 - shift, 1)
        hi = pltpu.roll(hi_ref[...], shift, 1)
        total = mine_ref[...] + jnp.where(at == 1, lo, 0.0) + jnp.where(at == 2, hi, 0.0)
        if last:
            r = iota((16, 128), 1)
            o = iota((16, 128), 0)
            from_lane = ((o >> 3) + 1) * 32 + (((o >> 2) & 1) + 1) * 8 + (((o >> 1) & 1) + 1) * 2 + (o & 1)
            pick = (r == from_lane).astype(f32)
            out_ref[...] = lax.dot_general(
                pick, total, (((1,), (1,)), ((), ())), precision=lax.Precision.HIGHEST, preferred_element_type=f32
            )[:, :3]
        else:
            out_ref[...] = total

    return kernel


VM = pl.BlockSpec(memory_space=pltpu.VMEM)
SM = pl.BlockSpec(memory_space=pltpu.SMEM)
AN = pl.BlockSpec(memory_space=pl.ANY)


def shape(dims, dtype):
    return jax.ShapeDtypeStruct(dims, dtype)


def weights_scratch():
    return [pltpu.VMEM((896, 896), bf16), pltpu.VMEM((2, 768, 768), bf16), pltpu.VMEM((2, 640, 640), bf16)]


def call(kernel, out, specs, scratch, limit, name, cost=None):
    return pl.pallas_call(
        kernel,
        out_shape=out,
        in_specs=specs,
        out_specs=jax.tree.map(lambda _: VM, out),
        scratch_shapes=scratch,
        compiler_params=pltpu.CompilerParams(vmem_limit_bytes=limit),
        name=name,
        cost_estimate=cost,
    )


def cost(us):
    return pl.CostEstimate(flops=int(us * 10**9), bytes_accessed=1 << 20, transcendentals=0)


def run_a1(wt, cot, dist, counts, src, dirs, rin, rout):
    tab = jnp.asarray(rotation_table(), dtype=bf16)
    out = [
        shape((G, 256, 128), bf16), shape((G, 64, 256), bf16),
        shape((E, 896), bf16), shape((2 * E, 768), bf16), shape((2 * E, 640), bf16),
        shape((E, 896), f32), shape((E, 128), f32), shape((E, NB), f32), shape((E, 128), f32), shape((E, 128), f32),
        shape((3, E, 128), f32), shape((800, 128), f32),
    ]
    specs = [VM, VM, VM, VM, SM, VM, VM, VM, VM]
    return call(kernel_a1, out, specs, [pltpu.VMEM((E, 128), f32)], 24 << 20, "rotations", cost(8))(
        wt, tab, cot, dist, counts, src, dirs, rin, rout
    )


def run_a2(z0, z1, z2, rad, w0, w1, w2):
    out = [shape((E, 896), f32), shape((G, 256, 128), bf16)]
    scratch = weights_scratch() + [pltpu.SemaphoreType.DMA((3,))]
    return call(kernel_a2, out, [VM] * 4 + [AN] * 3, scratch, 24 << 20, "mix_backward", cost(5))(
        z0, z1, z2, rad, w0, w1, w2
    )


def run_a3(v, gr, cs, counts, src):
    out = [shape((16 * CR, 128), bf16), shape((16 * CR, 128), bf16), shape((32 * CR, 128), f32)]
    scratch = [pltpu.VMEM((64 * CR + 16, 128), f32)]
    return call(kernel_a3, out, [VM, VM, VM, SM, SM], scratch, 20 << 20, "source_gradients", cost(4))(
        v, gr, cs, counts, src
    )


def run_b1(pieces, src, saved, rin, rout, w0, w1, w2):
    out = [shape((G, 256, 128), bf16), shape((8, 128), f32)]
    scratch = weights_scratch() + [
        pltpu.VMEM((6272 + 16, 128), f32),
        pltpu.VMEM((E, 896), bf16), pltpu.VMEM((2 * E, 768), bf16), pltpu.VMEM((2 * E, 640), bf16),
        pltpu.VMEM((E, 896), f32), pltpu.SemaphoreType.DMA((3,)),
    ]
    specs = [VM] * 7 + [SM, SM] + [VM] * 12 + [AN] * 3
    return call(kernel_b1, out, specs, scratch, 36 << 20, "hidden_and_forces", cost(9))(
        *pieces, jnp.asarray(base_table()), src, *saved, rin, rout, w0, w1, w2
    )


def run_b2(own, v, h, envo, counts):
    scratch = [pltpu.VMEM((800, 128), f32), pltpu.VMEM((800, 128), f32)]
    return call(kernel_b2, shape((784, 128), bf16), [VM] * 4 + [SM], scratch, 16 << 20, "updated", cost(3))(
        own, v, h, envo, counts
    )


def shifts(axis):
    n = lax.axis_size(axis)
    up = [(i, (i + 1) % n) for i in range(n)]
    return up, [(t, s) for s, t in up]


def exchange(to_up, to_down, axis):
    up, down = shifts(axis)
    return lax.ppermute(to_up, axis, up), lax.ppermute(to_down, axis, down)


def add_force(force, lo, hi, shift, bit, last=False):
    out = shape((16, 3) if last else (8, 128), f32)
    return call(fold_force(shift, bit, last), out, [VM] * 3, [], 8 << 20, "fold_force", cost(0.2))(force, lo, hi)


def tie(*values):
    return lax.optimization_barrier(values)


def test_run(pieces, wt, cot, src, cnt, dist, dirs, w0, w1, w2, rin, rout):
    cnt = cnt.reshape(2, 2, 2)
    u, v, z0, z1, z2, rad, dsilu, wb, ratio, envo, side, cs = run_a1(wt, cot, dist, cnt, src, dirs, rin, rout)
    gi0, gr = run_a2(z0, z1, z2, rad, w0, w1, w2)
    gxlo, gxhi, mid = run_a3(v, gr, cs, cnt, src)
    h, force = run_b1(pieces, src, (u, z0, z1, z2, gi0, rad, dsilu, wb, ratio, side), rin, rout, w0, w1, w2)
    return run_b2(pieces[0], v, h, envo, cnt), force, gxlo, gxhi, mid


def local(features, cotangent, counts, sources, wigner, distance, direction, w0, w1, w2, rin, rout):
    cot = jnp.transpose(cotangent, (0, 1, 2, 4, 3, 5)).reshape(784, 128)
    wt = jnp.transpose(wigner, (1, 2, 3, 5, 4, 0)).reshape(E, -1)
    wt = jnp.pad(wt, ((0, 0), (0, 256 - wt.shape[1])))
    src = sources.reshape(16, 12)
    dist = distance.reshape(16, 12)
    dirs = direction.reshape(48, 12)
    feats = jnp.transpose(features, (0, 1, 2, 4, 3, 5))

    ylo, yhi = exchange(feats[:, 1:2], feats[:, 0:1], "gy")
    a1 = run_a1(wt, cot, dist, counts, src, dirs, rin, rout)
    a1, ylo, yhi = tie(a1, ylo, yhi)
    u, v, z0, z1, z2, rad, dsilu, wb, ratio, envo, side, cs = a1
    tall = jnp.concatenate([ylo, feats, yhi], axis=1)
    up, down = tall[:, :, 1:2], tall[:, :, 0:1]
    (z0, z1, z2, rad), up, down = tie((z0, z1, z2, rad), up, down)
    zlo, zhi = exchange(up, down, "gz")
    gi0, gr = run_a2(z0, z1, z2, rad, w0, w1, w2)
    gr, zlo, zhi = tie(gr, zlo, zhi)
    top = jnp.concatenate([zlo[1:2], tall[1:2], zhi[1:2]], axis=2)
    low = jnp.concatenate([zlo[0:1], tall[0:1], zhi[0:1]], axis=2)
    gr, top, low = tie(gr, top, low)
    xlo, xhi = exchange(top, low, "gx")
    gxlo, gxhi, mid = run_a3(v, gr, cs, counts, src)
    gxlo, gxhi, mid, xlo, xhi = tie(gxlo, gxhi, mid, xlo, xhi)

    lo, hi = exchange(gxhi, gxlo, "gx")
    rows = [p.reshape(-1, 128) for p in (feats, ylo, yhi, zlo, zhi, xlo, xhi)]
    h, force = run_b1(rows, src, (u, z0, z1, z2, gi0, rad, dsilu, wb, ratio, side), rin, rout, w0, w1, w2)
    h, force, lo, hi = tie(h, force, lo, hi)
    flo, fhi = exchange(force, force, "gx")
    gzlo, gzhi, mid = call(
        fold_x,
        [shape((8 * CR, 128), bf16), shape((8 * CR, 128), bf16), shape((16 * CR, 128), f32)],
        [VM] * 3, [], 16 << 20, "fold_x", cost(1),
    )(mid, lo, hi)
    lo, hi = exchange(gzhi, gzlo, "gz")
    force = add_force(force, flo, fhi, 64, 5)
    force, h = tie(force, h)
    flo, fhi = exchange(force, force, "gz")
    updated = run_b2(rows[0], v, h, envo, counts)
    updated, flo, fhi = tie(updated, flo, fhi)
    force = add_force(force, flo, fhi, 4, 1)
    flo, fhi = exchange(force, force, "gy")
    gylo, gyhi, mid = call(
        fold_z,
        [shape((4 * CR, 128), bf16), shape((4 * CR, 128), bf16), shape((8 * CR, 128), f32)],
        [VM] * 3, [], 16 << 20, "fold_z", cost(1),
    )(mid, lo, hi)
    lo, hi = exchange(gyhi, gylo, "gy")
    force = add_force(force, flo, fhi, 16, 3, True)
    grads = call(fold_y, shape((784, 128), f32), [VM] * 3, [], 16 << 20, "fold_y", cost(1))(mid, lo, hi)
    forces = jnp.moveaxis(force.reshape(2, 2, 2, 2, 3), 4, 0)

    def back(x):
        return jnp.transpose(x.reshape(2, 2, 2, 49, 2, 128), (0, 1, 2, 4, 3, 5))

    return back(updated), back(grads), forces


def solution(mesh):
    cells = P("gx", "gy", "gz")
    behind = P(None, "gx", "gy", "gz")
    in_specs = (cells, cells, cells, cells, behind, cells, behind, P(), P(), P(), P(), P())
    return jax.shard_map(local, mesh=mesh, in_specs=in_specs, out_specs=(cells, cells, behind), check_vma=False)
```

```python
import math

import jax
import jax.numpy as jnp
import numpy as np
from jax import lax
from jax.experimental import pallas as pl
from jax.experimental.pallas import tpu as pltpu
from jax.sharding import PartitionSpec as P

LMAX = 6
NB = 256
E = 192
G = 24
CR = 104
cutoff = 6.0
sigma_width = 0.5
bf16 = jnp.bfloat16
f32 = jnp.float32
SCALE = 1.0 / math.sqrt(12.0)

PAIRS = (
    [((0, 2 * q), (0, 2 * q + 1)) for q in range(4)]
    + [((1, l), (-1, l)) for l in range(1, 7)]
    + [((2, l), (-2, l)) for l in range(2, 7)]
)


def row_starts():
    starts = []
    total = 0
    for degree in range(LMAX + 1):
        starts.append(total)
        total += min(2 * degree + 1, 5) * (2 * degree + 1)
    out = []
    for pair in PAIRS:
        for m, degree in pair:
            if degree > LMAX:
                out.append((-1, 0))
            else:
                out.append((starts[degree] + (m + min(degree, 2)) * (2 * degree + 1), degree))
    return out


def expansion(q):
    rows = row_starts()
    lane = iota((1, 256), 1)
    j = lane & 63
    target = jnp.full((1, 256), -1, jnp.int32)
    for h in range(2):
        start, degree = rows[2 * q + h]
        if start >= 0:
            low = degree * degree
            inside = ((lane >> 7) == h) & (j >= low) & (j < low + 2 * degree + 1)
            target = jnp.where(inside, start + j - low, target)
    return jnp.where(iota((256, 256), 0) == target, 1.0, 0.0).astype(bf16)


def base_table():
    out = np.zeros((64,), np.int32)
    for px in range(4):
        for py in range(4):
            for pz in range(4):
                if px in (0, 3):
                    at = 784 + 392 * 2 + 784 * 2 + (px == 3) * 1568 + (py * 4 + pz) * 98
                elif pz in (0, 3):
                    at = 784 + 392 * 2 + (pz == 3) * 784 + ((px - 1) * 4 + py) * 98
                elif py in (0, 3):
                    at = 784 + (py == 3) * 392 + ((px - 1) * 2 + pz - 1) * 98
                else:
                    at = (((px - 1) * 2 + py - 1) * 2 + pz - 1) * 98
                out[(px * 4 + py) * 4 + pz] = at
    return out


def iota(shape, dim):
    return lax.broadcasted_iota(jnp.int32, shape, dim)


def dot(a, b):
    return lax.dot_general(a, b, (((1,), (0,)), ((), ())), preferred_element_type=f32)


def dot_nt(a, b):
    return lax.dot_general(a, b, (((1,), (1,)), ((), ())), preferred_element_type=f32)


def split2(a):
    hi = a.astype(bf16)
    return hi, (a - hi.astype(f32)).astype(bf16)


def dot3(a, b, op=dot):
    ah, al = split2(a)
    bh, bl = split2(b)
    return op(ah, bh) + (op(ah, bl) + op(al, bh))


def edge_ids():
    e = iota((E, 128), 0)
    cell = (e * 2731) >> 16
    rest = e - 24 * cell
    return cell, rest & 1, rest >> 1


def column(block):
    e = iota((E, 16), 0)
    cell = (e * 2731) >> 16
    rest = e - 24 * cell
    pick = (iota((E, 16), 1) == 2 * cell + (rest & 1)).astype(f32)
    rows = lax.dot_general(
        pick, block, (((1,), (0,)), ((), ())), precision=lax.Precision.HIGHEST, preferred_element_type=f32
    )
    e = iota((E, 12), 0)
    rest = e - 24 * ((e * 2731) >> 16)
    return jnp.sum(jnp.where(iota((E, 12), 1) == (rest >> 1), rows, 0.0), axis=1, keepdims=True)


def occupied_edges(counts_ref):
    cell, slot, _ = edge_ids()
    out = jnp.zeros((E, 128), f32)
    for c in range(8):
        out = jnp.where((cell == c) & (slot < counts_ref[c >> 2, (c >> 1) & 1, c & 1]), 1.0, out)
    return out


def basis_of(dist):
    centers = iota((E, NB), 1).astype(f32) * (cutoff / (NB - 1))
    offset = dist - centers
    return jnp.exp(-0.5 * (offset / sigma_width) ** 2), offset


def row_masks():
    r = iota((16, 128), 0) & 3
    h = iota((16, 128), 1) >> 6
    return [jnp.where(r == 2 * t + h, 1.0, 0.0).astype(bf16) for t in range(2)]


def lane_masks():
    lane = iota((16, 256), 1) & 7
    return [jnp.where(lane == e, 1.0, 0.0).astype(bf16) for e in range(8)]


def masked(block, mask):
    n, w = block.shape
    return (block.reshape(n // 16, 16, w) * mask[None]).reshape(n, w)


def padded_cell(q, cell):
    o = q >> 1
    dx = (o * 57) >> 9
    r = o - 9 * dx
    dy = (r * 11) >> 5
    dz = r - 3 * dy
    px = (cell >> 2) + dx
    py = ((cell >> 1) & 1) + dy
    pz = (cell & 1) + dz
    return (px * 4 + py) * 4 + pz


def pair_block(a, b):
    return jnp.concatenate([a.reshape(G, 8, 128), b.reshape(G, 8, 128)], axis=1).astype(bf16)


def z_place(m, degree):
    if m == 0:
        return 0, 0, degree * 128
    return abs(m), (0 if m > 0 else E), (degree - abs(m)) * 128


def start_copies(pairs, sems):
    copies = [pltpu.make_async_copy(src, dst, sems.at[i]) for i, (src, dst) in enumerate(pairs)]
    for c in copies:
        c.start()
    return copies


def kernel_a1(
    wt_ref, counts_hbm, dist_hbm, rin_hbm, rout_hbm, cot_hbm,
    u_ref, z0_ref, z1_ref, z2_ref, rad_ref, dsilu_ref, wb_ref, ratio_ref, envl_ref, cs_ref,
    dist_ref, rin_ref, rout_ref, cot_ref, counts_ref, env_ref, sems,
):
    copies = start_copies(
        ((dist_hbm, dist_ref), (rin_hbm, rin_ref), (rout_hbm, rout_ref), (cot_hbm, cot_ref), (counts_hbm, counts_ref)), sems
    )
    zs = (z0_ref, z1_ref, z2_ref)
    copies[0].wait()
    copies[1].wait()
    dist = column(dist_ref[...])
    basis, offset = basis_of(dist)
    wb_ref[...] = basis * (-offset / (sigma_width * sigma_width))
    inner = dot3(basis, rin_ref[...])
    sig = jax.nn.sigmoid(inner)
    dsilu_ref[...] = sig * (1.0 + inner * (1.0 - sig))
    copies[2].wait()
    copies[4].wait()
    rad_ref[...] = dot3(inner * sig, rout_ref[...])
    angle = jnp.broadcast_to(dist, (E, 128)) * (math.pi / cutoff)
    env = 0.5 * (jnp.cos(angle) + 1.0)
    pick = ((iota((G, E), 1) >> 3) == iota((G, E), 0)).astype(f32)
    spread = jnp.where(
        (iota((E, 256), 0) & 7) == (iota((E, 256), 1) & 7), jnp.concatenate([env, env], axis=1) * SCALE, 0.0
    )
    envl_ref[...] = lax.dot_general(
        pick, spread, (((1,), (0,)), ((), ())), precision=lax.Precision.HIGHEST, preferred_element_type=f32
    )
    ratio_ref[...] = (-0.5 * math.pi / cutoff) * jnp.sin(angle) / env
    env_ref[...] = env * (occupied_edges(counts_ref) * SCALE)
    wt = wt_ref[...]
    for q in range(15):
        res = dot(wt, expansion(q))
        u_ref[:, 16 * q : 16 * q + 16, :] = pair_block(res[:, :128], res[:, 128:])
    u_ref[:, 240:256, :] = jnp.zeros((G, 16, 128), bf16)

    copies[3].wait()
    cs_ref[0:784, :] = cot_ref[...].astype(f32)
    cs_ref[784:800, :] = jnp.zeros((16, 128), f32)
    m_rot = jnp.where((iota((16, 128), 0) & 1) == (iota((16, 128), 1) >> 6), 1.0, 0.0).astype(bf16)
    zero8 = jnp.zeros((8, 128), f32)

    def rotate(cp, carry):
        parts = []
        for half in range(2):
            cell = 2 * cp + half
            rhs = jnp.concatenate(
                [
                    cs_ref[pl.ds(98 * cell, 56, 2), :],
                    zero8,
                    cs_ref[pl.ds(98 * cell + 1, 56, 2), :],
                    zero8,
                ],
                axis=0,
            ).astype(bf16)
            for i in range(3):
                g = 3 * cell + i
                res = dot(masked(u_ref[g, 0:240, :], m_rot), rhs)
                scale = env_ref[pl.ds(pl.multiple_of(8 * g, 8), 8), :]
                parts.append(res.reshape(30, 8, 128) * scale[None])
        for j in range(3):
            both = jnp.concatenate([parts[2 * j], parts[2 * j + 1]], axis=1).astype(bf16)
            row = pl.multiple_of(48 * cp + 16 * j, 16)
            for q, pair in enumerate(PAIRS):
                for h, (m, degree) in enumerate(pair):
                    if degree <= LMAX:
                        z, up, col = z_place(m, degree)
                        zs[z][pl.ds(row + up, 16), col : col + 128] = both[2 * q + h]
        return carry

    lax.fori_loop(0, 4, rotate, 0)


def halves(k0, k1):
    low = (iota((1, 8, 128), 1) < 4)
    return jnp.where(low, k0, pltpu.roll(k1, 4, 1)), jnp.where(low, pltpu.roll(k0, 4, 1), k1)


def kernel_a2(u_ref, z0_ref, z1_ref, z2_ref, rad_ref, w0v, w1v, w2v, gi0_ref, gr_ref, v_ref, u4_ref):
    def turn(g, carry):
        u = u_ref[g]
        v_ref[g] = u.T[:64]
        pairs = u.astype(f32).reshape(16, 2, 8, 128)
        a, b = halves(pairs[:, 0], pairs[:, 1])
        u4_ref[g, 0] = a.reshape(128, 128).astype(bf16)
        u4_ref[g, 1] = b.reshape(128, 128).astype(bf16)
        return carry

    lax.fori_loop(0, G, turn, 0)
    zs = (z0_ref, z1_ref, z2_ref)
    gr_ref[:, 240:256, :] = jnp.zeros((G, 16, 128), bf16)
    z0 = z0_ref[...]
    for q in range(4):
        width = 256 if q < 3 else 128
        at = 256 * q
        gi = dot_nt(z0, w0v[at : at + width, :])
        gi0_ref[:, at : at + width] = gi
        gr = gi * rad_ref[:, at : at + width]
        second = gr[:, 128:] if q < 3 else jnp.zeros((E, 128), f32)
        gr_ref[:, 16 * q : 16 * q + 16, :] = pair_block(gr[:, :128], second)
    for m, wv, first in ((1, w1v, 4), (2, w2v, 10)):
        z = zs[m][...]
        count = 7 - m
        for l0 in range(0, count, 2):
            n = min(2, count - l0)
            a = dot_nt(z, wv[0, 128 * l0 : 128 * (l0 + n), :])
            b = dot_nt(z, wv[1, 128 * l0 : 128 * (l0 + n), :])
            gp = a[:E] + b[E:]
            gn = a[E:] - b[:E]
            for i in range(n):
                q = first + l0 + i
                gr_ref[:, 16 * q : 16 * q + 16, :] = pair_block(
                    gp[:, 128 * i : 128 * i + 128], gn[:, 128 * i : 128 * i + 128]
                )


def kernel_a3(
    v_ref, gr_ref, cs_ref, counts_ref, src_ref, srcv_ref, dir_ref,
    xlo_ref, xhi_ref, mid_ref, side_ref, acc_ref,
):
    cell, slot, _ = edge_ids()
    q = jnp.broadcast_to(column(srcv_ref[...].astype(f32)), (E, 128)).astype(jnp.int32)
    lane = iota((E, 128), 1)
    from_slot = 2 * padded_cell(q, cell) + (q & 1)
    to_slot = 2 * padded_cell(jnp.full((E, 128), 26, jnp.int32), cell) + slot
    sign = jnp.where(lane == from_slot, 1.0, 0.0) - jnp.where(lane == to_slot, 1.0, 0.0)
    for d in range(3):
        side_ref[d] = sign * column(dir_ref[16 * d : 16 * d + 16, :])

    acc_ref[...] = jnp.zeros(acc_ref.shape, f32)
    row_ok = iota((56, 128), 0) < 49
    for cell in range(8):
        p = (((cell >> 2) + 1) * 4 + ((cell >> 1) & 1) + 1) * 4 + (cell & 1) + 1
        for s in range(2):
            occ = jnp.where(s < counts_ref[cell >> 2, (cell >> 1) & 1, cell & 1], 1.0, 0.0).astype(f32)
            acc_ref[pl.ds(p * CR + s, 56, 2), :] = jnp.where(
                row_ok, cs_ref[pl.ds(98 * cell + s, 56, 2), :] * occ, 0.0
            )
    masks = lane_masks()

    def back(cell, carry):
        for i in range(3):
            g = 3 * cell + i
            v = v_ref[g]
            lhs = jnp.concatenate([masked(v, m) for m in masks], axis=0)
            res = dot(lhs, gr_ref[g])
            for e in range(8):
                q = src_ref[2 * cell + (e & 1), 4 * i + (e >> 1)]
                row = padded_cell(q, cell) * CR + (q & 1)
                acc_ref[pl.ds(row, 56, 2), :] += res[64 * e : 64 * e + 56]
        return carry

    lax.fori_loop(0, 8, back, 0)
    xlo_ref[...] = acc_ref[0 : 16 * CR, :].astype(bf16)
    xhi_ref[...] = acc_ref[48 * CR : 64 * CR, :].astype(bf16)
    mid_ref[...] = acc_ref[16 * CR : 48 * CR, :]


def kernel_b1(
    own_ref, ylo_ref, yhi_ref, zlo_ref, zhi_ref, xlo_ref, xhi_ref, base_ref, src_ref,
    u4_ref, g0_ref, g1_ref, g2_ref, gi0_ref, rad_ref, dsilu_ref, wb_ref, ratio_ref, side_ref, rin_ref, rout_ref,
    w0v, w1v, w2v,
    h_ref, force_ref,
    fs_ref, x0_ref, x1_ref, x2_ref, p0_ref,
):
    at = 0
    for piece in (own_ref, ylo_ref, yhi_ref, zlo_ref, zhi_ref, xlo_ref, xhi_ref):
        n = piece.shape[0]
        fs_ref[at : at + n, :] = piece[...].astype(f32)
        at += n
    fs_ref[at : at + 16, :] = jnp.zeros((16, 128), f32)
    xs = (x0_ref, x1_ref, x2_ref)
    gs = (g0_ref, g1_ref, g2_ref)
    masks_r = row_masks()
    zero8 = jnp.zeros((8, 128), f32)

    def rotate(cp, carry):
        parts = []
        for half in range(2):
            cell = 2 * cp + half
            for i in range(3):
                g = 3 * cell + i
                res = []
                for half4 in range(2):
                    rows = []
                    for e in range(4 * half4, 4 * half4 + 4):
                        q = src_ref[2 * cell + (e & 1), 4 * i + (e >> 1)]
                        base = base_ref[padded_cell(q, cell)] + (q & 1)
                        rows += [fs_ref[pl.ds(base, 56, 2), :], zero8]
                    rhs = jnp.concatenate(rows, axis=0).astype(bf16)
                    u = u4_ref[g, half4]
                    lhs = jnp.concatenate([masked(u, m) for m in masks_r], axis=1)
                    res.append(dot(lhs, rhs).reshape(16, 8, 128))
                parts.append(halves(*res))
        for j in range(3):
            both = [jnp.concatenate([parts[2 * j][h], parts[2 * j + 1][h]], axis=1) for h in range(2)]
            row = pl.multiple_of(48 * cp + 16 * j, 16)
            for q, pair in enumerate(PAIRS):
                for h, (m, degree) in enumerate(pair):
                    if degree > LMAX:
                        continue
                    z, up, col = z_place(m, degree)
                    value = both[h][q]
                    if m == 0:
                        p0_ref[pl.ds(row, 16), col : col + 128] = value
                        value = value * rad_ref[pl.ds(row, 16), col : col + 128]
                    xs[z][pl.ds(row + up, 16), col : col + 128] = value.astype(bf16)
        return carry

    lax.fori_loop(0, 4, rotate, 0)
    h_ref[:, 240:256, :] = jnp.zeros((G, 16, 128), bf16)
    along = jnp.zeros((E, 128), f32)

    def rounded(x):
        return x.astype(bf16).astype(f32)

    x0 = x0_ref[...]
    for q in range(4):
        width = 256 if q < 3 else 128
        at = 256 * q
        hid = rounded(dot(x0, w0v[:, at : at + width]))
        prod = hid * g0_ref[:, at : at + width].astype(f32)
        along = along + prod[:, :128]
        if q < 3:
            along = along + prod[:, 128:]
        second = hid[:, 128:] if q < 3 else jnp.zeros((E, 128), f32)
        h_ref[:, 16 * q : 16 * q + 16, :] = pair_block(hid[:, :128], second)
    for m, wv, first in ((1, w1v, 4), (2, w2v, 10)):
        x = xs[m][...]
        count = 7 - m
        for l0 in range(0, count, 2):
            n = min(2, count - l0)
            a = dot(x, wv[0, :, 128 * l0 : 128 * (l0 + n)])
            b = dot(x, wv[1, :, 128 * l0 : 128 * (l0 + n)])
            hp = rounded(a[:E] - b[E:])
            hn = rounded(b[:E] + a[E:])
            gp = gs[m][0:E, 128 * l0 : 128 * (l0 + n)].astype(f32)
            gn = gs[m][E : 2 * E, 128 * l0 : 128 * (l0 + n)].astype(f32)
            prod = hp * gp + hn * gn
            for i in range(n):
                cut = slice(128 * i, 128 * i + 128)
                along = along + prod[:, cut]
                q = first + l0 + i
                h_ref[:, 16 * q : 16 * q + 16, :] = pair_block(hp[:, cut], hn[:, cut])
    grad_act = dot3(gi0_ref[...] * p0_ref[...], rout_ref[...], dot_nt)
    grad_basis = dot3(grad_act * dsilu_ref[...], rin_ref[...], dot_nt)
    parts = grad_basis * wb_ref[...]
    total = along * ratio_ref[...] + parts[:, :128] + parts[:, 128:]
    grad_dist = jnp.sum(total, axis=1, keepdims=True)
    force_ref[...] = jnp.zeros((8, 128), f32)
    for d in range(3):
        force_ref[d : d + 1, :] = jnp.sum(side_ref[d] * grad_dist, axis=0, keepdims=True)


def kernel_b2(own_ref, v_ref, h_ref, envl_ref, counts_ref, upd_ref, fs_ref, us_ref):
    fs_ref[0:784, :] = own_ref[...].astype(f32)
    fs_ref[784:800, :] = jnp.zeros((16, 128), f32)
    slot = iota((64, 256), 1) & 1

    def back(cell, carry):
        sums = jnp.zeros((128, 128), f32)
        for i in range(3):
            g = 3 * cell + i
            v = v_ref[g].astype(f32) * envl_ref[pl.ds(g, 1), :]
            lhs = jnp.concatenate([jnp.where(slot == s, v, 0.0) for s in range(2)], axis=0).astype(bf16)
            sums = sums + dot(lhs, h_ref[g])
        for s in range(2):
            occ = jnp.where(s < counts_ref[cell >> 2, (cell >> 1) & 1, cell & 1], 1.0, 0.0).astype(f32)
            own = fs_ref[pl.ds(98 * cell + s, 56, 2), :]
            us_ref[pl.ds(98 * cell + s, 56, 2), :] = (own + sums[64 * s : 64 * s + 56]) * occ
        return carry

    lax.fori_loop(0, 8, back, 0)
    upd_ref[...] = us_ref[0:784, :].astype(bf16)


def fold_x(mid_ref, lo_ref, hi_ref, zlo_ref, zhi_ref, out_ref):
    for px in range(2):
        arrived = lo_ref if px == 0 else hi_ref
        for py in range(0, 4, 2):
            ends = {0: [], 3: []}
            for pj in range(2):
                for pz in range(4):
                    at = ((py + pj) * 4 + pz) * CR
                    both = mid_ref[px * 16 * CR + at : px * 16 * CR + at + CR, :]
                    if pz % 2 == 0:
                        pair = arrived[at : at + 2 * CR, :].astype(f32)
                    both = both + pair[(pz % 2) * CR : (pz % 2) * CR + CR]
                    if pz in ends:
                        ends[pz].append(both)
                    else:
                        to = ((px * 4 + py + pj) * 2 + pz - 1) * CR
                        out_ref[to : to + CR, :] = both
            to = (px * 4 + py) * CR
            zlo_ref[to : to + 2 * CR, :] = jnp.concatenate(ends[0], axis=0).astype(bf16)
            zhi_ref[to : to + 2 * CR, :] = jnp.concatenate(ends[3], axis=0).astype(bf16)


def force_sum(mine, lo, hi, shift, bit):
    at = (iota((8, 128), 1) >> bit) & 3
    lo = pltpu.roll(lo, 128 - shift, 1)
    hi = pltpu.roll(hi, shift, 1)
    return mine + jnp.where(at == 1, lo, 0.0) + jnp.where(at == 2, hi, 0.0)


def fold_force_x(mine_ref, lo_ref, hi_ref, out_ref):
    out_ref[...] = force_sum(mine_ref[...], lo_ref[...], hi_ref[...], 64, 5)


def fold_z(
    mid_ref, lo_ref, hi_ref, force_ref, flo_ref, fhi_ref, ylo_ref, yhi_ref, out_ref, fout_ref,
):
    force = force_sum(force_ref[...], flo_ref[...], fhi_ref[...], 4, 1)
    fout_ref[...] = force
    rest = force - force.astype(bf16).astype(f32)
    for ref in (ylo_ref, yhi_ref):
        ref[4 * CR : 4 * CR + 16, :] = jnp.concatenate([force, rest], axis=0).astype(bf16)
    for px in range(2):
        arrived = [[], []]
        for z, ref in enumerate((lo_ref, hi_ref)):
            for py in range(0, 4, 2):
                at = (px * 4 + py) * CR
                pair = ref[at : at + 2 * CR, :].astype(f32)
                arrived[z] += [pair[:CR], pair[CR:]]
        for py in range(4):
            done = []
            for z in range(2):
                at = ((px * 4 + py) * 2 + z) * CR
                done.append(mid_ref[at : at + CR, :] + arrived[z][py])
            if py in (0, 3):
                to = px * 2 * CR
                ref = ylo_ref if py == 0 else yhi_ref
                ref[to : to + 2 * CR, :] = jnp.concatenate(done, axis=0).astype(bf16)
            else:
                to = (px * 2 + py - 1) * 2 * CR
                out_ref[to : to + 2 * CR, :] = jnp.concatenate(done, axis=0)


def fold_y(mid_ref, force_ref, lo_ref, hi_ref, out_ref, fout_ref):
    sides = []
    for ref in (lo_ref, hi_ref):
        both = ref[4 * CR : 4 * CR + 16, :].astype(f32)
        sides.append(both[:8] + both[8:])
    total = force_sum(force_ref[...], sides[0], sides[1], 16, 3)
    r = iota((16, 128), 1)
    o = iota((16, 128), 0)
    from_lane = ((o >> 3) + 1) * 32 + (((o >> 2) & 1) + 1) * 8 + (((o >> 1) & 1) + 1) * 2 + (o & 1)
    pick = (r == from_lane).astype(f32)
    fout_ref[...] = lax.dot_general(
        pick, total, (((1,), (1,)), ((), ())), precision=lax.Precision.HIGHEST, preferred_element_type=f32
    )[:, :3]
    for px in range(2):
        for py, ref in enumerate((lo_ref, hi_ref)):
            pair = ref[px * 2 * CR : (px + 1) * 2 * CR, :].astype(f32)
            at = (px * 2 + py) * 2 * CR
            value = mid_ref[at : at + 2 * CR, :] + pair
            for z in range(2):
                to = ((px * 2 + py) * 2 + z) * 98
                out_ref[to : to + 98, :] = value[z * CR : z * CR + 98]


VM = pl.BlockSpec(memory_space=pltpu.VMEM)
SM = pl.BlockSpec(memory_space=pltpu.SMEM)
HB = pl.BlockSpec(memory_space=pltpu.HBM)


def shape(dims, dtype):
    return jax.ShapeDtypeStruct(dims, dtype)


def weights_scratch():
    return [pltpu.VMEM((896, 896), bf16), pltpu.VMEM((2, 768, 768), bf16), pltpu.VMEM((2, 640, 640), bf16)]


def call(kernel, out, specs, scratch, limit, name, cost=None):
    return pl.pallas_call(
        kernel,
        out_shape=out,
        in_specs=specs,
        out_specs=jax.tree.map(lambda _: VM, out),
        scratch_shapes=scratch,
        compiler_params=pltpu.CompilerParams(vmem_limit_bytes=limit),
        name=name,
        cost_estimate=cost,
    )


def cost(us):
    return pl.CostEstimate(flops=int(us * 10**9), bytes_accessed=1 << 20, transcendentals=0)


def run_a1(wt, counts, dist, rin, rout, cot):
    out = [
        shape((G, 256, 128), bf16),
        shape((E, 896), bf16), shape((2 * E, 768), bf16), shape((2 * E, 640), bf16),
        shape((E, 896), f32), shape((E, 128), f32), shape((E, NB), f32), shape((E, 128), f32), shape((G, 256), f32),
        shape((800, 128), f32),
    ]
    scratch = [
        pltpu.VMEM((16, 12), f32), pltpu.VMEM((NB, 128), f32), pltpu.VMEM((128, 896), f32),
        pltpu.VMEM((784, 128), bf16), pltpu.SMEM((2, 2, 2), jnp.int32), pltpu.VMEM((E, 128), f32),
        pltpu.SemaphoreType.DMA((5,)),
    ]
    return call(kernel_a1, out, [VM] + [HB] * 5, scratch, 24 << 20, "rotations", cost(6))(
        wt, *[pltpu.with_memory_space_constraint(x, pltpu.HBM) for x in (counts, dist, rin, rout, cot)]
    )


def run_a2(u, z0, z1, z2, rad, w0, w1, w2):
    out = [
        shape((E, 896), f32), shape((G, 256, 128), bf16), shape((G, 64, 256), bf16), shape((G, 2, 128, 128), bf16),
    ]
    return call(kernel_a2, out, [VM] * 8, [], 20 << 20, "mix_backward", cost(4))(u, z0, z1, z2, rad, w0, w1, w2)


def run_a3(v, gr, cs, counts, src, dirs):
    out = [
        shape((16 * CR, 128), bf16), shape((16 * CR, 128), bf16), shape((32 * CR, 128), f32),
        shape((3, E, 128), f32),
    ]
    scratch = [pltpu.VMEM((64 * CR + 16, 128), f32)]
    return call(kernel_a3, out, [VM, VM, VM, SM, SM, VM, VM], scratch, 20 << 20, "source_gradients", cost(5))(
        v, gr, cs, counts, src, src, dirs
    )


def run_b1(pieces, src, saved, rin, rout, w0, w1, w2):
    out = [shape((G, 256, 128), bf16), shape((8, 128), f32)]
    scratch = [
        pltpu.VMEM((6272 + 16, 128), f32),
        pltpu.VMEM((E, 896), bf16), pltpu.VMEM((2 * E, 768), bf16), pltpu.VMEM((2 * E, 640), bf16),
        pltpu.VMEM((E, 896), f32),
    ]
    specs = [VM] * 7 + [SM, SM] + [VM] * 15
    return call(kernel_b1, out, specs, scratch, 28 << 20, "hidden_and_forces", cost(7))(
        *pieces, jnp.asarray(base_table()), src, *saved, rin, rout, w0, w1, w2
    )


def run_b2(own, v, h, envl, counts):
    scratch = [pltpu.VMEM((800, 128), f32), pltpu.VMEM((800, 128), f32)]
    return call(kernel_b2, shape((784, 128), bf16), [VM] * 4 + [SM], scratch, 16 << 20, "updated", cost(2))(
        own, v, h, envl, counts
    )


def shifts(axis):
    n = lax.axis_size(axis)
    up = [(i, (i + 1) % n) for i in range(n)]
    return up, [(t, s) for s, t in up]


def exchange(to_up, to_down, axis):
    up, down = shifts(axis)
    return lax.ppermute(to_up, axis, up), lax.ppermute(to_down, axis, down)


def tie(*values):
    return lax.optimization_barrier(values)


def test_run(pieces, wt, cot, src, cnt, dist, dirs, w0, w1, w2, rin, rout):
    cnt = cnt.reshape(2, 2, 2)
    u, z0, z1, z2, rad, dsilu, wb, ratio, envl, cs = run_a1(wt, cnt, dist, rin, rout, cot)
    gi0, gr, v, u4 = run_a2(u, z0, z1, z2, rad, w0, w1, w2)
    gxlo, gxhi, mid, side = run_a3(v, gr, cs, cnt, src, dirs)
    h, force = run_b1(pieces, src, (u4, z0, z1, z2, gi0, rad, dsilu, wb, ratio, side), rin, rout, w0, w1, w2)
    return run_b2(pieces[0], v, h, envl, cnt), force, gxlo, gxhi, mid


def local(features, cotangent, counts, sources, wigner, distance, direction, w0, w1, w2, rin, rout):
    cot = jnp.transpose(cotangent, (0, 1, 2, 4, 3, 5)).reshape(784, 128)
    wt = jnp.transpose(wigner, (1, 2, 3, 5, 4, 0)).reshape(E, -1)
    wt = jnp.pad(wt, ((0, 0), (0, 256 - wt.shape[1])))
    src = sources.reshape(16, 12)
    dist = distance.reshape(16, 12)
    dirs = direction.reshape(48, 12)
    feats = jnp.transpose(features, (0, 1, 2, 4, 3, 5))

    ylo, yhi = exchange(feats[:, 1:2], feats[:, 0:1], "gy")
    a1 = run_a1(wt, counts, dist, rin, rout, cot)
    a1, ylo, yhi = tie(a1, ylo, yhi)
    u, z0, z1, z2, rad, dsilu, wb, ratio, envl, cs = a1
    tall = jnp.concatenate([ylo, feats, yhi], axis=1)
    up, down = tall[:, :, 1:2], tall[:, :, 0:1]
    (u, z0, z1, z2, rad), up, down = tie((u, z0, z1, z2, rad), up, down)
    zlo, zhi = exchange(up, down, "gz")
    gi0, gr, v, u4 = run_a2(u, z0, z1, z2, rad, w0, w1, w2)
    gr, zlo, zhi = tie(gr, zlo, zhi)
    top = jnp.concatenate([zlo[1:2], tall[1:2], zhi[1:2]], axis=2)
    low = jnp.concatenate([zlo[0:1], tall[0:1], zhi[0:1]], axis=2)
    gr, top, low = tie(gr, top, low)
    xlo, xhi = exchange(top, low, "gx")
    gxlo, gxhi, mid, side = run_a3(v, gr, cs, counts, src, dirs)

    lo, hi = exchange(gxhi, gxlo, "gx")
    rows = [p.reshape(-1, 128) for p in (feats, ylo, yhi, zlo, zhi, xlo, xhi)]
    h, force = run_b1(rows, src, (u4, z0, z1, z2, gi0, rad, dsilu, wb, ratio, side), rin, rout, w0, w1, w2)
    h, force, lo, hi = tie(h, force, lo, hi)
    flo, fhi = exchange(force, force, "gx")
    gzlo, gzhi, mid = call(
        fold_x,
        [shape((8 * CR, 128), bf16), shape((8 * CR, 128), bf16), shape((16 * CR, 128), f32)],
        [VM] * 3, [], 16 << 20, "fold_x", cost(4),
    )(mid, lo, hi)
    lo, hi = exchange(gzhi, gzlo, "gz")
    force = call(fold_force_x, shape((8, 128), f32), [VM] * 3, [], 8 << 20, "fold_force", cost(0.2))(force, flo, fhi)
    flo, fhi = exchange(force, force, "gz")
    gylo, gyhi, mid, force = call(
        fold_z,
        [
            shape((4 * CR + 16, 128), bf16), shape((4 * CR + 16, 128), bf16), shape((8 * CR, 128), f32),
            shape((8, 128), f32),
        ],
        [VM] * 6, [], 16 << 20, "fold_z", cost(1),
    )(mid, lo, hi, force, flo, fhi)
    force, h = tie(force, h)
    lo, hi = exchange(gyhi, gylo, "gy")
    updated = run_b2(rows[0], v, h, envl, counts)
    updated, lo, hi = tie(updated, lo, hi)
    grads, force = call(
        fold_y, [shape((784, 128), f32), shape((16, 3), f32)], [VM] * 4, [], 16 << 20, "fold_y", cost(1),
    )(mid, force, lo, hi)
    forces = jnp.moveaxis(force.reshape(2, 2, 2, 2, 3), 4, 0)

    def back(x):
        return jnp.transpose(x.reshape(2, 2, 2, 49, 2, 128), (0, 1, 2, 4, 3, 5))

    return back(updated), back(grads), forces


def solution(mesh):
    cells = P("gx", "gy", "gz")
    behind = P(None, "gx", "gy", "gz")
    in_specs = (cells, cells, cells, cells, behind, cells, behind, P(), P(), P(), P(), P())
    return jax.shard_map(local, mesh=mesh, in_specs=in_specs, out_specs=(cells, cells, behind), check_vma=False)
```

```python
import math

import jax
import jax.numpy as jnp
import numpy as np
from jax import lax
from jax.experimental import pallas as pl
from jax.experimental.pallas import tpu as pltpu
from jax.sharding import PartitionSpec as P

LMAX = 6
NB = 256
E = 192
G = 24
CR = 104
cutoff = 6.0
sigma_width = 0.5
bf16 = jnp.bfloat16
f32 = jnp.float32
SCALE = 1.0 / math.sqrt(12.0)

PAIRS = (
    [((0, 2 * q), (0, 2 * q + 1)) for q in range(4)]
    + [((1, l), (-1, l)) for l in range(1, 7)]
    + [((2, l), (-2, l)) for l in range(2, 7)]
)


def row_starts():
    starts = []
    total = 0
    for degree in range(LMAX + 1):
        starts.append(total)
        total += min(2 * degree + 1, 5) * (2 * degree + 1)
    out = []
    for pair in PAIRS:
        for m, degree in pair:
            if degree > LMAX:
                out.append((-1, 0))
            else:
                out.append((starts[degree] + (m + min(degree, 2)) * (2 * degree + 1), degree))
    return out


def expansion(q):
    rows = row_starts()
    lane = iota((1, 256), 1)
    j = lane & 63
    target = jnp.full((1, 256), -1, jnp.int32)
    for h in range(2):
        start, degree = rows[2 * q + h]
        if start >= 0:
            low = degree * degree
            inside = ((lane >> 7) == h) & (j >= low) & (j < low + 2 * degree + 1)
            target = jnp.where(inside, start + j - low, target)
    return jnp.where(iota((256, 256), 0) == target, 1.0, 0.0).astype(bf16)


def base_table():
    out = np.zeros((64,), np.int32)
    for px in range(4):
        for py in range(4):
            for pz in range(4):
                if px in (0, 3):
                    at = 784 + 392 * 2 + 784 * 2 + (px == 3) * 1568 + (py * 4 + pz) * 98
                elif pz in (0, 3):
                    at = 784 + 392 * 2 + (pz == 3) * 784 + ((px - 1) * 4 + py) * 98
                elif py in (0, 3):
                    at = 784 + (py == 3) * 392 + ((px - 1) * 2 + pz - 1) * 98
                else:
                    at = (((px - 1) * 2 + py - 1) * 2 + pz - 1) * 98
                out[(px * 4 + py) * 4 + pz] = at
    return out


def iota(shape, dim):
    return lax.broadcasted_iota(jnp.int32, shape, dim)


def dot(a, b):
    return lax.dot_general(a, b, (((1,), (0,)), ((), ())), preferred_element_type=f32)


def dot_nt(a, b):
    return lax.dot_general(a, b, (((1,), (1,)), ((), ())), preferred_element_type=f32)


def split2(a):
    hi = a.astype(bf16)
    return hi, (a - hi.astype(f32)).astype(bf16)


def dot3(a, b, op=dot):
    ah, al = split2(a)
    bh, bl = split2(b)
    return op(ah, bh) + (op(ah, bl) + op(al, bh))


def edge_ids():
    e = iota((E, 128), 0)
    cell = (e * 2731) >> 16
    rest = e - 24 * cell
    return cell, rest & 1, rest >> 1


def column(block):
    e = iota((E, 16), 0)
    cell = (e * 2731) >> 16
    rest = e - 24 * cell
    pick = (iota((E, 16), 1) == 2 * cell + (rest & 1)).astype(f32)
    rows = lax.dot_general(
        pick, block, (((1,), (0,)), ((), ())), precision=lax.Precision.HIGHEST, preferred_element_type=f32
    )
    e = iota((E, 12), 0)
    rest = e - 24 * ((e * 2731) >> 16)
    return jnp.sum(jnp.where(iota((E, 12), 1) == (rest >> 1), rows, 0.0), axis=1, keepdims=True)


def occupied_edges(counts_ref):
    cell, slot, _ = edge_ids()
    out = jnp.zeros((E, 128), f32)
    for c in range(8):
        out = jnp.where((cell == c) & (slot < counts_ref[c >> 2, (c >> 1) & 1, c & 1]), 1.0, out)
    return out


def basis_of(dist):
    centers = iota((E, NB), 1).astype(f32) * (cutoff / (NB - 1))
    offset = dist - centers
    return jnp.exp(-0.5 * (offset / sigma_width) ** 2), offset


def row_masks():
    r = iota((16, 128), 0) & 3
    h = iota((16, 128), 1) >> 6
    return [jnp.where(r == 2 * t + h, 1.0, 0.0).astype(bf16) for t in range(2)]


def lane_masks():
    lane = iota((16, 256), 1) & 7
    return [jnp.where(lane == e, 1.0, 0.0).astype(bf16) for e in range(8)]


def masked(block, mask):
    n, w = block.shape
    return (block.reshape(n // 16, 16, w) * mask[None]).reshape(n, w)


def padded_cell(q, cell):
    o = q >> 1
    dx = (o * 57) >> 9
    r = o - 9 * dx
    dy = (r * 11) >> 5
    dz = r - 3 * dy
    px = (cell >> 2) + dx
    py = ((cell >> 1) & 1) + dy
    pz = (cell & 1) + dz
    return (px * 4 + py) * 4 + pz


def pair_block(a, b):
    return jnp.concatenate([a.reshape(G, 8, 128), b.reshape(G, 8, 128)], axis=1).astype(bf16)


def z_place(m, degree):
    if m == 0:
        return 0, 0, degree * 128
    return abs(m), (0 if m > 0 else E), (degree - abs(m)) * 128


def start_copies(pairs, sems):
    copies = [pltpu.make_async_copy(src, dst, sems.at[i]) for i, (src, dst) in enumerate(pairs)]
    for c in copies:
        c.start()
    return copies


def kernel_a1(
    wt_ref, counts_hbm, dist_hbm, rin_hbm, rout_hbm, cot_hbm,
    u_ref, z0_ref, z1_ref, z2_ref, rad_ref, dsilu_ref, wb_ref, ratio_ref, envl_ref, cs_ref,
    dist_ref, rin_ref, rout_ref, cot_ref, counts_ref, env_ref, sems,
):
    copies = start_copies(
        ((dist_hbm, dist_ref), (rin_hbm, rin_ref), (rout_hbm, rout_ref), (cot_hbm, cot_ref), (counts_hbm, counts_ref)), sems
    )
    zs = (z0_ref, z1_ref, z2_ref)
    copies[0].wait()
    copies[1].wait()
    dist = column(dist_ref[...])
    basis, offset = basis_of(dist)
    wb_ref[...] = basis * (-offset / (sigma_width * sigma_width))
    inner = dot3(basis, rin_ref[...])
    sig = jax.nn.sigmoid(inner)
    dsilu_ref[...] = sig * (1.0 + inner * (1.0 - sig))
    copies[2].wait()
    copies[4].wait()
    rad_ref[...] = dot3(inner * sig, rout_ref[...])
    angle = jnp.broadcast_to(dist, (E, 128)) * (math.pi / cutoff)
    env = 0.5 * (jnp.cos(angle) + 1.0)
    pick = ((iota((G, E), 1) >> 3) == iota((G, E), 0)).astype(f32)
    spread = jnp.where(
        (iota((E, 256), 0) & 7) == (iota((E, 256), 1) & 7), jnp.concatenate([env, env], axis=1) * SCALE, 0.0
    )
    envl_ref[...] = lax.dot_general(
        pick, spread, (((1,), (0,)), ((), ())), precision=lax.Precision.HIGHEST, preferred_element_type=f32
    )
    ratio_ref[...] = (-0.5 * math.pi / cutoff) * jnp.sin(angle) / env
    env_ref[...] = env * (occupied_edges(counts_ref) * SCALE)
    wt = wt_ref[...]
    for q in range(15):
        res = dot(wt, expansion(q))
        u_ref[:, 16 * q : 16 * q + 16, :] = pair_block(res[:, :128], res[:, 128:])
    u_ref[:, 240:256, :] = jnp.zeros((G, 16, 128), bf16)

    copies[3].wait()
    cs_ref[0:784, :] = cot_ref[...].astype(f32)
    cs_ref[784:800, :] = jnp.zeros((16, 128), f32)
    m_rot = jnp.where((iota((16, 128), 0) & 1) == (iota((16, 128), 1) >> 6), 1.0, 0.0).astype(bf16)
    zero8 = jnp.zeros((8, 128), f32)

    def rotate(cp, carry):
        parts = []
        for half in range(2):
            cell = 2 * cp + half
            rhs = jnp.concatenate(
                [
                    cs_ref[pl.ds(98 * cell, 56, 2), :],
                    zero8,
                    cs_ref[pl.ds(98 * cell + 1, 56, 2), :],
                    zero8,
                ],
                axis=0,
            ).astype(bf16)
            for i in range(3):
                g = 3 * cell + i
                res = dot(masked(u_ref[g, 0:240, :], m_rot), rhs)
                scale = env_ref[pl.ds(pl.multiple_of(8 * g, 8), 8), :]
                parts.append(res.reshape(30, 8, 128) * scale[None])
        for j in range(3):
            both = jnp.concatenate([parts[2 * j], parts[2 * j + 1]], axis=1).astype(bf16)
            row = pl.multiple_of(48 * cp + 16 * j, 16)
            for q, pair in enumerate(PAIRS):
                for h, (m, degree) in enumerate(pair):
                    if degree <= LMAX:
                        z, up, col = z_place(m, degree)
                        zs[z][pl.ds(row + up, 16), col : col + 128] = both[2 * q + h]
        return carry

    lax.fori_loop(0, 4, rotate, 0, unroll=True)


def halves(k0, k1):
    low = (iota((1, 8, 128), 1) < 4)
    return jnp.where(low, k0, pltpu.roll(k1, 4, 1)), jnp.where(low, pltpu.roll(k0, 4, 1), k1)


def kernel_a2(u_ref, z0_ref, z1_ref, z2_ref, rad_ref, w0v, w1v, w2v, gi0_ref, gr_ref, v_ref, u4_ref):
    def turn(g, carry):
        u = u_ref[g]
        v_ref[g] = u.T[:64]
        pairs = u.astype(f32).reshape(16, 2, 8, 128)
        a, b = halves(pairs[:, 0], pairs[:, 1])
        u4_ref[g, 0] = a.reshape(128, 128).astype(bf16)
        u4_ref[g, 1] = b.reshape(128, 128).astype(bf16)
        return carry

    lax.fori_loop(0, G, turn, 0, unroll=4)
    zs = (z0_ref, z1_ref, z2_ref)
    gr_ref[:, 240:256, :] = jnp.zeros((G, 16, 128), bf16)
    z0 = z0_ref[...]
    for q in range(4):
        width = 256 if q < 3 else 128
        at = 256 * q
        gi = dot_nt(z0, w0v[at : at + width, :])
        gi0_ref[:, at : at + width] = gi
        gr = gi * rad_ref[:, at : at + width]
        second = gr[:, 128:] if q < 3 else jnp.zeros((E, 128), f32)
        gr_ref[:, 16 * q : 16 * q + 16, :] = pair_block(gr[:, :128], second)
    for m, wv, first in ((1, w1v, 4), (2, w2v, 10)):
        z = zs[m][...]
        count = 7 - m
        for l0 in range(0, count, 2):
            n = min(2, count - l0)
            a = dot_nt(z, wv[0, 128 * l0 : 128 * (l0 + n), :])
            b = dot_nt(z, wv[1, 128 * l0 : 128 * (l0 + n), :])
            gp = a[:E] + b[E:]
            gn = a[E:] - b[:E]
            for i in range(n):
                q = first + l0 + i
                gr_ref[:, 16 * q : 16 * q + 16, :] = pair_block(
                    gp[:, 128 * i : 128 * i + 128], gn[:, 128 * i : 128 * i + 128]
                )


def kernel_a3(
    v_ref, gr_ref, cs_ref, counts_ref, src_ref, srcv_ref, dir_ref,
    xlo_ref, xhi_ref, mid_ref, side_ref, acc_ref,
):
    cell, slot, _ = edge_ids()
    q = jnp.broadcast_to(column(srcv_ref[...].astype(f32)), (E, 128)).astype(jnp.int32)
    lane = iota((E, 128), 1)
    from_slot = 2 * padded_cell(q, cell) + (q & 1)
    to_slot = 2 * padded_cell(jnp.full((E, 128), 26, jnp.int32), cell) + slot
    sign = jnp.where(lane == from_slot, 1.0, 0.0) - jnp.where(lane == to_slot, 1.0, 0.0)
    for d in range(3):
        side_ref[d] = sign * column(dir_ref[16 * d : 16 * d + 16, :])

    acc_ref[...] = jnp.zeros(acc_ref.shape, f32)
    row_ok = iota((56, 128), 0) < 49
    for cell in range(8):
        p = (((cell >> 2) + 1) * 4 + ((cell >> 1) & 1) + 1) * 4 + (cell & 1) + 1
        for s in range(2):
            occ = jnp.where(s < counts_ref[cell >> 2, (cell >> 1) & 1, cell & 1], 1.0, 0.0).astype(f32)
            acc_ref[pl.ds(p * CR + s, 56, 2), :] = jnp.where(
                row_ok, cs_ref[pl.ds(98 * cell + s, 56, 2), :] * occ, 0.0
            )
    masks = lane_masks()

    def back(cell, carry):
        for i in range(3):
            g = 3 * cell + i
            v = v_ref[g]
            lhs = jnp.concatenate([masked(v, m) for m in masks], axis=0)
            res = dot(lhs, gr_ref[g])
            for e in range(8):
                q = src_ref[2 * cell + (e & 1), 4 * i + (e >> 1)]
                row = padded_cell(q, cell) * CR + (q & 1)
                acc_ref[pl.ds(row, 56, 2), :] += res[64 * e : 64 * e + 56]
        return carry

    lax.fori_loop(0, 8, back, 0, unroll=2)
    xlo_ref[...] = acc_ref[0 : 16 * CR, :].astype(bf16)
    xhi_ref[...] = acc_ref[48 * CR : 64 * CR, :].astype(bf16)
    mid_ref[...] = acc_ref[16 * CR : 48 * CR, :]


def kernel_b1(
    own_ref, ylo_ref, yhi_ref, zlo_ref, zhi_ref, xlo_ref, xhi_ref, base_ref, src_ref,
    u4_ref, g0_ref, g1_ref, g2_ref, gi0_ref, rad_ref, dsilu_ref, wb_ref, ratio_ref, side_ref, rin_ref, rout_ref,
    w0v, w1v, w2v,
    h_ref, force_ref,
    fs_ref, x0_ref, x1_ref, x2_ref, p0_ref,
):
    at = 0
    for piece in (own_ref, ylo_ref, yhi_ref, zlo_ref, zhi_ref, xlo_ref, xhi_ref):
        n = piece.shape[0]
        fs_ref[at : at + n, :] = piece[...].astype(f32)
        at += n
    fs_ref[at : at + 16, :] = jnp.zeros((16, 128), f32)
    xs = (x0_ref, x1_ref, x2_ref)
    gs = (g0_ref, g1_ref, g2_ref)
    masks_r = row_masks()
    zero8 = jnp.zeros((8, 128), f32)

    def rotate(cp, carry):
        parts = []
        for half in range(2):
            cell = 2 * cp + half
            for i in range(3):
                g = 3 * cell + i
                res = []
                for half4 in range(2):
                    rows = []
                    for e in range(4 * half4, 4 * half4 + 4):
                        q = src_ref[2 * cell + (e & 1), 4 * i + (e >> 1)]
                        base = base_ref[padded_cell(q, cell)] + (q & 1)
                        rows += [fs_ref[pl.ds(base, 56, 2), :], zero8]
                    rhs = jnp.concatenate(rows, axis=0).astype(bf16)
                    u = u4_ref[g, half4]
                    lhs = jnp.concatenate([masked(u, m) for m in masks_r], axis=1)
                    res.append(dot(lhs, rhs).reshape(16, 8, 128))
                parts.append(halves(*res))
        for j in range(3):
            both = [jnp.concatenate([parts[2 * j][h], parts[2 * j + 1][h]], axis=1) for h in range(2)]
            row = pl.multiple_of(48 * cp + 16 * j, 16)
            for q, pair in enumerate(PAIRS):
                for h, (m, degree) in enumerate(pair):
                    if degree > LMAX:
                        continue
                    z, up, col = z_place(m, degree)
                    value = both[h][q]
                    if m == 0:
                        p0_ref[pl.ds(row, 16), col : col + 128] = value
                        value = value * rad_ref[pl.ds(row, 16), col : col + 128]
                    xs[z][pl.ds(row + up, 16), col : col + 128] = value.astype(bf16)
        return carry

    lax.fori_loop(0, 4, rotate, 0, unroll=True)
    h_ref[:, 240:256, :] = jnp.zeros((G, 16, 128), bf16)
    along = jnp.zeros((E, 128), f32)

    def rounded(x):
        return x.astype(bf16).astype(f32)

    x0 = x0_ref[...]
    for q in range(4):
        width = 256 if q < 3 else 128
        at = 256 * q
        hid = rounded(dot(x0, w0v[:, at : at + width]))
        prod = hid * g0_ref[:, at : at + width].astype(f32)
        along = along + prod[:, :128]
        if q < 3:
            along = along + prod[:, 128:]
        second = hid[:, 128:] if q < 3 else jnp.zeros((E, 128), f32)
        h_ref[:, 16 * q : 16 * q + 16, :] = pair_block(hid[:, :128], second)
    for m, wv, first in ((1, w1v, 4), (2, w2v, 10)):
        x = xs[m][...]
        count = 7 - m
        for l0 in range(0, count, 2):
            n = min(2, count - l0)
            a = dot(x, wv[0, :, 128 * l0 : 128 * (l0 + n)])
            b = dot(x, wv[1, :, 128 * l0 : 128 * (l0 + n)])
            hp = rounded(a[:E] - b[E:])
            hn = rounded(b[:E] + a[E:])
            gp = gs[m][0:E, 128 * l0 : 128 * (l0 + n)].astype(f32)
            gn = gs[m][E : 2 * E, 128 * l0 : 128 * (l0 + n)].astype(f32)
            prod = hp * gp + hn * gn
            for i in range(n):
                cut = slice(128 * i, 128 * i + 128)
                along = along + prod[:, cut]
                q = first + l0 + i
                h_ref[:, 16 * q : 16 * q + 16, :] = pair_block(hp[:, cut], hn[:, cut])
    grad_act = dot3(gi0_ref[...] * p0_ref[...], rout_ref[...], dot_nt)
    grad_basis = dot3(grad_act * dsilu_ref[...], rin_ref[...], dot_nt)
    parts = grad_basis * wb_ref[...]
    total = along * ratio_ref[...] + parts[:, :128] + parts[:, 128:]
    grad_dist = jnp.sum(total, axis=1, keepdims=True)
    force_ref[...] = jnp.zeros((8, 128), f32)
    for d in range(3):
        force_ref[d : d + 1, :] = jnp.sum(side_ref[d] * grad_dist, axis=0, keepdims=True)


def kernel_b2(own_ref, v_ref, h_ref, envl_ref, counts_ref, upd_ref, fs_ref, us_ref):
    fs_ref[0:784, :] = own_ref[...].astype(f32)
    fs_ref[784:800, :] = jnp.zeros((16, 128), f32)
    slot = iota((64, 256), 1) & 1

    def back(cell, carry):
        sums = jnp.zeros((128, 128), f32)
        for i in range(3):
            g = 3 * cell + i
            v = v_ref[g].astype(f32) * envl_ref[pl.ds(g, 1), :]
            lhs = jnp.concatenate([jnp.where(slot == s, v, 0.0) for s in range(2)], axis=0).astype(bf16)
            sums = sums + dot(lhs, h_ref[g])
        for s in range(2):
            occ = jnp.where(s < counts_ref[cell >> 2, (cell >> 1) & 1, cell & 1], 1.0, 0.0).astype(f32)
            own = fs_ref[pl.ds(98 * cell + s, 56, 2), :]
            us_ref[pl.ds(98 * cell + s, 56, 2), :] = (own + sums[64 * s : 64 * s + 56]) * occ
        return carry

    lax.fori_loop(0, 8, back, 0, unroll=4)
    upd_ref[...] = us_ref[0:784, :].astype(bf16)


def fold_x(mid_ref, lo_ref, hi_ref, zlo_ref, zhi_ref, out_ref):
    for px in range(2):
        arrived = lo_ref if px == 0 else hi_ref
        for py in range(0, 4, 2):
            ends = {0: [], 3: []}
            for pj in range(2):
                for pz in range(4):
                    at = ((py + pj) * 4 + pz) * CR
                    both = mid_ref[px * 16 * CR + at : px * 16 * CR + at + CR, :]
                    if pz % 2 == 0:
                        pair = arrived[at : at + 2 * CR, :].astype(f32)
                    both = both + pair[(pz % 2) * CR : (pz % 2) * CR + CR]
                    if pz in ends:
                        ends[pz].append(both)
                    else:
                        to = ((px * 4 + py + pj) * 2 + pz - 1) * CR
                        out_ref[to : to + CR, :] = both
            to = (px * 4 + py) * CR
            zlo_ref[to : to + 2 * CR, :] = jnp.concatenate(ends[0], axis=0).astype(bf16)
            zhi_ref[to : to + 2 * CR, :] = jnp.concatenate(ends[3], axis=0).astype(bf16)


def force_sum(mine, lo, hi, shift, bit):
    at = (iota((8, 128), 1) >> bit) & 3
    lo = pltpu.roll(lo, 128 - shift, 1)
    hi = pltpu.roll(hi, shift, 1)
    return mine + jnp.where(at == 1, lo, 0.0) + jnp.where(at == 2, hi, 0.0)


def fold_force_x(mine_ref, lo_ref, hi_ref, out_ref):
    out_ref[...] = force_sum(mine_ref[...], lo_ref[...], hi_ref[...], 64, 5)


def fold_z(
    mid_ref, lo_ref, hi_ref, force_ref, flo_ref, fhi_ref, ylo_ref, yhi_ref, out_ref, fout_ref,
):
    force = force_sum(force_ref[...], flo_ref[...], fhi_ref[...], 4, 1)
    fout_ref[...] = force
    rest = force - force.astype(bf16).astype(f32)
    for ref in (ylo_ref, yhi_ref):
        ref[4 * CR : 4 * CR + 16, :] = jnp.concatenate([force, rest], axis=0).astype(bf16)
    for px in range(2):
        arrived = [[], []]
        for z, ref in enumerate((lo_ref, hi_ref)):
            for py in range(0, 4, 2):
                at = (px * 4 + py) * CR
                pair = ref[at : at + 2 * CR, :].astype(f32)
                arrived[z] += [pair[:CR], pair[CR:]]
        for py in range(4):
            done = []
            for z in range(2):
                at = ((px * 4 + py) * 2 + z) * CR
                done.append(mid_ref[at : at + CR, :] + arrived[z][py])
            if py in (0, 3):
                to = px * 2 * CR
                ref = ylo_ref if py == 0 else yhi_ref
                ref[to : to + 2 * CR, :] = jnp.concatenate(done, axis=0).astype(bf16)
            else:
                to = (px * 2 + py - 1) * 2 * CR
                out_ref[to : to + 2 * CR, :] = jnp.concatenate(done, axis=0)


def fold_y(mid_ref, force_ref, lo_ref, hi_ref, out_ref, fout_ref):
    sides = []
    for ref in (lo_ref, hi_ref):
        both = ref[4 * CR : 4 * CR + 16, :].astype(f32)
        sides.append(both[:8] + both[8:])
    total = force_sum(force_ref[...], sides[0], sides[1], 16, 3)
    r = iota((16, 128), 1)
    o = iota((16, 128), 0)
    from_lane = ((o >> 3) + 1) * 32 + (((o >> 2) & 1) + 1) * 8 + (((o >> 1) & 1) + 1) * 2 + (o & 1)
    pick = (r == from_lane).astype(f32)
    fout_ref[...] = lax.dot_general(
        pick, total, (((1,), (1,)), ((), ())), precision=lax.Precision.HIGHEST, preferred_element_type=f32
    )[:, :3]
    for px in range(2):
        for py, ref in enumerate((lo_ref, hi_ref)):
            pair = ref[px * 2 * CR : (px + 1) * 2 * CR, :].astype(f32)
            at = (px * 2 + py) * 2 * CR
            value = mid_ref[at : at + 2 * CR, :] + pair
            for z in range(2):
                to = ((px * 2 + py) * 2 + z) * 98
                out_ref[to : to + 98, :] = value[z * CR : z * CR + 98]


VM = pl.BlockSpec(memory_space=pltpu.VMEM)
SM = pl.BlockSpec(memory_space=pltpu.SMEM)
HB = pl.BlockSpec(memory_space=pltpu.HBM)


def shape(dims, dtype):
    return jax.ShapeDtypeStruct(dims, dtype)


def weights_scratch():
    return [pltpu.VMEM((896, 896), bf16), pltpu.VMEM((2, 768, 768), bf16), pltpu.VMEM((2, 640, 640), bf16)]


def call(kernel, out, specs, scratch, limit, name, cost=None):
    return pl.pallas_call(
        kernel,
        out_shape=out,
        in_specs=specs,
        out_specs=jax.tree.map(lambda _: VM, out),
        scratch_shapes=scratch,
        compiler_params=pltpu.CompilerParams(vmem_limit_bytes=limit),
        name=name,
        cost_estimate=cost,
    )


def cost(us):
    return pl.CostEstimate(flops=int(us * 10**9), bytes_accessed=1 << 20, transcendentals=0)


def run_a1(wt, counts, dist, rin, rout, cot):
    out = [
        shape((G, 256, 128), bf16),
        shape((E, 896), bf16), shape((2 * E, 768), bf16), shape((2 * E, 640), bf16),
        shape((E, 896), f32), shape((E, 128), f32), shape((E, NB), f32), shape((E, 128), f32), shape((G, 256), f32),
        shape((800, 128), f32),
    ]
    scratch = [
        pltpu.VMEM((16, 12), f32), pltpu.VMEM((NB, 128), f32), pltpu.VMEM((128, 896), f32),
        pltpu.VMEM((784, 128), bf16), pltpu.SMEM((2, 2, 2), jnp.int32), pltpu.VMEM((E, 128), f32),
        pltpu.SemaphoreType.DMA((5,)),
    ]
    return call(kernel_a1, out, [VM] + [HB] * 5, scratch, 24 << 20, "rotations", cost(6))(
        wt, *[pltpu.with_memory_space_constraint(x, pltpu.HBM) for x in (counts, dist, rin, rout, cot)]
    )


def run_a2(u, z0, z1, z2, rad, w0, w1, w2):
    out = [
        shape((E, 896), f32), shape((G, 256, 128), bf16), shape((G, 64, 256), bf16), shape((G, 2, 128, 128), bf16),
    ]
    return call(kernel_a2, out, [VM] * 8, [], 20 << 20, "mix_backward", cost(4))(u, z0, z1, z2, rad, w0, w1, w2)


def run_a3(v, gr, cs, counts, src, dirs):
    out = [
        shape((16 * CR, 128), bf16), shape((16 * CR, 128), bf16), shape((32 * CR, 128), f32),
        shape((3, E, 128), f32),
    ]
    scratch = [pltpu.VMEM((64 * CR + 16, 128), f32)]
    return call(kernel_a3, out, [VM, VM, VM, SM, SM, VM, VM], scratch, 20 << 20, "source_gradients", cost(5))(
        v, gr, cs, counts, src, src, dirs
    )


def run_b1(pieces, src, saved, rin, rout, w0, w1, w2):
    out = [shape((G, 256, 128), bf16), shape((8, 128), f32)]
    scratch = [
        pltpu.VMEM((6272 + 16, 128), f32),
        pltpu.VMEM((E, 896), bf16), pltpu.VMEM((2 * E, 768), bf16), pltpu.VMEM((2 * E, 640), bf16),
        pltpu.VMEM((E, 896), f32),
    ]
    specs = [VM] * 7 + [SM, SM] + [VM] * 15
    return call(kernel_b1, out, specs, scratch, 28 << 20, "hidden_and_forces", cost(7))(
        *pieces, jnp.asarray(base_table()), src, *saved, rin, rout, w0, w1, w2
    )


def run_b2(own, v, h, envl, counts):
    scratch = [pltpu.VMEM((800, 128), f32), pltpu.VMEM((800, 128), f32)]
    return call(kernel_b2, shape((784, 128), bf16), [VM] * 4 + [SM], scratch, 16 << 20, "updated", cost(2))(
        own, v, h, envl, counts
    )


def shifts(axis):
    n = lax.axis_size(axis)
    up = [(i, (i + 1) % n) for i in range(n)]
    return up, [(t, s) for s, t in up]


def exchange(to_up, to_down, axis):
    up, down = shifts(axis)
    return lax.ppermute(to_up, axis, up), lax.ppermute(to_down, axis, down)


def tie(*values):
    return lax.optimization_barrier(values)


def test_run(pieces, wt, cot, src, cnt, dist, dirs, w0, w1, w2, rin, rout):
    cnt = cnt.reshape(2, 2, 2)
    u, z0, z1, z2, rad, dsilu, wb, ratio, envl, cs = run_a1(wt, cnt, dist, rin, rout, cot)
    gi0, gr, v, u4 = run_a2(u, z0, z1, z2, rad, w0, w1, w2)
    gxlo, gxhi, mid, side = run_a3(v, gr, cs, cnt, src, dirs)
    h, force = run_b1(pieces, src, (u4, z0, z1, z2, gi0, rad, dsilu, wb, ratio, side), rin, rout, w0, w1, w2)
    return run_b2(pieces[0], v, h, envl, cnt), force, gxlo, gxhi, mid


def local(features, cotangent, counts, sources, wigner, distance, direction, w0, w1, w2, rin, rout):
    cot = jnp.transpose(cotangent, (0, 1, 2, 4, 3, 5)).reshape(784, 128)
    wt = jnp.transpose(wigner, (1, 2, 3, 5, 4, 0)).reshape(E, -1)
    wt = jnp.pad(wt, ((0, 0), (0, 256 - wt.shape[1])))
    src = sources.reshape(16, 12)
    dist = distance.reshape(16, 12)
    dirs = direction.reshape(48, 12)
    feats = jnp.transpose(features, (0, 1, 2, 4, 3, 5))

    ylo, yhi = exchange(feats[:, 1:2], feats[:, 0:1], "gy")
    a1 = run_a1(wt, counts, dist, rin, rout, cot)
    a1, ylo, yhi = tie(a1, ylo, yhi)
    u, z0, z1, z2, rad, dsilu, wb, ratio, envl, cs = a1
    tall = jnp.concatenate([ylo, feats, yhi], axis=1)
    up, down = tall[:, :, 1:2], tall[:, :, 0:1]
    (u, z0, z1, z2, rad), up, down = tie((u, z0, z1, z2, rad), up, down)
    zlo, zhi = exchange(up, down, "gz")
    gi0, gr, v, u4 = run_a2(u, z0, z1, z2, rad, w0, w1, w2)
    gr, zlo, zhi = tie(gr, zlo, zhi)
    top = jnp.concatenate([zlo[1:2], tall[1:2], zhi[1:2]], axis=2)
    low = jnp.concatenate([zlo[0:1], tall[0:1], zhi[0:1]], axis=2)
    gr, top, low = tie(gr, top, low)
    xlo, xhi = exchange(top, low, "gx")
    gxlo, gxhi, mid, side = run_a3(v, gr, cs, counts, src, dirs)

    lo, hi = exchange(gxhi, gxlo, "gx")
    rows = [p.reshape(-1, 128) for p in (feats, ylo, yhi, zlo, zhi, xlo, xhi)]
    h, force = run_b1(rows, src, (u4, z0, z1, z2, gi0, rad, dsilu, wb, ratio, side), rin, rout, w0, w1, w2)
    h, lo, hi = tie(h, lo, hi)
    flo, fhi = exchange(force, force, "gx")
    gzlo, gzhi, mid = call(
        fold_x,
        [shape((8 * CR, 128), bf16), shape((8 * CR, 128), bf16), shape((16 * CR, 128), f32)],
        [VM] * 3, [], 16 << 20, "fold_x", cost(0.1),
    )(mid, lo, hi)
    lo, hi = exchange(gzhi, gzlo, "gz")
    force = call(fold_force_x, shape((8, 128), f32), [VM] * 3, [], 8 << 20, "fold_force", cost(4))(force, flo, fhi)
    flo, fhi = exchange(force, force, "gz")
    gylo, gyhi, mid, force = call(
        fold_z,
        [
            shape((4 * CR + 16, 128), bf16), shape((4 * CR + 16, 128), bf16), shape((8 * CR, 128), f32),
            shape((8, 128), f32),
        ],
        [VM] * 6, [], 16 << 20, "fold_z", cost(1),
    )(mid, lo, hi, force, flo, fhi)
    force, h = tie(force, h)
    lo, hi = exchange(gyhi, gylo, "gy")
    updated = run_b2(rows[0], v, h, envl, counts)
    updated, lo, hi = tie(updated, lo, hi)
    grads, force = call(
        fold_y, [shape((784, 128), f32), shape((16, 3), f32)], [VM] * 4, [], 16 << 20, "fold_y", cost(1),
    )(mid, force, lo, hi)
    forces = jnp.moveaxis(force.reshape(2, 2, 2, 2, 3), 4, 0)

    def back(x):
        return jnp.transpose(x.reshape(2, 2, 2, 49, 2, 128), (0, 1, 2, 4, 3, 5))

    return back(updated), back(grads), forces


def solution(mesh):
    cells = P("gx", "gy", "gz")
    behind = P(None, "gx", "gy", "gz")
    in_specs = (cells, cells, cells, cells, behind, cells, behind, P(), P(), P(), P(), P())
    return jax.shard_map(local, mesh=mesh, in_specs=in_specs, out_specs=(cells, cells, behind), check_vma=False)
```

```python
import math

import jax
import jax.numpy as jnp
import numpy as np
from jax import lax
from jax.experimental import pallas as pl
from jax.experimental.pallas import tpu as pltpu
from jax.sharding import PartitionSpec as P

LMAX = 6
NB = 256
E = 192
G = 24
CR = 104
cutoff = 6.0
sigma_width = 0.5
bf16 = jnp.bfloat16
f32 = jnp.float32
SCALE = 1.0 / math.sqrt(12.0)

PAIRS = (
    [((0, 2 * q), (0, 2 * q + 1)) for q in range(4)]
    + [((1, l), (-1, l)) for l in range(1, 7)]
    + [((2, l), (-2, l)) for l in range(2, 7)]
)


def row_starts():
    starts = []
    total = 0
    for degree in range(LMAX + 1):
        starts.append(total)
        total += min(2 * degree + 1, 5) * (2 * degree + 1)
    out = []
    for pair in PAIRS:
        for m, degree in pair:
            if degree > LMAX:
                out.append((-1, 0))
            else:
                out.append((starts[degree] + (m + min(degree, 2)) * (2 * degree + 1), degree))
    return out


def expansion(q):
    rows = row_starts()
    lane = iota((1, 256), 1)
    j = lane & 63
    target = jnp.full((1, 256), -1, jnp.int32)
    for h in range(2):
        start, degree = rows[2 * q + h]
        if start >= 0:
            low = degree * degree
            inside = ((lane >> 7) == h) & (j >= low) & (j < low + 2 * degree + 1)
            target = jnp.where(inside, start + j - low, target)
    return jnp.where(iota((256, 256), 0) == target, 1.0, 0.0).astype(bf16)


def base_table():
    out = np.zeros((64,), np.int32)
    for px in range(4):
        for py in range(4):
            for pz in range(4):
                if px in (0, 3):
                    at = 784 + 392 * 2 + 784 * 2 + (px == 3) * 784
                    if pz in (0, 3):
                        at += 784 * 2 + (pz == 3) * 392 + py * 98
                    else:
                        at += (py * 2 + pz - 1) * 98
                elif pz in (0, 3):
                    at = 784 + 392 * 2 + (pz == 3) * 784 + ((px - 1) * 4 + py) * 98
                elif py in (0, 3):
                    at = 784 + (py == 3) * 392 + ((px - 1) * 2 + pz - 1) * 98
                else:
                    at = (((px - 1) * 2 + py - 1) * 2 + pz - 1) * 98
                out[(px * 4 + py) * 4 + pz] = at
    return out


def iota(shape, dim):
    return lax.broadcasted_iota(jnp.int32, shape, dim)


def dot(a, b):
    return lax.dot_general(a, b, (((1,), (0,)), ((), ())), preferred_element_type=f32)


def dot_nt(a, b):
    return lax.dot_general(a, b, (((1,), (1,)), ((), ())), preferred_element_type=f32)


def split2(a):
    hi = a.astype(bf16)
    return hi, (a - hi.astype(f32)).astype(bf16)


def dot3(a, b, op=dot):
    ah, al = split2(a)
    bh, bl = split2(b)
    return op(ah, bh) + (op(ah, bl) + op(al, bh))


def edge_ids():
    e = iota((E, 128), 0)
    cell = (e * 2731) >> 16
    rest = e - 24 * cell
    return cell, rest & 1, rest >> 1


def column(block):
    e = iota((E, 16), 0)
    cell = (e * 2731) >> 16
    rest = e - 24 * cell
    pick = (iota((E, 16), 1) == 2 * cell + (rest & 1)).astype(f32)
    rows = lax.dot_general(
        pick, block, (((1,), (0,)), ((), ())), precision=lax.Precision.HIGHEST, preferred_element_type=f32
    )
    e = iota((E, 12), 0)
    rest = e - 24 * ((e * 2731) >> 16)
    return jnp.sum(jnp.where(iota((E, 12), 1) == (rest >> 1), rows, 0.0), axis=1, keepdims=True)


def occupied_edges(counts_ref):
    cell, slot, _ = edge_ids()
    out = jnp.zeros((E, 128), f32)
    for c in range(8):
        out = jnp.where((cell == c) & (slot < counts_ref[c >> 2, (c >> 1) & 1, c & 1]), 1.0, out)
    return out


def basis_of(dist):
    centers = iota((E, NB), 1).astype(f32) * (cutoff / (NB - 1))
    offset = dist - centers
    return jnp.exp(-0.5 * (offset / sigma_width) ** 2), offset


def row_masks():
    r = iota((16, 128), 0) & 3
    h = iota((16, 128), 1) >> 6
    return [jnp.where(r == 2 * t + h, 1.0, 0.0).astype(bf16) for t in range(2)]


def lane_masks():
    lane = iota((16, 256), 1) & 7
    return [jnp.where(lane == e, 1.0, 0.0).astype(bf16) for e in range(8)]


def masked(block, mask):
    n, w = block.shape
    return (block.reshape(n // 16, 16, w) * mask[None]).reshape(n, w)


def padded_cell(q, cell):
    o = q >> 1
    dx = (o * 57) >> 9
    r = o - 9 * dx
    dy = (r * 11) >> 5
    dz = r - 3 * dy
    px = (cell >> 2) + dx
    py = ((cell >> 1) & 1) + dy
    pz = (cell & 1) + dz
    return (px * 4 + py) * 4 + pz


def pair_block(a, b):
    return jnp.concatenate([a.reshape(G, 8, 128), b.reshape(G, 8, 128)], axis=1).astype(bf16)


def z_place(m, degree):
    if m == 0:
        return 0, 0, degree * 128
    return abs(m), (0 if m > 0 else E), (degree - abs(m)) * 128


def start_copies(pairs, sems):
    copies = [pltpu.make_async_copy(src, dst, sems.at[i]) for i, (src, dst) in enumerate(pairs)]
    for c in copies:
        c.start()
    return copies


def kernel_a1(
    wt_ref, counts_hbm, dist_hbm, rin_hbm, rout_hbm, cot_hbm,
    u_ref, z0_ref, z1_ref, z2_ref, rad_ref, dsilu_ref, wb_ref, ratio_ref, envl_ref, cs_ref,
    dist_ref, rin_ref, rout_ref, cot_ref, counts_ref, env_ref, sems,
):
    copies = start_copies(
        ((dist_hbm, dist_ref), (rin_hbm, rin_ref), (rout_hbm, rout_ref), (cot_hbm, cot_ref), (counts_hbm, counts_ref)), sems
    )
    zs = (z0_ref, z1_ref, z2_ref)
    copies[0].wait()
    copies[1].wait()
    dist = column(dist_ref[...])
    basis, offset = basis_of(dist)
    wb_ref[...] = basis * (-offset / (sigma_width * sigma_width))
    inner = dot3(basis, rin_ref[...])
    sig = jax.nn.sigmoid(inner)
    dsilu_ref[...] = sig * (1.0 + inner * (1.0 - sig))
    copies[2].wait()
    copies[4].wait()
    rad_ref[...] = dot3(inner * sig, rout_ref[...])
    angle = jnp.broadcast_to(dist, (E, 128)) * (math.pi / cutoff)
    env = 0.5 * (jnp.cos(angle) + 1.0)
    pick = ((iota((G, E), 1) >> 3) == iota((G, E), 0)).astype(f32)
    spread = jnp.where(
        (iota((E, 256), 0) & 7) == (iota((E, 256), 1) & 7), jnp.concatenate([env, env], axis=1) * SCALE, 0.0
    )
    envl_ref[...] = lax.dot_general(
        pick, spread, (((1,), (0,)), ((), ())), precision=lax.Precision.HIGHEST, preferred_element_type=f32
    )
    ratio_ref[...] = (-0.5 * math.pi / cutoff) * jnp.sin(angle) / env
    env_ref[...] = env * (occupied_edges(counts_ref) * SCALE)
    wt = wt_ref[...]
    for q in range(15):
        res = dot(wt, expansion(q))
        u_ref[:, 16 * q : 16 * q + 16, :] = pair_block(res[:, :128], res[:, 128:])
    u_ref[:, 240:256, :] = jnp.zeros((G, 16, 128), bf16)

    copies[3].wait()
    cs_ref[0:784, :] = cot_ref[...].astype(f32)
    cs_ref[784:800, :] = jnp.zeros((16, 128), f32)
    m_rot = jnp.where((iota((16, 128), 0) & 1) == (iota((16, 128), 1) >> 6), 1.0, 0.0).astype(bf16)
    zero8 = jnp.zeros((8, 128), f32)

    def rotate(cp, carry):
        parts = []
        for half in range(2):
            cell = 2 * cp + half
            rhs = jnp.concatenate(
                [
                    cs_ref[pl.ds(98 * cell, 56, 2), :],
                    zero8,
                    cs_ref[pl.ds(98 * cell + 1, 56, 2), :],
                    zero8,
                ],
                axis=0,
            ).astype(bf16)
            for i in range(3):
                g = 3 * cell + i
                res = dot(masked(u_ref[g, 0:240, :], m_rot), rhs)
                scale = env_ref[pl.ds(pl.multiple_of(8 * g, 8), 8), :]
                parts.append(res.reshape(30, 8, 128) * scale[None])
        for j in range(3):
            both = jnp.concatenate([parts[2 * j], parts[2 * j + 1]], axis=1).astype(bf16)
            row = pl.multiple_of(48 * cp + 16 * j, 16)
            for q, pair in enumerate(PAIRS):
                for h, (m, degree) in enumerate(pair):
                    if degree <= LMAX:
                        z, up, col = z_place(m, degree)
                        zs[z][pl.ds(row + up, 16), col : col + 128] = both[2 * q + h]
        return carry

    lax.fori_loop(0, 4, rotate, 0, unroll=True)


def halves(k0, k1):
    low = (iota((1, 8, 128), 1) < 4)
    return jnp.where(low, k0, pltpu.roll(k1, 4, 1)), jnp.where(low, pltpu.roll(k0, 4, 1), k1)


def kernel_a2(u_ref, z0_ref, z1_ref, z2_ref, rad_ref, w0v, w1v, w2v, gi0_ref, gr_ref, v_ref, u4_ref):
    def turn(g, carry):
        u = u_ref[g]
        v_ref[g] = u.T[:64]
        pairs = u.astype(f32).reshape(16, 2, 8, 128)
        a, b = halves(pairs[:, 0], pairs[:, 1])
        u4_ref[g, 0] = a.reshape(128, 128).astype(bf16)
        u4_ref[g, 1] = b.reshape(128, 128).astype(bf16)
        return carry

    lax.fori_loop(0, G, turn, 0, unroll=4)
    zs = (z0_ref, z1_ref, z2_ref)
    gr_ref[:, 240:256, :] = jnp.zeros((G, 16, 128), bf16)
    z0 = z0_ref[...]
    for q in range(4):
        width = 256 if q < 3 else 128
        at = 256 * q
        gi = dot_nt(z0, w0v[at : at + width, :])
        gi0_ref[:, at : at + width] = gi
        gr = gi * rad_ref[:, at : at + width]
        second = gr[:, 128:] if q < 3 else jnp.zeros((E, 128), f32)
        gr_ref[:, 16 * q : 16 * q + 16, :] = pair_block(gr[:, :128], second)
    for m, wv, first in ((1, w1v, 4), (2, w2v, 10)):
        z = zs[m][...]
        count = 7 - m
        for l0 in range(0, count, 2):
            n = min(2, count - l0)
            a = dot_nt(z, wv[0, 128 * l0 : 128 * (l0 + n), :])
            b = dot_nt(z, wv[1, 128 * l0 : 128 * (l0 + n), :])
            gp = a[:E] + b[E:]
            gn = a[E:] - b[:E]
            for i in range(n):
                q = first + l0 + i
                gr_ref[:, 16 * q : 16 * q + 16, :] = pair_block(
                    gp[:, 128 * i : 128 * i + 128], gn[:, 128 * i : 128 * i + 128]
                )


def kernel_a3(
    v_ref, gr_ref, cs_ref, counts_ref, src_ref, srcv_ref, dir_ref,
    xlo_ref, xhi_ref, mid_ref, side_ref, acc_ref,
):
    cell, slot, _ = edge_ids()
    q = jnp.broadcast_to(column(srcv_ref[...].astype(f32)), (E, 128)).astype(jnp.int32)
    lane = iota((E, 128), 1)
    from_slot = 2 * padded_cell(q, cell) + (q & 1)
    to_slot = 2 * padded_cell(jnp.full((E, 128), 26, jnp.int32), cell) + slot
    sign = jnp.where(lane == from_slot, 1.0, 0.0) - jnp.where(lane == to_slot, 1.0, 0.0)
    for d in range(3):
        side_ref[d] = sign * column(dir_ref[16 * d : 16 * d + 16, :])

    acc_ref[...] = jnp.zeros(acc_ref.shape, f32)
    row_ok = iota((56, 128), 0) < 49
    for cell in range(8):
        p = (((cell >> 2) + 1) * 4 + ((cell >> 1) & 1) + 1) * 4 + (cell & 1) + 1
        for s in range(2):
            occ = jnp.where(s < counts_ref[cell >> 2, (cell >> 1) & 1, cell & 1], 1.0, 0.0).astype(f32)
            acc_ref[pl.ds(p * CR + s, 56, 2), :] = jnp.where(
                row_ok, cs_ref[pl.ds(98 * cell + s, 56, 2), :] * occ, 0.0
            )
    masks = lane_masks()

    def back(cell, carry):
        for i in range(3):
            g = 3 * cell + i
            v = v_ref[g]
            lhs = jnp.concatenate([masked(v, m) for m in masks], axis=0)
            res = dot(lhs, gr_ref[g])
            for e in range(8):
                q = src_ref[2 * cell + (e & 1), 4 * i + (e >> 1)]
                row = padded_cell(q, cell) * CR + (q & 1)
                acc_ref[pl.ds(row, 56, 2), :] += res[64 * e : 64 * e + 56]
        return carry

    lax.fori_loop(0, 8, back, 0, unroll=2)
    xlo_ref[...] = acc_ref[0 : 16 * CR, :].astype(bf16)
    xhi_ref[...] = acc_ref[48 * CR : 64 * CR, :].astype(bf16)
    mid_ref[...] = acc_ref[16 * CR : 48 * CR, :]


def kernel_b1(
    own_ref, ylo_ref, yhi_ref, zlo_ref, zhi_ref, xlo_ref, xhi_ref, xzlo_ref, xzhi_ref, base_ref, src_ref,
    u4_ref, g0_ref, g1_ref, g2_ref, gi0_ref, rad_ref, dsilu_ref, wb_ref, ratio_ref, side_ref, rin_ref, rout_ref,
    w0v, w1v, w2v,
    h_ref, force_ref,
    fs_ref, x0_ref, x1_ref, x2_ref, p0_ref,
):
    at = 0
    for piece in (own_ref, ylo_ref, yhi_ref, zlo_ref, zhi_ref, xlo_ref, xhi_ref, xzlo_ref, xzhi_ref):
        n = piece.shape[0]
        fs_ref[at : at + n, :] = piece[...].astype(f32)
        at += n
    fs_ref[at : at + 16, :] = jnp.zeros((16, 128), f32)
    xs = (x0_ref, x1_ref, x2_ref)
    gs = (g0_ref, g1_ref, g2_ref)
    masks_r = row_masks()
    zero8 = jnp.zeros((8, 128), f32)

    def rotate(cp, carry):
        parts = []
        for half in range(2):
            cell = 2 * cp + half
            for i in range(3):
                g = 3 * cell + i
                res = []
                for half4 in range(2):
                    rows = []
                    for e in range(4 * half4, 4 * half4 + 4):
                        q = src_ref[2 * cell + (e & 1), 4 * i + (e >> 1)]
                        base = base_ref[padded_cell(q, cell)] + (q & 1)
                        rows += [fs_ref[pl.ds(base, 56, 2), :], zero8]
                    rhs = jnp.concatenate(rows, axis=0).astype(bf16)
                    u = u4_ref[g, half4]
                    lhs = jnp.concatenate([masked(u, m) for m in masks_r], axis=1)
                    res.append(dot(lhs, rhs).reshape(16, 8, 128))
                parts.append(halves(*res))
        for j in range(3):
            both = [jnp.concatenate([parts[2 * j][h], parts[2 * j + 1][h]], axis=1) for h in range(2)]
            row = pl.multiple_of(48 * cp + 16 * j, 16)
            for q, pair in enumerate(PAIRS):
                for h, (m, degree) in enumerate(pair):
                    if degree > LMAX:
                        continue
                    z, up, col = z_place(m, degree)
                    value = both[h][q]
                    if m == 0:
                        p0_ref[pl.ds(row, 16), col : col + 128] = value
                        value = value * rad_ref[pl.ds(row, 16), col : col + 128]
                    xs[z][pl.ds(row + up, 16), col : col + 128] = value.astype(bf16)
        return carry

    lax.fori_loop(0, 4, rotate, 0, unroll=True)
    h_ref[:, 240:256, :] = jnp.zeros((G, 16, 128), bf16)
    along = jnp.zeros((E, 128), f32)

    def rounded(x):
        return x.astype(bf16).astype(f32)

    x0 = x0_ref[...]
    for q in range(4):
        width = 256 if q < 3 else 128
        at = 256 * q
        hid = rounded(dot(x0, w0v[:, at : at + width]))
        prod = hid * g0_ref[:, at : at + width].astype(f32)
        along = along + prod[:, :128]
        if q < 3:
            along = along + prod[:, 128:]
        second = hid[:, 128:] if q < 3 else jnp.zeros((E, 128), f32)
        h_ref[:, 16 * q : 16 * q + 16, :] = pair_block(hid[:, :128], second)
    for m, wv, first in ((1, w1v, 4), (2, w2v, 10)):
        x = xs[m][...]
        count = 7 - m
        for l0 in range(0, count, 2):
            n = min(2, count - l0)
            a = dot(x, wv[0, :, 128 * l0 : 128 * (l0 + n)])
            b = dot(x, wv[1, :, 128 * l0 : 128 * (l0 + n)])
            hp = rounded(a[:E] - b[E:])
            hn = rounded(b[:E] + a[E:])
            gp = gs[m][0:E, 128 * l0 : 128 * (l0 + n)].astype(f32)
            gn = gs[m][E : 2 * E, 128 * l0 : 128 * (l0 + n)].astype(f32)
            prod = hp * gp + hn * gn
            for i in range(n):
                cut = slice(128 * i, 128 * i + 128)
                along = along + prod[:, cut]
                q = first + l0 + i
                h_ref[:, 16 * q : 16 * q + 16, :] = pair_block(hp[:, cut], hn[:, cut])
    grad_act = dot3(gi0_ref[...] * p0_ref[...], rout_ref[...], dot_nt)
    grad_basis = dot3(grad_act * dsilu_ref[...], rin_ref[...], dot_nt)
    parts = grad_basis * wb_ref[...]
    total = along * ratio_ref[...] + parts[:, :128] + parts[:, 128:]
    grad_dist = jnp.sum(total, axis=1, keepdims=True)
    force_ref[...] = jnp.zeros((8, 128), f32)
    for d in range(3):
        force_ref[d : d + 1, :] = jnp.sum(side_ref[d] * grad_dist, axis=0, keepdims=True)


def kernel_b2(own_ref, v_ref, h_ref, envl_ref, counts_ref, upd_ref, fs_ref, us_ref):
    fs_ref[0:784, :] = own_ref[...].astype(f32)
    fs_ref[784:800, :] = jnp.zeros((16, 128), f32)
    slot = iota((64, 256), 1) & 1

    def back(cell, carry):
        sums = jnp.zeros((128, 128), f32)
        for i in range(3):
            g = 3 * cell + i
            v = v_ref[g].astype(f32) * envl_ref[pl.ds(g, 1), :]
            lhs = jnp.concatenate([jnp.where(slot == s, v, 0.0) for s in range(2)], axis=0).astype(bf16)
            sums = sums + dot(lhs, h_ref[g])
        for s in range(2):
            occ = jnp.where(s < counts_ref[cell >> 2, (cell >> 1) & 1, cell & 1], 1.0, 0.0).astype(f32)
            own = fs_ref[pl.ds(98 * cell + s, 56, 2), :]
            us_ref[pl.ds(98 * cell + s, 56, 2), :] = (own + sums[64 * s : 64 * s + 56]) * occ
        return carry

    lax.fori_loop(0, 8, back, 0, unroll=4)
    upd_ref[...] = us_ref[0:784, :].astype(bf16)


def fold_x(mid_ref, lo_ref, hi_ref, zlo_ref, zhi_ref, out_ref):
    for px in range(2):
        arrived = lo_ref if px == 0 else hi_ref
        for py in range(0, 4, 2):
            ends = {0: [], 3: []}
            for pj in range(2):
                for pz in range(4):
                    at = ((py + pj) * 4 + pz) * CR
                    both = mid_ref[px * 16 * CR + at : px * 16 * CR + at + CR, :]
                    if pz % 2 == 0:
                        pair = arrived[at : at + 2 * CR, :].astype(f32)
                    both = both + pair[(pz % 2) * CR : (pz % 2) * CR + CR]
                    if pz in ends:
                        ends[pz].append(both)
                    else:
                        to = ((px * 4 + py + pj) * 2 + pz - 1) * CR
                        out_ref[to : to + CR, :] = both
            to = (px * 4 + py) * CR
            zlo_ref[to : to + 2 * CR, :] = jnp.concatenate(ends[0], axis=0).astype(bf16)
            zhi_ref[to : to + 2 * CR, :] = jnp.concatenate(ends[3], axis=0).astype(bf16)


def force_sum(mine, lo, hi, shift, bit):
    at = (iota((8, 128), 1) >> bit) & 3
    lo = pltpu.roll(lo, 128 - shift, 1)
    hi = pltpu.roll(hi, shift, 1)
    return mine + jnp.where(at == 1, lo, 0.0) + jnp.where(at == 2, hi, 0.0)


def fold_force_x(mine_ref, lo_ref, hi_ref, out_ref):
    out_ref[...] = force_sum(mine_ref[...], lo_ref[...], hi_ref[...], 64, 5)


def fold_z(
    mid_ref, lo_ref, hi_ref, force_ref, flo_ref, fhi_ref, ylo_ref, yhi_ref, out_ref, fout_ref,
):
    force = force_sum(force_ref[...], flo_ref[...], fhi_ref[...], 4, 1)
    fout_ref[...] = force
    rest = force - force.astype(bf16).astype(f32)
    for ref in (ylo_ref, yhi_ref):
        ref[4 * CR : 4 * CR + 16, :] = jnp.concatenate([force, rest], axis=0).astype(bf16)
    for px in range(2):
        arrived = [[], []]
        for z, ref in enumerate((lo_ref, hi_ref)):
            for py in range(0, 4, 2):
                at = (px * 4 + py) * CR
                pair = ref[at : at + 2 * CR, :].astype(f32)
                arrived[z] += [pair[:CR], pair[CR:]]
        for py in range(4):
            done = []
            for z in range(2):
                at = ((px * 4 + py) * 2 + z) * CR
                done.append(mid_ref[at : at + CR, :] + arrived[z][py])
            if py in (0, 3):
                to = px * 2 * CR
                ref = ylo_ref if py == 0 else yhi_ref
                ref[to : to + 2 * CR, :] = jnp.concatenate(done, axis=0).astype(bf16)
            else:
                to = (px * 2 + py - 1) * 2 * CR
                out_ref[to : to + 2 * CR, :] = jnp.concatenate(done, axis=0)


def fold_y(mid_ref, force_ref, lo_ref, hi_ref, out_ref, fout_ref):
    sides = []
    for ref in (lo_ref, hi_ref):
        both = ref[4 * CR : 4 * CR + 16, :].astype(f32)
        sides.append(both[:8] + both[8:])
    total = force_sum(force_ref[...], sides[0], sides[1], 16, 3)
    r = iota((16, 128), 1)
    o = iota((16, 128), 0)
    from_lane = ((o >> 3) + 1) * 32 + (((o >> 2) & 1) + 1) * 8 + (((o >> 1) & 1) + 1) * 2 + (o & 1)
    pick = (r == from_lane).astype(f32)
    fout_ref[...] = lax.dot_general(
        pick, total, (((1,), (1,)), ((), ())), precision=lax.Precision.HIGHEST, preferred_element_type=f32
    )[:, :3]
    for px in range(2):
        for py, ref in enumerate((lo_ref, hi_ref)):
            pair = ref[px * 2 * CR : (px + 1) * 2 * CR, :].astype(f32)
            at = (px * 2 + py) * 2 * CR
            value = mid_ref[at : at + 2 * CR, :] + pair
            for z in range(2):
                to = ((px * 2 + py) * 2 + z) * 98
                out_ref[to : to + 98, :] = value[z * CR : z * CR + 98]


VM = pl.BlockSpec(memory_space=pltpu.VMEM)
SM = pl.BlockSpec(memory_space=pltpu.SMEM)
HB = pl.BlockSpec(memory_space=pltpu.HBM)


def shape(dims, dtype):
    return jax.ShapeDtypeStruct(dims, dtype)


def weights_scratch():
    return [pltpu.VMEM((896, 896), bf16), pltpu.VMEM((2, 768, 768), bf16), pltpu.VMEM((2, 640, 640), bf16)]


def call(kernel, out, specs, scratch, limit, name, cost=None):
    return pl.pallas_call(
        kernel,
        out_shape=out,
        in_specs=specs,
        out_specs=jax.tree.map(lambda _: VM, out),
        scratch_shapes=scratch,
        compiler_params=pltpu.CompilerParams(vmem_limit_bytes=limit),
        name=name,
        cost_estimate=cost,
    )


def cost(us):
    return pl.CostEstimate(flops=int(us * 10**9), bytes_accessed=1 << 20, transcendentals=0)


def run_a1(wt, counts, dist, rin, rout, cot):
    out = [
        shape((G, 256, 128), bf16),
        shape((E, 896), bf16), shape((2 * E, 768), bf16), shape((2 * E, 640), bf16),
        shape((E, 896), f32), shape((E, 128), f32), shape((E, NB), f32), shape((E, 128), f32), shape((G, 256), f32),
        shape((800, 128), f32),
    ]
    scratch = [
        pltpu.VMEM((16, 12), f32), pltpu.VMEM((NB, 128), f32), pltpu.VMEM((128, 896), f32),
        pltpu.VMEM((784, 128), bf16), pltpu.SMEM((2, 2, 2), jnp.int32), pltpu.VMEM((E, 128), f32),
        pltpu.SemaphoreType.DMA((5,)),
    ]
    return call(kernel_a1, out, [VM] + [HB] * 5, scratch, 24 << 20, "rotations", cost(6))(
        wt, *[pltpu.with_memory_space_constraint(x, pltpu.HBM) for x in (counts, dist, rin, rout, cot)]
    )


def run_a2(u, z0, z1, z2, rad, w0, w1, w2):
    out = [
        shape((E, 896), f32), shape((G, 256, 128), bf16), shape((G, 64, 256), bf16), shape((G, 2, 128, 128), bf16),
    ]
    return call(kernel_a2, out, [VM] * 8, [], 20 << 20, "mix_backward", cost(4))(u, z0, z1, z2, rad, w0, w1, w2)


def run_a3(v, gr, cs, counts, src, dirs):
    out = [
        shape((16 * CR, 128), bf16), shape((16 * CR, 128), bf16), shape((32 * CR, 128), f32),
        shape((3, E, 128), f32),
    ]
    scratch = [pltpu.VMEM((64 * CR + 16, 128), f32)]
    return call(kernel_a3, out, [VM, VM, VM, SM, SM, VM, VM], scratch, 20 << 20, "source_gradients", cost(5))(
        v, gr, cs, counts, src, src, dirs
    )


def run_b1(pieces, src, saved, rin, rout, w0, w1, w2):
    out = [shape((G, 256, 128), bf16), shape((8, 128), f32)]
    scratch = [
        pltpu.VMEM((6272 + 16, 128), f32),
        pltpu.VMEM((E, 896), bf16), pltpu.VMEM((2 * E, 768), bf16), pltpu.VMEM((2 * E, 640), bf16),
        pltpu.VMEM((E, 896), f32),
    ]
    specs = [VM] * 9 + [SM, SM] + [VM] * 15
    return call(kernel_b1, out, specs, scratch, 28 << 20, "hidden_and_forces", cost(7))(
        *pieces, jnp.asarray(base_table()), src, *saved, rin, rout, w0, w1, w2
    )


def run_b2(own, v, h, envl, counts):
    scratch = [pltpu.VMEM((800, 128), f32), pltpu.VMEM((800, 128), f32)]
    return call(kernel_b2, shape((784, 128), bf16), [VM] * 4 + [SM], scratch, 16 << 20, "updated", cost(2))(
        own, v, h, envl, counts
    )


def shifts(axis):
    n = lax.axis_size(axis)
    up = [(i, (i + 1) % n) for i in range(n)]
    return up, [(t, s) for s, t in up]


def exchange(to_up, to_down, axis):
    up, down = shifts(axis)
    return lax.ppermute(to_up, axis, up), lax.ppermute(to_down, axis, down)


def tie(*values):
    return lax.optimization_barrier(values)


def test_run(pieces, wt, cot, src, cnt, dist, dirs, w0, w1, w2, rin, rout):
    cnt = cnt.reshape(2, 2, 2)
    u, z0, z1, z2, rad, dsilu, wb, ratio, envl, cs = run_a1(wt, cnt, dist, rin, rout, cot)
    gi0, gr, v, u4 = run_a2(u, z0, z1, z2, rad, w0, w1, w2)
    gxlo, gxhi, mid, side = run_a3(v, gr, cs, cnt, src, dirs)
    h, force = run_b1(pieces, src, (u4, z0, z1, z2, gi0, rad, dsilu, wb, ratio, side), rin, rout, w0, w1, w2)
    return run_b2(pieces[0], v, h, envl, cnt), force, gxlo, gxhi, mid


def local(features, cotangent, counts, sources, wigner, distance, direction, w0, w1, w2, rin, rout):
    cot = jnp.transpose(cotangent, (0, 1, 2, 4, 3, 5)).reshape(784, 128)
    wt = jnp.transpose(wigner, (1, 2, 3, 5, 4, 0)).reshape(E, -1)
    wt = jnp.pad(wt, ((0, 0), (0, 256 - wt.shape[1])))
    src = sources.reshape(16, 12)
    dist = distance.reshape(16, 12)
    dirs = direction.reshape(48, 12)
    feats = jnp.transpose(features, (0, 1, 2, 4, 3, 5))

    ylo, yhi = exchange(feats[:, 1:2], feats[:, 0:1], "gy")
    a1 = run_a1(wt, counts, dist, rin, rout, cot)
    a1, ylo, yhi = tie(a1, ylo, yhi)
    u, z0, z1, z2, rad, dsilu, wb, ratio, envl, cs = a1
    tall = jnp.concatenate([ylo, feats, yhi], axis=1)
    up, down = tall[:, :, 1:2], tall[:, :, 0:1]
    (u, z0, z1, z2, rad), up, down = tie((u, z0, z1, z2, rad), up, down)
    zlo, zhi = exchange(up, down, "gz")
    xlo, xhi = exchange(tall[1:2], tall[0:1], "gx")
    gi0, gr, v, u4 = run_a2(u, z0, z1, z2, rad, w0, w1, w2)
    gr, zlo, zhi = tie(gr, zlo, zhi)
    top = jnp.concatenate([zlo[1:2], zhi[1:2]], axis=0)
    low = jnp.concatenate([zlo[0:1], zhi[0:1]], axis=0)
    gr, top, low = tie(gr, top, low)
    xzlo, xzhi = exchange(top, low, "gx")
    gxlo, gxhi, mid, side = run_a3(v, gr, cs, counts, src, dirs)

    lo, hi = exchange(gxhi, gxlo, "gx")
    rows = [p.reshape(-1, 128) for p in (feats, ylo, yhi, zlo, zhi, xlo, xhi, xzlo, xzhi)]
    h, force = run_b1(rows, src, (u4, z0, z1, z2, gi0, rad, dsilu, wb, ratio, side), rin, rout, w0, w1, w2)
    h, lo, hi = tie(h, lo, hi)
    flo, fhi = exchange(force, force, "gx")
    gzlo, gzhi, mid = call(
        fold_x,
        [shape((8 * CR, 128), bf16), shape((8 * CR, 128), bf16), shape((16 * CR, 128), f32)],
        [VM] * 3, [], 16 << 20, "fold_x", cost(0.1),
    )(mid, lo, hi)
    lo, hi = exchange(gzhi, gzlo, "gz")
    force = call(fold_force_x, shape((8, 128), f32), [VM] * 3, [], 8 << 20, "fold_force", cost(4))(force, flo, fhi)
    flo, fhi = exchange(force, force, "gz")
    gylo, gyhi, mid, force = call(
        fold_z,
        [
            shape((4 * CR + 16, 128), bf16), shape((4 * CR + 16, 128), bf16), shape((8 * CR, 128), f32),
            shape((8, 128), f32),
        ],
        [VM] * 6, [], 16 << 20, "fold_z", cost(1),
    )(mid, lo, hi, force, flo, fhi)
    force, h = tie(force, h)
    lo, hi = exchange(gyhi, gylo, "gy")
    updated = run_b2(rows[0], v, h, envl, counts)
    updated, lo, hi = tie(updated, lo, hi)
    grads, force = call(
        fold_y, [shape((784, 128), f32), shape((16, 3), f32)], [VM] * 4, [], 16 << 20, "fold_y", cost(1),
    )(mid, force, lo, hi)
    forces = jnp.moveaxis(force.reshape(2, 2, 2, 2, 3), 4, 0)

    def back(x):
        return jnp.transpose(x.reshape(2, 2, 2, 49, 2, 128), (0, 1, 2, 4, 3, 5))

    return back(updated), back(grads), forces


def solution(mesh):
    cells = P("gx", "gy", "gz")
    behind = P(None, "gx", "gy", "gz")
    in_specs = (cells, cells, cells, cells, behind, cells, behind, P(), P(), P(), P(), P())
    return jax.shard_map(local, mesh=mesh, in_specs=in_specs, out_specs=(cells, cells, behind), check_vma=False)
```

```python
import math

import jax
import jax.numpy as jnp
import numpy as np
from jax import lax
from jax.experimental import pallas as pl
from jax.experimental.pallas import tpu as pltpu
from jax.sharding import PartitionSpec as P

LMAX = 6
NB = 256
E = 192
G = 24
CR = 104
cutoff = 6.0
sigma_width = 0.5
bf16 = jnp.bfloat16
f32 = jnp.float32
SCALE = 1.0 / math.sqrt(12.0)

PAIRS = (
    [((0, 2 * q), (0, 2 * q + 1)) for q in range(4)]
    + [((1, l), (-1, l)) for l in range(1, 7)]
    + [((2, l), (-2, l)) for l in range(2, 7)]
)


def row_starts():
    starts = []
    total = 0
    for degree in range(LMAX + 1):
        starts.append(total)
        total += min(2 * degree + 1, 5) * (2 * degree + 1)
    out = []
    for pair in PAIRS:
        for m, degree in pair:
            if degree > LMAX:
                out.append((-1, 0))
            else:
                out.append((starts[degree] + (m + min(degree, 2)) * (2 * degree + 1), degree))
    return out


def expansion(q):
    rows = row_starts()
    lane = iota((1, 256), 1)
    j = lane & 63
    target = jnp.full((1, 256), -1, jnp.int32)
    for h in range(2):
        start, degree = rows[2 * q + h]
        if start >= 0:
            low = degree * degree
            inside = ((lane >> 7) == h) & (j >= low) & (j < low + 2 * degree + 1)
            target = jnp.where(inside, start + j - low, target)
    return jnp.where(iota((256, 256), 0) == target, 1.0, 0.0).astype(bf16)


def base_table():
    out = np.zeros((64,), np.int32)
    for px in range(4):
        for py in range(4):
            for pz in range(4):
                if px in (0, 3):
                    at = 784 + 392 * 2 + 784 * 2 + (px == 3) * 784
                    if pz in (0, 3):
                        at += 784 * 2 + (pz == 3) * 392 + py * 98
                    else:
                        at += (py * 2 + pz - 1) * 98
                elif pz in (0, 3):
                    at = 784 + 392 * 2 + (pz == 3) * 784 + ((px - 1) * 4 + py) * 98
                elif py in (0, 3):
                    at = 784 + (py == 3) * 392 + ((px - 1) * 2 + pz - 1) * 98
                else:
                    at = (((px - 1) * 2 + py - 1) * 2 + pz - 1) * 98
                out[(px * 4 + py) * 4 + pz] = at
    return out


def iota(shape, dim):
    return lax.broadcasted_iota(jnp.int32, shape, dim)


def dot(a, b):
    return lax.dot_general(a, b, (((1,), (0,)), ((), ())), preferred_element_type=f32)


def dot_nt(a, b):
    return lax.dot_general(a, b, (((1,), (1,)), ((), ())), preferred_element_type=f32)


def split2(a):
    hi = a.astype(bf16)
    return hi, (a - hi.astype(f32)).astype(bf16)


def dot3(a, b, op=dot):
    ah, al = split2(a)
    bh, bl = split2(b)
    return op(ah, bh) + (op(ah, bl) + op(al, bh))


def dot3_narrow(a, b, nt):
    ah, al = split2(a)
    bh, bl = split2(b)
    wide = dot_nt(ah, jnp.concatenate([bh, bl], axis=0)) if nt else dot(ah, jnp.concatenate([bh, bl], axis=1))
    return wide[:, :128] + (wide[:, 128:] + (dot_nt(al, bh) if nt else dot(al, bh)))


def edge_ids():
    e = iota((E, 128), 0)
    cell = (e * 2731) >> 16
    rest = e - 24 * cell
    return cell, rest & 1, rest >> 1


def column(block):
    e = iota((E, 16), 0)
    cell = (e * 2731) >> 16
    rest = e - 24 * cell
    pick = (iota((E, 16), 1) == 2 * cell + (rest & 1)).astype(f32)
    rows = lax.dot_general(
        pick, block, (((1,), (0,)), ((), ())), precision=lax.Precision.HIGHEST, preferred_element_type=f32
    )
    e = iota((E, 12), 0)
    rest = e - 24 * ((e * 2731) >> 16)
    return jnp.sum(jnp.where(iota((E, 12), 1) == (rest >> 1), rows, 0.0), axis=1, keepdims=True)


def occupied_edges(counts_ref):
    cell, slot, _ = edge_ids()
    out = jnp.zeros((E, 128), f32)
    for c in range(8):
        out = jnp.where((cell == c) & (slot < counts_ref[c >> 2, (c >> 1) & 1, c & 1]), 1.0, out)
    return out


def basis_of(dist):
    centers = iota((E, NB), 1).astype(f32) * (cutoff / (NB - 1))
    offset = dist - centers
    return jnp.exp(-0.5 * (offset / sigma_width) ** 2), offset


def row_masks():
    r = iota((16, 128), 0) & 3
    h = iota((16, 128), 1) >> 6
    return [jnp.where(r == 2 * t + h, 1.0, 0.0).astype(bf16) for t in range(2)]


def lane_masks():
    lane = iota((16, 256), 1) & 7
    return [jnp.where(lane == e, 1.0, 0.0).astype(bf16) for e in range(8)]


def masked(block, mask):
    n, w = block.shape
    return (block.reshape(n // 16, 16, w) * mask[None]).reshape(n, w)


def padded_cell(q, cell):
    o = q >> 1
    dx = (o * 57) >> 9
    r = o - 9 * dx
    dy = (r * 11) >> 5
    dz = r - 3 * dy
    px = (cell >> 2) + dx
    py = ((cell >> 1) & 1) + dy
    pz = (cell & 1) + dz
    return (px * 4 + py) * 4 + pz


def pair_block(a, b):
    return jnp.concatenate([a.reshape(G, 8, 128), b.reshape(G, 8, 128)], axis=1).astype(bf16)


def z_place(m, degree):
    if m == 0:
        return 0, 0, degree * 128
    return abs(m), (0 if m > 0 else E), (degree - abs(m)) * 128


def start_copies(pairs, sems):
    copies = [pltpu.make_async_copy(src, dst, sems.at[i]) for i, (src, dst) in enumerate(pairs)]
    for c in copies:
        c.start()
    return copies


def kernel_a1(
    wt_ref, counts_hbm, dist_hbm, rin_hbm, rout_hbm, cot_hbm,
    u_ref, z0_ref, z1_ref, z2_ref, rad_ref, dsilu_ref, wb_ref, ratio_ref, envl_ref, cs_ref,
    dist_ref, rin_ref, rout_ref, cot_ref, counts_ref, env_ref, sems,
):
    copies = start_copies(
        ((dist_hbm, dist_ref), (rin_hbm, rin_ref), (rout_hbm, rout_ref), (cot_hbm, cot_ref), (counts_hbm, counts_ref)), sems
    )
    zs = (z0_ref, z1_ref, z2_ref)
    copies[0].wait()
    copies[1].wait()
    dist = column(dist_ref[...])
    basis, offset = basis_of(dist)
    wb_ref[...] = basis * (-offset / (sigma_width * sigma_width))
    inner = dot3_narrow(basis, rin_ref[...], False)
    sig = jax.nn.sigmoid(inner)
    dsilu_ref[...] = sig * (1.0 + inner * (1.0 - sig))
    copies[2].wait()
    copies[4].wait()
    rad_ref[...] = dot3(inner * sig, rout_ref[...])
    angle = jnp.broadcast_to(dist, (E, 128)) * (math.pi / cutoff)
    env = 0.5 * (jnp.cos(angle) + 1.0)
    pick = ((iota((G, E), 1) >> 3) == iota((G, E), 0)).astype(f32)
    spread = jnp.where(
        (iota((E, 256), 0) & 7) == (iota((E, 256), 1) & 7), jnp.concatenate([env, env], axis=1) * SCALE, 0.0
    )
    envl_ref[...] = lax.dot_general(
        pick, spread, (((1,), (0,)), ((), ())), precision=lax.Precision.HIGHEST, preferred_element_type=f32
    )
    ratio_ref[...] = (-0.5 * math.pi / cutoff) * jnp.sin(angle) / env
    env_ref[...] = env * (occupied_edges(counts_ref) * SCALE)
    wt = wt_ref[...]
    for q in range(15):
        res = dot(wt, expansion(q))
        u_ref[:, 16 * q : 16 * q + 16, :] = pair_block(res[:, :128], res[:, 128:])
    u_ref[:, 240:256, :] = jnp.zeros((G, 16, 128), bf16)

    copies[3].wait()
    cs_ref[0:784, :] = cot_ref[...].astype(f32)
    cs_ref[784:800, :] = jnp.zeros((16, 128), f32)
    m_rot = jnp.where((iota((16, 128), 0) & 1) == (iota((16, 128), 1) >> 6), 1.0, 0.0).astype(bf16)
    zero8 = jnp.zeros((8, 128), f32)

    def rotate(cp, carry):
        parts = []
        for half in range(2):
            cell = 2 * cp + half
            rhs = jnp.concatenate(
                [
                    cs_ref[pl.ds(98 * cell, 56, 2), :],
                    zero8,
                    cs_ref[pl.ds(98 * cell + 1, 56, 2), :],
                    zero8,
                ],
                axis=0,
            ).astype(bf16)
            for i in range(3):
                g = 3 * cell + i
                res = dot(masked(u_ref[g, 0:240, :], m_rot), rhs)
                scale = env_ref[pl.ds(pl.multiple_of(8 * g, 8), 8), :]
                parts.append(res.reshape(30, 8, 128) * scale[None])
        for j in range(3):
            both = jnp.concatenate([parts[2 * j], parts[2 * j + 1]], axis=1).astype(bf16)
            row = pl.multiple_of(48 * cp + 16 * j, 16)
            for q, pair in enumerate(PAIRS):
                for h, (m, degree) in enumerate(pair):
                    if degree <= LMAX:
                        z, up, col = z_place(m, degree)
                        zs[z][pl.ds(row + up, 16), col : col + 128] = both[2 * q + h]
        return carry

    lax.fori_loop(0, 4, rotate, 0, unroll=True)


def halves(k0, k1):
    low = (iota((1, 8, 128), 1) < 4)
    return jnp.where(low, k0, pltpu.roll(k1, 4, 1)), jnp.where(low, pltpu.roll(k0, 4, 1), k1)


def kernel_a2(
    u_ref, z0_ref, z1_ref, z2_ref, rad_ref, srcv_ref, dir_ref, w0v, w1v, w2v,
    gi0_ref, gr_ref, v_ref, u4_ref, side_ref,
):
    cell, slot, _ = edge_ids()
    q = jnp.broadcast_to(column(srcv_ref[...].astype(f32)), (E, 128)).astype(jnp.int32)
    lane = iota((E, 128), 1)
    from_slot = 2 * padded_cell(q, cell) + (q & 1)
    to_slot = 2 * padded_cell(jnp.full((E, 128), 26, jnp.int32), cell) + slot
    sign = jnp.where(lane == from_slot, 1.0, 0.0) - jnp.where(lane == to_slot, 1.0, 0.0)
    for d in range(3):
        side_ref[d] = sign * column(dir_ref[16 * d : 16 * d + 16, :])
    def turn(g, carry):
        u = u_ref[g]
        v_ref[g] = u.T[:64]
        pairs = u.astype(f32).reshape(16, 2, 8, 128)
        a, b = halves(pairs[:, 0], pairs[:, 1])
        u4_ref[g, 0] = a.reshape(128, 128).astype(bf16)
        u4_ref[g, 1] = b.reshape(128, 128).astype(bf16)
        return carry

    lax.fori_loop(0, G, turn, 0, unroll=4)
    zs = (z0_ref, z1_ref, z2_ref)
    gr_ref[:, 240:256, :] = jnp.zeros((G, 16, 128), bf16)
    z0 = z0_ref[...]
    for q in range(4):
        width = 256 if q < 3 else 128
        at = 256 * q
        gi = dot_nt(z0, w0v[at : at + width, :])
        gi0_ref[:, at : at + width] = gi
        gr = gi * rad_ref[:, at : at + width]
        second = gr[:, 128:] if q < 3 else jnp.zeros((E, 128), f32)
        gr_ref[:, 16 * q : 16 * q + 16, :] = pair_block(gr[:, :128], second)
    for m, wv, first in ((1, w1v, 4), (2, w2v, 10)):
        z = zs[m][...]
        count = 7 - m
        for l0 in range(0, count, 2):
            n = min(2, count - l0)
            a = dot_nt(z, wv[0, 128 * l0 : 128 * (l0 + n), :])
            b = dot_nt(z, wv[1, 128 * l0 : 128 * (l0 + n), :])
            gp = a[:E] + b[E:]
            gn = a[E:] - b[:E]
            for i in range(n):
                q = first + l0 + i
                gr_ref[:, 16 * q : 16 * q + 16, :] = pair_block(
                    gp[:, 128 * i : 128 * i + 128], gn[:, 128 * i : 128 * i + 128]
                )


def kernel_a3(
    v_ref, gr_ref, cs_ref, counts_ref, src_ref,
    xlo_ref, xhi_ref, mid_ref, acc_ref,
):
    acc_ref[...] = jnp.zeros(acc_ref.shape, f32)
    row_ok = iota((56, 128), 0) < 49
    for cell in range(8):
        p = (((cell >> 2) + 1) * 4 + ((cell >> 1) & 1) + 1) * 4 + (cell & 1) + 1
        for s in range(2):
            occ = jnp.where(s < counts_ref[cell >> 2, (cell >> 1) & 1, cell & 1], 1.0, 0.0).astype(f32)
            acc_ref[pl.ds(p * CR + s, 56, 2), :] = jnp.where(
                row_ok, cs_ref[pl.ds(98 * cell + s, 56, 2), :] * occ, 0.0
            )
    masks = lane_masks()

    def back(cell, carry):
        for i in range(3):
            g = 3 * cell + i
            v = v_ref[g]
            lhs = jnp.concatenate([masked(v, m) for m in masks], axis=0)
            res = dot(lhs, gr_ref[g])
            for e in range(8):
                q = src_ref[2 * cell + (e & 1), 4 * i + (e >> 1)]
                row = padded_cell(q, cell) * CR + (q & 1)
                acc_ref[pl.ds(row, 56, 2), :] += res[64 * e : 64 * e + 56]
        return carry

    lax.fori_loop(0, 8, back, 0, unroll=2)
    xlo_ref[...] = acc_ref[0 : 16 * CR, :].astype(bf16)
    xhi_ref[...] = acc_ref[48 * CR : 64 * CR, :].astype(bf16)
    mid_ref[...] = acc_ref[16 * CR : 48 * CR, :]


def kernel_b1(
    own_ref, ylo_ref, yhi_ref, zlo_ref, zhi_ref, xlo_ref, xhi_ref, xzlo_ref, xzhi_ref, base_ref, src_ref,
    u4_ref, g0_ref, g1_ref, g2_ref, gi0_ref, rad_ref, dsilu_ref, wb_ref, ratio_ref, side_ref, rin_ref, rout_ref,
    w0v, w1v, w2v,
    h_ref, force_ref,
    fs_ref, x0_ref, x1_ref, x2_ref, p0_ref,
):
    at = 0
    for piece in (own_ref, ylo_ref, yhi_ref, zlo_ref, zhi_ref, xlo_ref, xhi_ref, xzlo_ref, xzhi_ref):
        n = piece.shape[0]
        fs_ref[at : at + n, :] = piece[...].astype(f32)
        at += n
    fs_ref[at : at + 16, :] = jnp.zeros((16, 128), f32)
    xs = (x0_ref, x1_ref, x2_ref)
    gs = (g0_ref, g1_ref, g2_ref)
    masks_r = row_masks()
    zero8 = jnp.zeros((8, 128), f32)

    def rotate(cp, carry):
        parts = []
        for half in range(2):
            cell = 2 * cp + half
            for i in range(3):
                g = 3 * cell + i
                res = []
                for half4 in range(2):
                    rows = []
                    for e in range(4 * half4, 4 * half4 + 4):
                        q = src_ref[2 * cell + (e & 1), 4 * i + (e >> 1)]
                        base = base_ref[padded_cell(q, cell)] + (q & 1)
                        rows += [fs_ref[pl.ds(base, 56, 2), :], zero8]
                    rhs = jnp.concatenate(rows, axis=0).astype(bf16)
                    u = u4_ref[g, half4]
                    lhs = jnp.concatenate([masked(u, m) for m in masks_r], axis=1)
                    res.append(dot(lhs, rhs).reshape(16, 8, 128))
                parts.append(halves(*res))
        for j in range(3):
            both = [jnp.concatenate([parts[2 * j][h], parts[2 * j + 1][h]], axis=1) for h in range(2)]
            row = pl.multiple_of(48 * cp + 16 * j, 16)
            for q, pair in enumerate(PAIRS):
                for h, (m, degree) in enumerate(pair):
                    if degree > LMAX:
                        continue
                    z, up, col = z_place(m, degree)
                    value = both[h][q]
                    if m == 0:
                        p0_ref[pl.ds(row, 16), col : col + 128] = value
                        value = value * rad_ref[pl.ds(row, 16), col : col + 128]
                    xs[z][pl.ds(row + up, 16), col : col + 128] = value.astype(bf16)
        return carry

    lax.fori_loop(0, 4, rotate, 0, unroll=True)
    h_ref[:, 240:256, :] = jnp.zeros((G, 16, 128), bf16)
    along = jnp.zeros((E, 128), f32)

    def rounded(x):
        return x.astype(bf16).astype(f32)

    x0 = x0_ref[...]
    for q in range(4):
        width = 256 if q < 3 else 128
        at = 256 * q
        hid = rounded(dot(x0, w0v[:, at : at + width]))
        prod = hid * g0_ref[:, at : at + width].astype(f32)
        along = along + prod[:, :128]
        if q < 3:
            along = along + prod[:, 128:]
        second = hid[:, 128:] if q < 3 else jnp.zeros((E, 128), f32)
        h_ref[:, 16 * q : 16 * q + 16, :] = pair_block(hid[:, :128], second)
    for m, wv, first in ((1, w1v, 4), (2, w2v, 10)):
        x = xs[m][...]
        count = 7 - m
        for l0 in range(0, count, 2):
            n = min(2, count - l0)
            a = dot(x, wv[0, :, 128 * l0 : 128 * (l0 + n)])
            b = dot(x, wv[1, :, 128 * l0 : 128 * (l0 + n)])
            hp = rounded(a[:E] - b[E:])
            hn = rounded(b[:E] + a[E:])
            gp = gs[m][0:E, 128 * l0 : 128 * (l0 + n)].astype(f32)
            gn = gs[m][E : 2 * E, 128 * l0 : 128 * (l0 + n)].astype(f32)
            prod = hp * gp + hn * gn
            for i in range(n):
                cut = slice(128 * i, 128 * i + 128)
                along = along + prod[:, cut]
                q = first + l0 + i
                h_ref[:, 16 * q : 16 * q + 16, :] = pair_block(hp[:, cut], hn[:, cut])
    grad_act = dot3_narrow(gi0_ref[...] * p0_ref[...], rout_ref[...], True)
    grad_basis = dot3(grad_act * dsilu_ref[...], rin_ref[...], dot_nt)
    parts = grad_basis * wb_ref[...]
    total = along * ratio_ref[...] + parts[:, :128] + parts[:, 128:]
    grad_dist = jnp.sum(total, axis=1, keepdims=True)
    force_ref[...] = jnp.zeros((8, 128), f32)
    for d in range(3):
        force_ref[d : d + 1, :] = jnp.sum(side_ref[d] * grad_dist, axis=0, keepdims=True)


def kernel_b2(own_ref, v_ref, h_ref, envl_ref, counts_ref, upd_ref, fs_ref, us_ref):
    fs_ref[0:784, :] = own_ref[...].astype(f32)
    fs_ref[784:800, :] = jnp.zeros((16, 128), f32)
    slot = iota((64, 256), 1) & 1

    def back(cell, carry):
        sums = jnp.zeros((128, 128), f32)
        for i in range(3):
            g = 3 * cell + i
            v = v_ref[g].astype(f32) * envl_ref[pl.ds(g, 1), :]
            lhs = jnp.concatenate([jnp.where(slot == s, v, 0.0) for s in range(2)], axis=0).astype(bf16)
            sums = sums + dot(lhs, h_ref[g])
        for s in range(2):
            occ = jnp.where(s < counts_ref[cell >> 2, (cell >> 1) & 1, cell & 1], 1.0, 0.0).astype(f32)
            own = fs_ref[pl.ds(98 * cell + s, 56, 2), :]
            us_ref[pl.ds(98 * cell + s, 56, 2), :] = (own + sums[64 * s : 64 * s + 56]) * occ
        return carry

    lax.fori_loop(0, 8, back, 0, unroll=4)
    upd_ref[...] = us_ref[0:784, :].astype(bf16)


def fold_x(mid_ref, lo_ref, hi_ref, zlo_ref, zhi_ref, out_ref):
    for px in range(2):
        arrived = lo_ref if px == 0 else hi_ref
        for py in range(0, 4, 2):
            ends = {0: [], 3: []}
            for pj in range(2):
                for pz in range(4):
                    at = ((py + pj) * 4 + pz) * CR
                    both = mid_ref[px * 16 * CR + at : px * 16 * CR + at + CR, :]
                    if pz % 2 == 0:
                        pair = arrived[at : at + 2 * CR, :].astype(f32)
                    both = both + pair[(pz % 2) * CR : (pz % 2) * CR + CR]
                    if pz in ends:
                        ends[pz].append(both)
                    else:
                        to = ((px * 4 + py + pj) * 2 + pz - 1) * CR
                        out_ref[to : to + CR, :] = both
            to = (px * 4 + py) * CR
            zlo_ref[to : to + 2 * CR, :] = jnp.concatenate(ends[0], axis=0).astype(bf16)
            zhi_ref[to : to + 2 * CR, :] = jnp.concatenate(ends[3], axis=0).astype(bf16)


def force_sum(mine, lo, hi, shift, bit):
    at = (iota((8, 128), 1) >> bit) & 3
    lo = pltpu.roll(lo, 128 - shift, 1)
    hi = pltpu.roll(hi, shift, 1)
    return mine + jnp.where(at == 1, lo, 0.0) + jnp.where(at == 2, hi, 0.0)


def fold_force_z(mine_ref, lo_ref, hi_ref, out_ref):
    out_ref[...] = force_sum(mine_ref[...], lo_ref[...], hi_ref[...], 4, 1)


def fold_z(
    mid_ref, lo_ref, hi_ref, force_ref, flo_ref, fhi_ref, ylo_ref, yhi_ref, out_ref, fout_ref,
):
    force = force_sum(force_ref[...], flo_ref[...], fhi_ref[...], 64, 5)
    fout_ref[...] = force
    rest = force - force.astype(bf16).astype(f32)
    for ref in (ylo_ref, yhi_ref):
        ref[4 * CR : 4 * CR + 16, :] = jnp.concatenate([force, rest], axis=0).astype(bf16)
    for px in range(2):
        arrived = [[], []]
        for z, ref in enumerate((lo_ref, hi_ref)):
            for py in range(0, 4, 2):
                at = (px * 4 + py) * CR
                pair = ref[at : at + 2 * CR, :].astype(f32)
                arrived[z] += [pair[:CR], pair[CR:]]
        for py in range(4):
            done = []
            for z in range(2):
                at = ((px * 4 + py) * 2 + z) * CR
                done.append(mid_ref[at : at + CR, :] + arrived[z][py])
            if py in (0, 3):
                to = px * 2 * CR
                ref = ylo_ref if py == 0 else yhi_ref
                ref[to : to + 2 * CR, :] = jnp.concatenate(done, axis=0).astype(bf16)
            else:
                to = (px * 2 + py - 1) * 2 * CR
                out_ref[to : to + 2 * CR, :] = jnp.concatenate(done, axis=0)


def fold_y(mid_ref, force_ref, lo_ref, hi_ref, out_ref, fout_ref):
    sides = []
    for ref in (lo_ref, hi_ref):
        both = ref[4 * CR : 4 * CR + 16, :].astype(f32)
        sides.append(both[:8] + both[8:])
    total = force_sum(force_ref[...], sides[0], sides[1], 16, 3)
    r = iota((16, 128), 1)
    o = iota((16, 128), 0)
    from_lane = ((o >> 3) + 1) * 32 + (((o >> 2) & 1) + 1) * 8 + (((o >> 1) & 1) + 1) * 2 + (o & 1)
    pick = (r == from_lane).astype(f32)
    fout_ref[...] = lax.dot_general(
        pick, total, (((1,), (1,)), ((), ())), precision=lax.Precision.HIGHEST, preferred_element_type=f32
    )[:, :3]
    for px in range(2):
        for py, ref in enumerate((lo_ref, hi_ref)):
            pair = ref[px * 2 * CR : (px + 1) * 2 * CR, :].astype(f32)
            at = (px * 2 + py) * 2 * CR
            value = mid_ref[at : at + 2 * CR, :] + pair
            for z in range(2):
                to = ((px * 2 + py) * 2 + z) * 98
                out_ref[to : to + 98, :] = value[z * CR : z * CR + 98]


VM = pl.BlockSpec(memory_space=pltpu.VMEM)
SM = pl.BlockSpec(memory_space=pltpu.SMEM)
HB = pl.BlockSpec(memory_space=pltpu.HBM)


def shape(dims, dtype):
    return jax.ShapeDtypeStruct(dims, dtype)


def weights_scratch():
    return [pltpu.VMEM((896, 896), bf16), pltpu.VMEM((2, 768, 768), bf16), pltpu.VMEM((2, 640, 640), bf16)]


def call(kernel, out, specs, scratch, limit, name, cost=None):
    return pl.pallas_call(
        kernel,
        out_shape=out,
        in_specs=specs,
        out_specs=jax.tree.map(lambda _: VM, out),
        scratch_shapes=scratch,
        compiler_params=pltpu.CompilerParams(vmem_limit_bytes=limit),
        name=name,
        cost_estimate=cost,
    )


def cost(us):
    return pl.CostEstimate(flops=int(us * 10**9), bytes_accessed=1 << 20, transcendentals=0)


def run_a1(wt, counts, dist, rin, rout, cot):
    out = [
        shape((G, 256, 128), bf16),
        shape((E, 896), bf16), shape((2 * E, 768), bf16), shape((2 * E, 640), bf16),
        shape((E, 896), f32), shape((E, 128), f32), shape((E, NB), f32), shape((E, 128), f32), shape((G, 256), f32),
        shape((800, 128), f32),
    ]
    scratch = [
        pltpu.VMEM((16, 12), f32), pltpu.VMEM((NB, 128), f32), pltpu.VMEM((128, 896), f32),
        pltpu.VMEM((784, 128), bf16), pltpu.SMEM((2, 2, 2), jnp.int32), pltpu.VMEM((E, 128), f32),
        pltpu.SemaphoreType.DMA((5,)),
    ]
    return call(kernel_a1, out, [VM] + [HB] * 5, scratch, 24 << 20, "rotations", cost(6))(
        wt, *[pltpu.with_memory_space_constraint(x, pltpu.HBM) for x in (counts, dist, rin, rout, cot)]
    )


def run_a2(u, z0, z1, z2, rad, src, dirs, w0, w1, w2):
    out = [
        shape((E, 896), f32), shape((G, 256, 128), bf16), shape((G, 64, 256), bf16), shape((G, 2, 128, 128), bf16),
        shape((3, E, 128), f32),
    ]
    return call(kernel_a2, out, [VM] * 10, [], 20 << 20, "mix_backward", cost(4))(
        u, z0, z1, z2, rad, src, dirs, w0, w1, w2
    )


def run_a3(v, gr, cs, counts, src):
    out = [
        shape((16 * CR, 128), bf16), shape((16 * CR, 128), bf16), shape((32 * CR, 128), f32),
    ]
    scratch = [pltpu.VMEM((64 * CR + 16, 128), f32)]
    return call(kernel_a3, out, [VM, VM, VM, SM, SM], scratch, 20 << 20, "source_gradients", cost(5))(
        v, gr, cs, counts, src
    )


def run_b1(pieces, src, saved, rin, rout, w0, w1, w2):
    out = [shape((G, 256, 128), bf16), shape((8, 128), f32)]
    scratch = [
        pltpu.VMEM((6272 + 16, 128), f32),
        pltpu.VMEM((E, 896), bf16), pltpu.VMEM((2 * E, 768), bf16), pltpu.VMEM((2 * E, 640), bf16),
        pltpu.VMEM((E, 896), f32),
    ]
    specs = [VM] * 9 + [SM, SM] + [VM] * 15
    return call(kernel_b1, out, specs, scratch, 28 << 20, "hidden_and_forces", cost(7))(
        *pieces, jnp.asarray(base_table()), src, *saved, rin, rout, w0, w1, w2
    )


def run_b2(own, v, h, envl, counts):
    scratch = [pltpu.VMEM((800, 128), f32), pltpu.VMEM((800, 128), f32)]
    return call(kernel_b2, shape((784, 128), bf16), [VM] * 4 + [SM], scratch, 16 << 20, "updated", cost(2))(
        own, v, h, envl, counts
    )


def shifts(axis):
    n = lax.axis_size(axis)
    up = [(i, (i + 1) % n) for i in range(n)]
    return up, [(t, s) for s, t in up]


def exchange(to_up, to_down, axis):
    up, down = shifts(axis)
    return lax.ppermute(to_up, axis, up), lax.ppermute(to_down, axis, down)


def tie(*values):
    return lax.optimization_barrier(values)


def test_run(pieces, wt, cot, src, cnt, dist, dirs, w0, w1, w2, rin, rout):
    cnt = cnt.reshape(2, 2, 2)
    u, z0, z1, z2, rad, dsilu, wb, ratio, envl, cs = run_a1(wt, cnt, dist, rin, rout, cot)
    gi0, gr, v, u4, side = run_a2(u, z0, z1, z2, rad, src, dirs, w0, w1, w2)
    gxlo, gxhi, mid = run_a3(v, gr, cs, cnt, src)
    h, force = run_b1(pieces, src, (u4, z0, z1, z2, gi0, rad, dsilu, wb, ratio, side), rin, rout, w0, w1, w2)
    return run_b2(pieces[0], v, h, envl, cnt), force, gxlo, gxhi, mid


def local(features, cotangent, counts, sources, wigner, distance, direction, w0, w1, w2, rin, rout):
    cot = jnp.transpose(cotangent, (0, 1, 2, 4, 3, 5)).reshape(784, 128)
    wt = jnp.transpose(wigner, (1, 2, 3, 5, 4, 0)).reshape(E, -1)
    wt = jnp.pad(wt, ((0, 0), (0, 256 - wt.shape[1])))
    src = sources.reshape(16, 12)
    dist = distance.reshape(16, 12)
    dirs = direction.reshape(48, 12)
    feats = jnp.transpose(features, (0, 1, 2, 4, 3, 5))

    ylo, yhi = exchange(feats[:, 1:2], feats[:, 0:1], "gy")
    a1 = run_a1(wt, counts, dist, rin, rout, cot)
    a1, ylo, yhi = tie(a1, ylo, yhi)
    u, z0, z1, z2, rad, dsilu, wb, ratio, envl, cs = a1
    tall = jnp.concatenate([ylo, feats, yhi], axis=1)
    up, down = tall[:, :, 1:2], tall[:, :, 0:1]
    (u, z0, z1, z2, rad), up, down = tie((u, z0, z1, z2, rad), up, down)
    zlo, zhi = exchange(up, down, "gz")
    xlo, xhi = exchange(tall[1:2], tall[0:1], "gx")
    gi0, gr, v, u4, side = run_a2(u, z0, z1, z2, rad, src, dirs, w0, w1, w2)
    gr, zlo, zhi = tie(gr, zlo, zhi)
    top = jnp.concatenate([zlo[1:2], zhi[1:2]], axis=0)
    low = jnp.concatenate([zlo[0:1], zhi[0:1]], axis=0)
    gr, top, low = tie(gr, top, low)
    xzlo, xzhi = exchange(top, low, "gx")
    gxlo, gxhi, mid = run_a3(v, gr, cs, counts, src)

    lo, hi = exchange(gxhi, gxlo, "gx")
    rows = [p.reshape(-1, 128) for p in (feats, ylo, yhi, zlo, zhi, xlo, xhi, xzlo, xzhi)]
    h, force = run_b1(rows, src, (u4, z0, z1, z2, gi0, rad, dsilu, wb, ratio, side), rin, rout, w0, w1, w2)
    h, lo, hi = tie(h, lo, hi)
    flo, fhi = exchange(force, force, "gz")
    gzlo, gzhi, mid = call(
        fold_x,
        [shape((8 * CR, 128), bf16), shape((8 * CR, 128), bf16), shape((16 * CR, 128), f32)],
        [VM] * 3, [], 16 << 20, "fold_x", cost(0.1),
    )(mid, lo, hi)
    lo, hi = exchange(gzhi, gzlo, "gz")
    force = call(fold_force_z, shape((8, 128), f32), [VM] * 3, [], 8 << 20, "fold_force", cost(4))(force, flo, fhi)
    flo, fhi = exchange(force, force, "gx")
    gylo, gyhi, mid, force = call(
        fold_z,
        [
            shape((4 * CR + 16, 128), bf16), shape((4 * CR + 16, 128), bf16), shape((8 * CR, 128), f32),
            shape((8, 128), f32),
        ],
        [VM] * 6, [], 16 << 20, "fold_z", cost(1),
    )(mid, lo, hi, force, flo, fhi)
    force, h = tie(force, h)
    lo, hi = exchange(gyhi, gylo, "gy")
    updated = run_b2(rows[0], v, h, envl, counts)
    updated, lo, hi = tie(updated, lo, hi)
    grads, force = call(
        fold_y, [shape((784, 128), f32), shape((16, 3), f32)], [VM] * 4, [], 16 << 20, "fold_y", cost(1),
    )(mid, force, lo, hi)
    forces = jnp.moveaxis(force.reshape(2, 2, 2, 2, 3), 4, 0)

    def back(x):
        return jnp.transpose(x.reshape(2, 2, 2, 49, 2, 128), (0, 1, 2, 4, 3, 5))

    return back(updated), back(grads), forces


def solution(mesh):
    cells = P("gx", "gy", "gz")
    behind = P(None, "gx", "gy", "gz")
    in_specs = (cells, cells, cells, cells, behind, cells, behind, P(), P(), P(), P(), P())
    return jax.shard_map(local, mesh=mesh, in_specs=in_specs, out_specs=(cells, cells, behind), check_vma=False)
```
